256 devices in a mesh: dp: 16 (over x, z_lo, core), tensor: 16 (over y, z_hi).
Axes of the slice: x: 4, y: 4, z: 8 (z_hi: 4, z_lo: 2; z = z_hi * 2 + z_lo), core: 2. Of those that a mesh axis runs over, the one named last changes fastest.
Arguments:
- inputs: bfloat16 [8192, 4096], P(('dp', 'tensor')), may hold values from -60 to 60
- gate_pre: bfloat16 [8192, 7168], P('dp', 'tensor'), may hold values from -6 to 6
- up_pre: bfloat16 [8192, 7168], P('dp', 'tensor'), may hold values from -6 to 6
- grad_out: bfloat16 [8192, 4096], P(('dp', 'tensor')), may hold values from -24 to 24
- gain: float32 [4096], replicated, may hold values from 0.25 to 1.75
- w_gate: bfloat16 [4096, 7168], P(None, 'tensor'), may hold values from -0.09375 to 0.09375
- w_up: bfloat16 [4096, 7168], P(None, 'tensor'), may hold values from -0.09375 to 0.09375
- w_down: bfloat16 [7168, 4096], P('tensor'), may hold values from -0.0625 to 0.0625
Outputs:
- grad_inputs: bfloat16 [8192, 4096], P(('dp', 'tensor'))
- grad_gate: bfloat16 [4096, 7168], P('dp', 'tensor')
- grad_up: bfloat16 [4096, 7168], P('dp', 'tensor')
- grad_down: bfloat16 [7168, 4096], P('tensor', 'dp')
- grad_gain: float32 [4096], replicated
The draws below stay inside these ranges and needn't reach their ends.
All inputs are finite; a program needn't handle non-finite values.
Results may differ from the reference program's by a relative error of at most 0.023.
Values may be sent and summed in bfloat16 or wider, within the bound.
A program may use at most 128 MiB of HBM per device.

```python
import jax
import jax.numpy as jnp
from jax import lax

D = 4096
FF = 7168
TOK_GRP = 512
TOKENS = 8192
N_DP = 16


def draw_inputs(key, part):
    key = jax.random.fold_in(key, 7)
    key_scale, key_base = jax.random.split(key, 2)
    row_scale = jnp.exp(jax.random.uniform(key_scale, (TOKENS, 1), jnp.float32) * jnp.log(10.0))
    base = jnp.clip(jax.random.normal(key_base, (TOKENS, D), jnp.float32), -6.0, 6.0)
    return (base * row_scale).astype(jnp.bfloat16)


def strengthened(entries, stream_key, source, target, blocks, factor):
    def block_of(dim):
        return (jnp.arange(entries.shape[dim]) // (entries.shape[dim] // blocks)).reshape((-1,) + (1,) * (entries.ndim - 1 - dim))

    near = jax.random.permutation(stream_key, blocks)[block_of(target)]
    far = (block_of(target) + blocks // 2) % blocks
    return jnp.where((block_of(source) == near) | (block_of(source) == far), factor * entries, entries)


def levels(key, dims, shards, low, largest):
    factor_of, own = 1.0, jax.random.fold_in(key, 6)
    for dim, shards_of in shards:
        draws = jnp.exp(jax.random.uniform(jax.random.fold_in(own, dim), (shards_of,), jnp.float32, low / len(shards), largest / len(shards)))
        factor_of = factor_of * jnp.repeat(draws, dims[dim] // shards_of).reshape([-1 if axis == dim else 1 for axis in range(len(dims))])
    return factor_of


def bell_draw(own_key, shape, scale, most, cuts=(), held_as=jnp.bfloat16):
    level = levels(own_key, shape, cuts, -0.22, 0.18) if cuts else 1.0
    entries = jax.random.normal(own_key, shape, jnp.float32) * scale * level
    return jnp.minimum(jnp.maximum(entries, -most), most).astype(held_as)


def noise_with(rng, dims, width, most, shards, heavy, held_as=jnp.bfloat16):
    result = width * jax.random.normal(rng, dims, jnp.float32)
    if shards:
        result = result * levels(rng, dims, shards, -0.22, 0.18)
    return jnp.clip(strengthened(result, jax.random.fold_in(rng, 3), *heavy), -most, most).astype(held_as)


def setup_inputs(seed: int = 0) -> dict:
    key_list = jax.random.split(jax.random.key(seed), 9)
    inputs = draw_inputs(jax.random.fold_in(key_list[8], 71), 0)
    gate_pre = bell_draw(key_list[1], (TOKENS, FF), 1.5, 6.0, ((0, 16), (1, 16)))
    up_pre = bell_draw(key_list[2], (TOKENS, FF), 1.0, 6.0, ((0, 16), (1, 16)))
    grad_out = noise_with(key_list[3], (TOKENS, D), 1.0, 24.0, ((0, 256),), (0, 1, 256, 6.0))
    gain = jnp.clip(1.0 + 0.15 * jax.random.normal(key_list[4], (D,), jnp.float32), 0.25, 1.75)
    w_gate = bell_draw(key_list[5], (D, FF), D ** -0.5, 0.09375, ((1, 16),))
    w_up = bell_draw(key_list[6], (D, FF), D ** -0.5, 0.09375, ((1, 16),))
    w_down = bell_draw(key_list[7], (FF, D), FF ** -0.5, 0.0625, ((0, 16),))
    return dict(inputs=inputs, gate_pre=gate_pre, up_pre=up_pre, grad_out=grad_out, gain=gain, w_gate=w_gate, w_up=w_up, w_down=w_down)


def reference(inputs, gate_pre, up_pre, grad_out, gain, w_gate, w_up, w_down):
    wide_inputs = inputs.astype(jnp.float32)
    inv_rms = lax.rsqrt(lax.optimization_barrier(jnp.mean(wide_inputs * wide_inputs, axis=1, keepdims=True)) + 1e-05)
    unit_rows = wide_inputs * inv_rms
    normed = (unit_rows * gain[None, :]).astype(jnp.bfloat16)
    gate_wide = gate_pre.astype(jnp.float32)
    up_wide = up_pre.astype(jnp.float32)
    sigmoid_gate = jax.nn.sigmoid(gate_wide)
    hidden = (gate_wide * sigmoid_gate * up_wide).astype(jnp.bfloat16)
    grad_hidden = jnp.dot(grad_out, w_down.T, preferred_element_type=jnp.float32)
    grad_gate_pre = (grad_hidden * up_wide * sigmoid_gate * (1.0 + gate_wide * (1.0 - sigmoid_gate))).astype(jnp.bfloat16)
    grad_up_pre = (grad_hidden * gate_wide * sigmoid_gate).astype(jnp.bfloat16)

    def rounded(value):
        return lax.optimization_barrier(value.astype(jnp.bfloat16)).astype(jnp.float32)

    def group_step(carry, pieces):
        normed_group, gate_group, up_group, hidden_group, out_group = pieces
        sum_gate = carry[0] + rounded(jnp.dot(normed_group.T, gate_group, preferred_element_type=jnp.float32))
        sum_up = carry[1] + rounded(jnp.dot(normed_group.T, up_group, preferred_element_type=jnp.float32))
        sum_down = carry[2] + rounded(jnp.dot(hidden_group.T, out_group, preferred_element_type=jnp.float32))
        return ((sum_gate, sum_up, sum_down), None)
    pieces = (normed.reshape(N_DP, TOK_GRP, D), grad_gate_pre.reshape(N_DP, TOK_GRP, FF), grad_up_pre.reshape(N_DP, TOK_GRP, FF), hidden.reshape(N_DP, TOK_GRP, FF), grad_out.reshape(N_DP, TOK_GRP, D))
    begin = (jnp.zeros((D, FF), jnp.float32), jnp.zeros((D, FF), jnp.float32), jnp.zeros((FF, D), jnp.float32))
    totals, unused = lax.scan(group_step, begin, pieces)
    grad_gate = totals[0].astype(jnp.bfloat16)
    grad_up = totals[1].astype(jnp.bfloat16)
    grad_down = totals[2].astype(jnp.bfloat16)
    grad_normed = jnp.dot(grad_gate_pre, w_gate.T, preferred_element_type=jnp.float32) + jnp.dot(grad_up_pre, w_up.T, preferred_element_type=jnp.float32)
    grad_gain = lax.optimization_barrier(jnp.sum(grad_normed * unit_rows, axis=0))
    scaled = grad_normed * gain[None, :]
    grad_inputs = (grad_out.astype(jnp.float32) + inv_rms * (scaled - unit_rows * lax.optimization_barrier(jnp.mean(scaled * unit_rows, axis=1, keepdims=True)))).astype(jnp.bfloat16)
    return (grad_inputs, grad_gate, grad_up, grad_down, grad_gain)
```

```python
import functools

import jax
import jax.numpy as jnp
from jax import lax
from jax.experimental import pallas as pl
from jax.experimental.pallas import tpu as pltpu
from jax.sharding import PartitionSpec as P

MESH = pl.DeviceIdType.MESH
BF = jnp.bfloat16
F32 = jnp.float32
D = 4096
F = 448
T = 512
NQ = 4
QW = D // NQ
KS = (0, 1, 3, 2)
RELS = (2, 1, 3, 0)


def dot_nt(a, b):
    return lax.dot_general(a, b, (((1,), (1,)), ((), ())), preferred_element_type=F32)


def dot_nn(a, b):
    return lax.dot_general(a, b, (((1,), (0,)), ((), ())), preferred_element_type=F32)


def kernel(
    inputs, gate_pre, up_pre, grad_out, gain, w_gate, w_up, w_down,
    o_in, o_gate, o_up, o_down, o_gain,
    vin, vgain, vgp, vup, wg, wu, wd,
    g_all, g_sib, n_all, n_send, a1, a2, gh, acts, act_t, act_s,
    part, rh, rf, rs, zh_buf, zf_buf, gn,
    xp_d, xh_d, xf_d, xz_d, xp_w, xh_w, xf_w, xz_w,
    gy, gz, og,
    loc, ag_s, ag_r, r_s, r_r, x_s, x_r, c_s, c_r, g_s, g_r,
):
    p = lax.axis_index("dp")
    t = lax.axis_index("tensor")
    x, zl, c = p // 4, lax.rem(p // 2, 2), lax.rem(p, 2)
    y, zh = t // 4, lax.rem(t, 4)
    oc = 1 - c
    sib = (x * 4 + zl * 2 + oc, t)
    zsib = (x * 4 + (1 - zl) * 2 + c, t)

    def ring(v, k):
        return lax.rem(v + k, 4)

    def ydev(k):
        return (p, ring(y, k) * 4 + zh)

    def zdev(k):
        return (p, y * 4 + ring(zh, k))

    def xdev(k):
        return (ring(x, k) * 4 + zl * 2 + c, t)

    def tid(ky, kz):
        return ring(y, ky) * 4 + ring(zh, kz)

    sent = []

    def send(src, dst, ss, rs_, dev):
        cp = pltpu.make_async_remote_copy(
            src_ref=src, dst_ref=dst, send_sem=ss, recv_sem=rs_, device_id=dev, device_id_type=MESH
        )
        cp.start()
        sent.append(cp)

    def recv(dst, sem, ss, dev):
        pltpu.make_async_remote_copy(
            src_ref=dst, dst_ref=dst, send_sem=ss, recv_sem=sem, device_id=dev, device_id_type=MESH
        ).wait_recv()

    local = []
    for i, (src, dst) in enumerate((
        (inputs, vin), (gain, vgain), (gate_pre, vgp), (up_pre, vup),
        (grad_out, g_all.at[t]), (w_down, wd), (w_gate, wg), (w_up, wu),
    )):
        cp = pltpu.make_async_copy(src, dst, loc.at[i])
        cp.start()
        local.append(cp)

    barrier = pltpu.get_barrier_semaphore()
    partners = [ydev(k) for k in (1, 2, 3)] + [zdev(k) for k in (1, 2, 3)] + [xdev(k) for k in (1, 2, 3)] + [sib, zsib]
    for dev in partners:
        pl.semaphore_signal(barrier, inc=1, device_id=dev, device_id_type=MESH)
    pl.semaphore_wait(barrier, len(partners))

    class Gather:
        def __init__(self, item, q, zfirst, piece, half, own):
            self.piece_t, self.half_t, self.own = piece, half, own
            self.zfirst = zfirst
            self.s = lambda i: ag_s.at[item, q, i]
            self.r = lambda i: ag_r.at[item, q, i]
            self.dev1 = zdev if zfirst else ydev
            self.dev2 = ydev if zfirst else zdev

        def tt(self, ku, kv):
            return tid(kv, ku) if self.zfirst else tid(ku, kv)

        def piece(self, ku, kv):
            return self.piece_t(self.tt(ku, kv))

        def half(self, ku, kv, h):
            return self.half_t(self.tt(ku, kv), h)

        def push(self, src, dst, i, dev):
            send(src, dst, self.s(i), self.r(i), dev)

        def second(self, k, src=None):
            i = KS.index(k)
            ref = self.piece(k, 0)
            src = ref if src is None else src
            self.push(src, ref, 4 + 2 * i + 1, self.dev2(1))
            self.push(src, ref, 4 + 2 * i, self.dev2(3))

        def e0(self):
            ref = self.piece(0, 0)
            src = ref if self.own is None else self.own
            self.push(src, ref, 1, self.dev1(1))
            self.push(src, ref, 0, self.dev1(3))
            self.second(0, src)

        def e1(self):
            recv(self.piece(1, 0), self.r(0), self.s(0), self.dev1(1))
            self.push(self.half(1, 0, 0), self.half(1, 0, 0), 2, self.dev1(3))
            self.second(1)
            recv(self.piece(3, 0), self.r(1), self.s(1), self.dev1(3))
            self.push(self.half(3, 0, 1), self.half(3, 0, 1), 3, self.dev1(1))
            self.second(3)

        def fwd(self, k):
            i = KS.index(k)
            recv(self.piece(k, 1), self.r(4 + 2 * i), self.s(4 + 2 * i), self.dev2(1))
            self.push(self.half(k, 1, 0), self.half(k, 1, 0), 12 + 2 * i, self.dev2(3))
            recv(self.piece(k, 3), self.r(4 + 2 * i + 1), self.s(4 + 2 * i + 1), self.dev2(3))
            self.push(self.half(k, 3, 1), self.half(k, 3, 1), 12 + 2 * i + 1, self.dev2(1))

        def e3(self):
            recv(self.half(2, 0, 0), self.r(2), self.s(2), self.dev1(1))
            recv(self.half(2, 0, 1), self.r(3), self.s(3), self.dev1(3))
            self.second(2)

        def e7(self):
            for i, k in enumerate(KS):
                recv(self.half(k, 2, 0), self.r(12 + 2 * i), self.s(12 + 2 * i), self.dev2(1))
                recv(self.half(k, 2, 1), self.r(12 + 2 * i + 1), self.s(12 + 2 * i + 1), self.dev2(3))

    def g_cols(q):
        return pl.ds(q * QW, QW)

    def n_cols(q):
        return pl.ds(pl.multiple_of(ring(x, RELS[q]) * 512, 512), 512)

    GA = [
        Gather(
            0, q, True,
            lambda tt, q=q: g_all.at[tt, :, g_cols(q)],
            lambda tt, h, q=q: g_all.at[tt, pl.ds(16 * h, 16), g_cols(q)],
            grad_out.at[:, g_cols(q)],
        )
        for q in range(NQ)
    ]
    NA = [
        Gather(
            1, q, True,
            lambda tt, q=q: n_all.at[:, tt, :, n_cols(q)],
            lambda tt, h, q=q: n_all.at[h, tt, :, n_cols(q)],
            None,
        )
        for q in range(NQ)
    ]

    for q in range(NQ):
        GA[q].e0()

    local[0].wait()
    local[1].wait()
    xin = vin[...].astype(F32)
    inv = lax.rsqrt(jnp.mean(xin * xin, axis=1, keepdims=True) + 1e-05)

    @pl.loop(0, 8)
    def _(j):
        own = pl.ds(pl.multiple_of((2 * j + c) * 256, 256), 256)
        oth = pl.ds(pl.multiple_of((2 * j + oc) * 256, 256), 256)
        col = pl.ds(pl.multiple_of(j * 256, 256), 256)
        n_all[c, t, :, col] = (vin[:, own].astype(F32) * inv * vgain[:, own]).astype(BF)
        n_send[:, col] = (vin[:, oth].astype(F32) * inv * vgain[:, oth]).astype(BF)

    send(n_send, n_all.at[c, t], c_s.at[0], c_r.at[0], sib)

    local[2].wait()
    local[3].wait()

    @pl.loop(0, 4)
    def _(r):
        rows = pl.ds(pl.multiple_of(r * 128, 128), 128)
        gp = vgp[rows, :].astype(F32)
        up = vup[rows, :].astype(F32)
        s = jax.nn.sigmoid(gp)
        gs = gp * s
        a2[rows, :] = gs
        a1[rows, :] = up * (s * (1.0 + gp * (1.0 - s)))
        act_t[0, :, rows] = (gs * up).T.astype(BF)

    send(act_t.at[0], act_s.at[0], c_s.at[1], c_r.at[1], sib)

    for q in range(NQ):
        GA[q].e1()
        GA[q].fwd(0)
    for q in range(NQ):
        GA[q].e3()
        GA[q].fwd(1)
        GA[q].fwd(3)
    recv(n_all.at[oc, t], c_r.at[0], c_s.at[0], sib)
    local[4].wait()
    local[5].wait()
    for q in range(NQ):
        GA[q].fwd(2)
        if q >= 1:
            NA[q - 1].e0()
        GA[q].e7()
        v = dot_nt(g_all[:, :, g_cols(q)].reshape(T, QW), wd[:, g_cols(q)])
        if q == 0:
            gh[...] = v
        else:
            gh[...] += v
        for jj in range(2):
            j = 2 * q + jj
            src = g_all.at[:, :, pl.ds(pl.multiple_of((2 * j + oc) * 256, 256), 256)]
            send(src, g_sib.at[:, :, pl.ds(j * 256, 256)], c_s.at[4 + j], c_r.at[4 + j], sib)
    NA[3].e0()

    @pl.loop(0, 4)
    def _(r):
        rows = pl.ds(pl.multiple_of(r * 128, 128), 128)
        v = gh[rows, :]
        vg = v * a1[rows, :]
        vu = v * a2[rows, :]
        acts[0, rows, :] = vg.astype(BF)
        acts[1, rows, :] = vu.astype(BF)
        act_t[1, :, rows] = vg.T.astype(BF)
        act_t[2, :, rows] = vu.T.astype(BF)

    for i in (1, 2):
        send(act_t.at[i], act_s.at[i], c_s.at[1 + i], c_r.at[1 + i], sib)

    for q in range(NQ):
        NA[q].e1()
        NA[q].fwd(0)

    def add_rows(dst, srcs, rows, step):
        @pl.loop(0, rows // step)
        def _(r):
            rr = pl.ds(pl.multiple_of(r * step, step), step)
            v = dst[rr, :].astype(F32)
            for s_ in srcs:
                v = v + s_[rr, :].astype(F32)
            dst[rr, :] = v.astype(BF)

    class XSum:
        def __init__(self, base, rows, xp, xh, xf, xz):
            self.rows, self.xp, self.xh, self.xf, self.xz = rows, xp, xh, xf, xz
            self.s = lambda i: x_s.at[base + i]
            self.r = lambda i: x_r.at[base + i]

        def push(self, src, dst, i, dev):
            send(src, dst, self.s(i), self.r(i), dev)

        def step(self, rel):
            xr = ring(x, rel)
            if rel == 2:
                self.push(self.xp.at[xr, 0], self.xh.at[0], 0, xdev(1))
                self.push(self.xp.at[xr, 1], self.xh.at[1], 1, xdev(3))
            elif rel == 1:
                recv(self.xh.at[0], self.r(0), self.s(0), xdev(3))
                add_rows(self.xp.at[xr, 0], [self.xh.at[0]], self.rows, 64)
                self.push(self.xp.at[xr], self.xf.at[0], 2, xdev(1))
            elif rel == 3:
                recv(self.xh.at[1], self.r(1), self.s(1), xdev(1))
                add_rows(self.xp.at[xr, 1], [self.xh.at[1]], self.rows, 64)
                self.push(self.xp.at[xr], self.xf.at[1], 3, xdev(3))

        def cross(self):
            recv(self.xf.at[0], self.r(2), self.s(2), xdev(3))
            recv(self.xf.at[1], self.r(3), self.s(3), xdev(1))
            oz = 1 - zl
            add_rows(self.xp.at[x, oz], [self.xf.at[0, oz], self.xf.at[1, oz]], self.rows, 64)
            self.push(self.xp.at[x, oz], self.xz, 4, zsib)

        def total(self, rr):
            v = self.xp[x, zl, rr, :].astype(F32) + self.xf[0, zl, rr, :].astype(F32)
            return v + self.xf[1, zl, rr, :].astype(F32) + self.xz[rr, :].astype(F32)

        def arrive(self):
            recv(self.xz, self.r(4), self.s(4), zsib)

    XD = XSum(0, F, xp_d, xh_d, xf_d, xz_d)
    XW = XSum(5, 2 * F, xp_w, xh_w, xf_w, xz_w)

    def down_part(rel):
        xr = ring(x, rel)

        @pl.loop(0, 2)
        def _(z):
            j = xr * 2 + z
            mine = g_all[:, :, pl.ds(pl.multiple_of((2 * j + c) * 256, 256), 256)].reshape(T, 256)
            his = g_sib[:, :, pl.ds(pl.multiple_of(j * 256, 256), 256)].reshape(T, 256)
            xp_d[xr, z] = (dot_nn(act_t[0], mine) + dot_nn(act_s[0], his)).astype(BF)

    def weight_part(rel):
        xr = ring(x, rel)

        @pl.loop(0, 4)
        def _(i):
            z, k = i // 2, lax.rem(i, 2)
            cols = pl.ds(pl.multiple_of((xr * 2 + z) * 256, 256), 256)
            mine = n_all[c, :, :, cols].reshape(T, 256)
            his = n_all[oc, :, :, cols].reshape(T, 256)
            v = dot_nn(act_t[1 + k], mine) + dot_nn(act_s[1 + k], his)
            xp_w[xr, z, pl.ds(pl.multiple_of(k * F, F), F), :] = v.astype(BF)

    def p_part(i):
        cols = pl.ds(i * 512, 512)
        v = dot_nt(acts[0], wg[cols, :]) + dot_nt(acts[1], wu[cols, :])
        part[:, :, cols] = v.astype(BF).reshape(16, 32, 512)

    recv(act_s.at[0], c_r.at[1], c_s.at[1], sib)
    for j in range(8):
        recv(g_sib.at[:, :, pl.ds(j * 256, 256)], c_r.at[4 + j], c_s.at[4 + j], sib)
    local[6].wait()
    local[7].wait()
    for q in range(NQ):
        down_part(RELS[q])
        NA[q].e3()
        NA[q].fwd(1)
        NA[q].fwd(3)
        XD.step(RELS[q])
        p_part(2 * q)
        p_part(2 * q + 1)

    class Scatter:
        def __init__(self, q):
            self.cols = pl.ds(q * QW, QW)
            self.s = lambda i: r_s.at[q, i]
            self.r = lambda i: r_r.at[q, i]

        def push(self, src, dst, i, dev):
            send(src, dst, self.s(i), self.r(i), dev)

        def blk(self, ky, kz):
            return part.at[tid(ky, kz), :, self.cols]

        def hblk(self, ky, kz, h):
            return part.at[tid(ky, kz), pl.ds(16 * h, 16), self.cols]

        def r0(self, k):
            i = KS.index(k)
            self.push(self.hblk(2, k, 0), rh.at[i, 0, :, self.cols], 2 * i, ydev(1))
            self.push(self.hblk(2, k, 1), rh.at[i, 1, :, self.cols], 2 * i + 1, ydev(3))

        def r1(self, k):
            i = KS.index(k)
            for h, ky in ((0, 1), (1, 3)):
                src = rh.at[i, h, :, self.cols]
                recv(src, self.r(2 * i + h), self.s(2 * i + h), ydev(4 - ky))
                dst = self.hblk(ky, k, h)
                dst[...] = (dst[...].astype(F32) + src[...].astype(F32)).astype(BF)
                self.push(self.blk(ky, k), rf.at[i, h, :, self.cols], 8 + 2 * i + h, ydev(ky))

        def r2(self, k):
            i = KS.index(k)
            for h, ky in ((0, 3), (1, 1)):
                recv(rf.at[i, h, :, self.cols], self.r(8 + 2 * i + h), self.s(8 + 2 * i + h), ydev(ky))
            v = self.blk(0, k)[...].astype(F32) + rf[i, 0, :, self.cols].astype(F32)
            v = v + rf[i, 1, :, self.cols].astype(F32)
            rs[i, :, self.cols] = v.astype(BF)
            if k == 2:
                for h, kz in ((0, 1), (1, 3)):
                    src = rs.at[i, pl.ds(16 * h, 16), self.cols]
                    self.push(src, zh_buf.at[h, :, self.cols], 16 + h, zdev(kz))

        def r4(self):
            for h, kz in ((0, 1), (1, 3)):
                src = zh_buf.at[h, :, self.cols]
                recv(src, self.r(16 + h), self.s(16 + h), zdev(4 - kz))
                i = KS.index(kz)
                dst = rs.at[i, pl.ds(16 * h, 16), self.cols]
                dst[...] = (dst[...].astype(F32) + src[...].astype(F32)).astype(BF)
                self.push(rs.at[i, :, self.cols], zf_buf.at[h, :, self.cols], 18 + h, zdev(kz))

        def r5(self):
            for h, kz in ((0, 3), (1, 1)):
                recv(zf_buf.at[h, :, self.cols], self.r(18 + h), self.s(18 + h), zdev(kz))
            v = rs[0, :, self.cols].astype(F32) + zf_buf[0, :, self.cols].astype(F32)
            gn[:, self.cols] = v + zf_buf[1, :, self.cols].astype(F32)

    RA = [Scatter(q) for q in range(NQ)]
    ORDER = (2, 1, 3, 0)

    for i in (1, 2):
        recv(act_s.at[i], c_r.at[1 + i], c_s.at[1 + i], sib)
    for q in range(NQ):
        NA[q].fwd(2)
        if q >= 2:
            for k in ORDER:
                RA[q - 2].r0(k)
        NA[q].e7()
        weight_part(RELS[q])
        XW.step(RELS[q])
        if q == 0:
            XD.cross()
    XD.arrive()

    @pl.loop(0, F // 64)
    def _(r):
        rr = pl.ds(pl.multiple_of(r * 64, 64), 64)
        o_down[rr, :] = XD.total(rr).astype(BF)

    for q in range(NQ):
        for k in ORDER:
            RA[q].r1(k)
        if q + 2 < NQ:
            for k in ORDER:
                RA[q + 2].r0(k)
        if q >= 1:
            RA[q - 1].r4()
        for k in ORDER:
            RA[q].r2(k)
        if q == 1:
            XW.cross()

    XW.arrive()
    blk = pl.ds(pl.multiple_of(p * 256, 256), 256)
    gsum = jnp.zeros((1, 256), F32)
    for k, (o_ref, w_ref) in enumerate(((o_gate, wg), (o_up, wu))):
        v = XW.total(pl.ds(k * F, F))
        gsum = gsum + jnp.sum(v * w_ref[blk, :].astype(F32).T, axis=0, keepdims=True)
        o_ref[...] = v.T.astype(BF)
    gsum = gsum / vgain[:, blk]
    gy[y] = jnp.broadcast_to(gsum, (8, 256))
    for k in (1, 2, 3):
        send(gy.at[y], gy.at[y], g_s.at[k], g_r.at[k], ydev(k))

    RA[NQ - 1].r4()

    for k in (1, 2, 3):
        yk = ring(y, 4 - k)
        recv(gy.at[yk], g_r.at[k], g_s.at[k], ydev(4 - k))
    gz[zh] = gy[0] + gy[1] + gy[2] + gy[3]
    for k in (1, 2, 3):
        send(gz.at[zh], gz.at[zh], g_s.at[3 + k], g_r.at[3 + k], zdev(k))
    for q in range(NQ - 1):
        RA[q].r5()
    for k in (1, 2, 3):
        zk = ring(zh, 4 - k)
        recv(gz.at[zk], g_r.at[3 + k], g_s.at[3 + k], zdev(4 - k))
    og[p] = gz[0] + gz[1] + gz[2] + gz[3]
    send(og.at[p], og.at[p], g_s.at[7], g_r.at[7], sib)
    psib = x * 4 + zl * 2 + oc
    recv(og.at[psib], g_r.at[7], g_s.at[7], sib)
    pair = x * 4 + zl * 2
    opair = x * 4 + (1 - zl) * 2
    send(og.at[pl.ds(pair, 2)], og.at[pl.ds(pair, 2)], g_s.at[8], g_r.at[8], zsib)
    recv(og.at[pl.ds(opair, 2)], g_r.at[8], g_s.at[8], zsib)
    for k in (1, 2, 3):
        send(og.at[pl.ds(x * 4, 4)], og.at[pl.ds(x * 4, 4)], g_s.at[8 + k], g_r.at[8 + k], xdev(k))

    RA[NQ - 1].r5()
    xin = vin[...].astype(F32)
    inv = lax.rsqrt(jnp.mean(xin * xin, axis=1, keepdims=True) + 1e-05)
    dotp = jnp.zeros((32, 1), F32)
    for q in range(NQ):
        cols = pl.ds(q * QW, QW)
        dotp = dotp + jnp.sum(gn[:, cols] * vgain[:, cols] * (vin[:, cols].astype(F32) * inv), axis=1, keepdims=True)
    dotp = dotp * (1.0 / D)
    for q in range(NQ):
        cols = pl.ds(q * QW, QW)
        unit = vin[:, cols].astype(F32) * inv
        res = g_all[t, :, cols].astype(F32) + inv * (gn[:, cols] * vgain[:, cols] - unit * dotp)
        o_in[:, cols] = res.astype(BF)

    for k in (1, 2, 3):
        xk = ring(x, 4 - k)
        recv(og.at[pl.ds(xk * 4, 4)], g_r.at[8 + k], g_s.at[8 + k], xdev(4 - k))
    o_gain[...] = og[:, 0, :]
    for cp in sent:
        cp.wait_send()


def body(inputs, gate_pre, up_pre, grad_out, gain, w_gate, w_up, w_down):
    V = pltpu.VMEM
    DMA = pltpu.SemaphoreType.DMA
    any_spec = pl.BlockSpec(memory_space=pl.ANY)
    vm_spec = pl.BlockSpec(memory_space=pltpu.VMEM)
    outs = pl.pallas_call(
        kernel,
        out_shape=(
            jax.ShapeDtypeStruct((32, D), BF),
            jax.ShapeDtypeStruct((256, F), BF),
            jax.ShapeDtypeStruct((256, F), BF),
            jax.ShapeDtypeStruct((F, 256), BF),
            jax.ShapeDtypeStruct((16, 256), F32),
        ),
        in_specs=[any_spec] * 8,
        out_specs=(vm_spec,) * 5,
        scratch_shapes=[
            V((32, D), BF), V((1, D), F32), V((T, F), BF), V((T, F), BF),
            V((D, F), BF), V((D, F), BF), V((F, D), BF),
            V((16, 32, D), BF), V((16, 32, D // 2), BF), V((2, 16, 32, D // 2), BF), V((32, D // 2), BF),
            V((T, F), F32), V((T, F), F32), V((T, F), F32),
            V((2, T, F), BF), V((3, F, T), BF), V((3, F, T), BF),
            V((16, 32, D), BF), V((4, 2, 16, D), BF), V((4, 2, 32, D), BF), V((4, 32, D), BF),
            V((2, 16, D), BF), V((2, 32, D), BF), V((32, D), F32),
            V((4, 2, F, 256), BF), V((2, F, 256), BF), V((2, 2, F, 256), BF), V((F, 256), BF),
            V((4, 2, 2 * F, 256), BF), V((2, 2 * F, 256), BF), V((2, 2, 2 * F, 256), BF), V((2 * F, 256), BF),
            V((4, 8, 256), F32), V((4, 8, 256), F32), V((16, 8, 256), F32),
            DMA((8,)), DMA((2, NQ, 20)), DMA((2, NQ, 20)), DMA((NQ, 20)), DMA((NQ, 20)),
            DMA((10,)), DMA((10,)), DMA((12,)), DMA((12,)), DMA((12,)), DMA((12,)),
        ],
        compiler_params=pltpu.CompilerParams(
            collective_id=0, has_side_effects=True, vmem_limit_bytes=60 * 2**20
        ),
    )(inputs, gate_pre, up_pre, grad_out, gain.reshape(1, D), w_gate, w_up, w_down)
    return outs[0], outs[1], outs[2], outs[3], outs[4].reshape(D)


def solution(mesh):
    return jax.shard_map(
        body,
        mesh=mesh,
        in_specs=(
            P(("dp", "tensor"), None),
            P("dp", "tensor"),
            P("dp", "tensor"),
            P(("dp", "tensor"), None),
            P(),
            P(None, "tensor"),
            P(None, "tensor"),
            P("tensor", None),
        ),
        out_specs=(
            P(("dp", "tensor"), None),
            P("dp", "tensor"),
            P("dp", "tensor"),
            P("tensor", "dp"),
            P(),
        ),
        check_vma=False,
    )
```

```python
import functools

import jax
import jax.numpy as jnp
from jax import lax
from jax.experimental import pallas as pl
from jax.experimental.pallas import tpu as pltpu
from jax.sharding import PartitionSpec as P

MESH = pl.DeviceIdType.MESH
BF = jnp.bfloat16
F32 = jnp.float32
D = 4096
F = 448
T = 512
NQ = 4
QW = D // NQ
KS = (0, 1, 3, 2)
MODES = {'G': 'zzzy', 'N': 'zzzz', 'R': 'zzzy'}
ORDER = (
    ('G', 'e0', 2), ('normed',), ('G', 'e0', 0), ('G', 's2', 0, 0), ('G', 'e0', 1), ('G', 'e0', 3), ('G', 's2', 3, 0),
    ('G', 's2', 1, 0), ('prefac',), ('nx',), ('G', 's2', 2, 0), ('G', 'f2', 0, 0, 3), ('G', 'f2', 0, 0, 1),
    ('G', 'f1', 2, 3), ('G', 'f1', 2, 1), ('G', 's2', 2, 3), ('G', 'f1', 3, 3), ('G', 'f1', 3, 1), ('G', 's2', 3, 3),
    ('G', 's2', 3, 1), ('G', 's2', 2, 1), ('G', 'f2', 1, 0, 3), ('G', 'f2', 1, 0, 1), ('G', 'f1', 0, 3),
    ('G', 's2', 0, 3), ('G', 'f1', 0, 1), ('G', 's2', 0, 1), ('G', 'f2', 2, 0, 3), ('G', 'f2', 2, 0, 1),
    ('G', 'f2', 2, 3, 3), ('G', 'f2', 2, 3, 1), ('G', 'f1', 1, 3), ('G', 'f1', 1, 1), ('G', 's2', 1, 3),
    ('G', 's2', 1, 1), ('G', 'e3', 3), ('G', 's2', 3, 2), ('G', 'f2', 2, 1, 3), ('G', 'f2', 2, 1, 1),
    ('G', 'f2', 3, 0, 3), ('G', 'f2', 3, 0, 1), ('G', 'f2', 0, 3, 3), ('G', 'f2', 0, 3, 1), ('G', 'e3', 2),
    ('G', 's2', 2, 2), ('G', 'f2', 0, 1, 3), ('G', 'f2', 0, 1, 1), ('G', 'f2', 3, 3, 3), ('G', 'f2', 3, 3, 1),
    ('G', 'f2', 1, 3, 3), ('G', 'f2', 1, 3, 1), ('G', 'f2', 1, 1, 3), ('G', 'f2', 1, 1, 1), ('G', 'f2', 3, 1, 3),
    ('G', 'f2', 3, 1, 1), ('G', 'e3', 0), ('G', 's2', 0, 2), ('G', 'f2', 2, 2, 3), ('G', 'f2', 2, 2, 1),
    ('G', 'e3', 1), ('G', 's2', 1, 2), ('G', 'f2', 3, 2, 3), ('G', 'f2', 3, 2, 1), ('G', 'f2', 0, 2, 3),
    ('G', 'f2', 0, 2, 1), ('G', 'done', 2), ('gh', 2), ('G', 'f2', 1, 2, 3), ('G', 'f2', 1, 2, 1), ('N', 'e0', 0),
    ('N', 's2', 0, 0), ('G', 'done', 0), ('gh', 0), ('G', 'done', 3), ('N', 'e0', 1), ('N', 's2', 1, 0),
    ('G', 'done', 1), ('gh', 1), ('N', 'f2', 0, 0, 3), ('N', 'f2', 0, 0, 1), ('gh', 3), ('acts',),
    ('N', 'f2', 1, 0, 3), ('N', 'f2', 1, 0, 1), ('N', 'f1', 0, 3), ('N', 'f1', 0, 1), ('N', 's2', 0, 3),
    ('N', 's2', 0, 1), ('dready',), ('D', 'part', 2), ('D', 'x2'), ('N', 'e0', 2), ('N', 's2', 2, 0),
    ('D', 'part', 1), ('D', 'part', 3), ('D', 'part', 0), ('wready',), ('N', 'f1', 1, 3), ('N', 's2', 1, 3),
    ('N', 'e3', 0), ('N', 's2', 0, 2), ('N', 'f1', 1, 1), ('N', 'f2', 0, 3, 3), ('N', 'f2', 0, 3, 1), ('tr',),
    ('pp', 5), ('N', 'f2', 0, 1, 3), ('N', 'f2', 0, 1, 1), ('N', 'f1', 2, 3), ('N', 'f1', 2, 1), ('N', 's2', 1, 1),
    ('pp', 6), ('N', 'f2', 2, 0, 3), ('N', 'f2', 2, 0, 1), ('N', 'e0', 3), ('N', 'e3', 1), ('N', 's2', 1, 2),
    ('N', 'f2', 1, 3, 3), ('N', 'f2', 1, 3, 1), ('D', 'x1'), ('D', 'x3'), ('pp', 4), ('N', 'f2', 0, 2, 3),
    ('N', 'f2', 0, 2, 1), ('pp', 2), ('N', 'e3', 2), ('N', 's2', 2, 3), ('pp', 1), ('N', 'f2', 1, 1, 3),
    ('N', 'f2', 1, 1, 1), ('pp', 0), ('N', 's2', 2, 1), ('N', 'f1', 3, 3), ('N', 'f1', 3, 1), ('pp', 3),
    ('N', 'f2', 1, 2, 3), ('N', 'f2', 1, 2, 1), ('N', 's2', 2, 2), ('pp', 7), ('N', 'done', 0), ('W', 'part', 2),
    ('N', 'e3', 3), ('N', 'f2', 2, 3, 3), ('N', 'f2', 2, 3, 1), ('N', 's2', 3, 0), ('W', 'x2'), ('R', 'r0', 3, 2),
    ('N', 's2', 3, 3), ('R', 'r0', 3, 1), ('R', 'r0', 3, 3), ('R', 'r0', 3, 0), ('N', 'f2', 2, 1, 3),
    ('N', 'f2', 2, 1, 1), ('N', 'done', 1), ('W', 'part', 1), ('N', 'f2', 2, 2, 3), ('N', 'f2', 2, 2, 1),
    ('N', 's2', 3, 1), ('W', 'x1i'), ('D', 'cross'), ('N', 's2', 3, 2), ('R', 'r1', 3, 2, 0), ('R', 'r1', 3, 2, 1),
    ('N', 'f2', 3, 0, 3), ('N', 'f2', 3, 0, 1), ('R', 'r1', 3, 1, 0), ('R', 'r1', 3, 1, 1), ('N', 'f2', 3, 3, 3),
    ('N', 'f2', 3, 3, 1), ('R', 'r1', 3, 3, 0), ('R', 'r1', 3, 3, 1), ('R', 'r0', 0, 2), ('N', 'done', 2),
    ('W', 'part', 3), ('W', 'x3i'), ('N', 'f2', 3, 1, 3), ('N', 'f2', 3, 1, 1), ('R', 'r1', 3, 0, 0),
    ('R', 'r1', 3, 0, 1), ('R', 'r0', 0, 1), ('N', 'f2', 3, 2, 3), ('N', 'f2', 3, 2, 1), ('R', 'r0', 0, 3),
    ('R', 'r0', 0, 0), ('R', 'r0', 1, 2), ('R', 'r1', 0, 2, 0), ('R', 'r1', 0, 2, 1), ('W', 'x1d'), ('W', 'x3d'),
    ('D', 'fin'), ('N', 'done', 3), ('W', 'part', 0), ('R', 'r1', 1, 2, 0), ('R', 'r1', 1, 2, 1),
    ('R', 'r1', 0, 1, 0), ('R', 'r1', 0, 1, 1), ('R', 'r1', 0, 3, 0), ('R', 'r1', 0, 3, 1), ('R', 'r2', 0, 2),
    ('R', 'r1', 0, 0, 0), ('R', 'r1', 0, 0, 1), ('R', 'r2', 3, 2), ('R', 'r2', 3, 1), ('R', 'r2', 1, 2),
    ('R', 'r2', 3, 3), ('R', 'r0', 2, 2), ('R', 'r0', 1, 1), ('R', 'r2', 0, 1), ('R', 'r0', 2, 1), ('R', 'r0', 1, 3),
    ('R', 'r2', 0, 3), ('R', 'r2', 3, 0), ('R', 'r0', 2, 3), ('R', 'r0', 1, 0), ('R', 'r4', 0, 0), ('R', 'r4', 0, 1),
    ('R', 'r4', 3, 0), ('R', 'r4', 3, 1), ('R', 'r2', 0, 0), ('R', 'r1', 2, 2, 0), ('R', 'r1', 2, 2, 1),
    ('R', 'r1', 1, 1, 0), ('R', 'r1', 1, 1, 1), ('R', 'r1', 2, 1, 0), ('R', 'r1', 2, 1, 1), ('W', 'cross'),
    ('R', 'r1', 1, 3, 0), ('R', 'r1', 1, 3, 1), ('R', 'r1', 2, 3, 0), ('R', 'r1', 1, 0, 0), ('R', 'r1', 1, 0, 1),
    ('R', 'r1', 2, 3, 1), ('R', 'r5', 0), ('R', 'r5', 3), ('R', 'r2', 2, 2), ('R', 'r2', 1, 1), ('R', 'r4', 1, 0),
    ('R', 'r0', 2, 0), ('R', 'r2', 2, 1), ('R', 'r2', 1, 3), ('R', 'r4', 1, 1), ('R', 'r2', 1, 0), ('R', 'r2', 2, 3),
    ('R', 'r1', 2, 0, 0), ('R', 'r1', 2, 0, 1), ('W', 'fin'), ('R', 'r4', 2, 0), ('R', 'r4', 2, 1), ('R', 'r2', 2, 0),
    ('R', 'r5', 1), ('gain1',), ('R', 'r5', 2), ('fin',), ('gain2',),
)
RELS = (2, 1, 3, 0)


def dot_nt(a, b):
    return lax.dot_general(a, b, (((1,), (1,)), ((), ())), preferred_element_type=F32)


def dot_nn(a, b):
    return lax.dot_general(a, b, (((1,), (0,)), ((), ())), preferred_element_type=F32)


def kernel(
    inputs, gate_pre, up_pre, grad_out, gain, w_gate, w_up, w_down,
    o_in, o_gate, o_up, o_down, o_gain,
    vin, vgain, vgp, vup, wg, wu, wd,
    g_all, g_sib, n_all, n_send, a1, a2, gh, acts, act_t, act_s,
    part, rh, rf, rs, zh_buf, zf_buf, gn,
    xp_d, xh_d, xf_d, xz_d, xp_w, xh_w, xf_w, xz_w,
    gt, og,
    loc, ag_s, ag_r, r_s, r_r, x_s, x_r, c_s, c_r, g_s, g_r,
):
    p = lax.axis_index("dp")
    t = lax.axis_index("tensor")
    x, zl, c = p // 4, lax.rem(p // 2, 2), lax.rem(p, 2)
    y, zh = t // 4, lax.rem(t, 4)
    oc = 1 - c
    sib = (x * 4 + zl * 2 + oc, t)
    zsib = (x * 4 + (1 - zl) * 2 + c, t)

    def ring(v, k):
        return lax.rem(v + k, 4)

    def ydev(k):
        return (p, ring(y, k) * 4 + zh)

    def zdev(k):
        return (p, y * 4 + ring(zh, k))

    def xdev(k):
        return (ring(x, k) * 4 + zl * 2 + c, t)

    def tdev(k):
        return (p, lax.rem(t + k, 16))

    def pdev(k):
        return (lax.rem(p + k, 16), t)

    def tid(ky, kz):
        return ring(y, ky) * 4 + ring(zh, kz)

    sent = []

    def send(src, dst, ss, rs_, dev):
        cp = pltpu.make_async_remote_copy(
            src_ref=src, dst_ref=dst, send_sem=ss, recv_sem=rs_, device_id=dev, device_id_type=MESH
        )
        cp.start()
        sent.append(cp)

    def recv(dst, sem, ss, dev):
        pltpu.make_async_remote_copy(
            src_ref=dst, dst_ref=dst, send_sem=ss, recv_sem=sem, device_id=dev, device_id_type=MESH
        ).wait_recv()

    barrier = pltpu.get_barrier_semaphore()
    partners = [f(k) for f in (ydev, zdev, xdev) for k in (1, 3)] + [sib, zsib]
    for dev in partners:
        pl.semaphore_signal(barrier, inc=1, device_id=dev, device_id_type=MESH)
    local = []
    for i, (src, dst) in enumerate((
        (inputs, vin), (gain, vgain), (gate_pre, vgp), (up_pre, vup),
        (grad_out, g_all.at[t]), (w_down, wd), (w_gate, wg), (w_up, wu),
    )):
        cp = pltpu.make_async_copy(src, dst, loc.at[i])
        cp.start()
        local.append(cp)

    local[0].wait()
    local[1].wait()
    xin = vin[...].astype(F32)
    inv = lax.rsqrt(jnp.mean(xin * xin, axis=1, keepdims=True) + 1e-05)

    @pl.loop(0, 8)
    def _(j):
        own = pl.ds(pl.multiple_of((2 * j + c) * 256, 256), 256)
        oth = pl.ds(pl.multiple_of((2 * j + oc) * 256, 256), 256)
        col = pl.ds(pl.multiple_of(j * 256, 256), 256)
        n_all[c, t, :, col] = (vin[:, own].astype(F32) * inv * vgain[:, own]).astype(BF)
        n_send[:, col] = (vin[:, oth].astype(F32) * inv * vgain[:, oth]).astype(BF)
    pl.semaphore_wait(barrier, len(partners))

    class Gather:
        def __init__(self, item, q, zfirst, piece, half, own):
            self.piece_t, self.half_t, self.own = piece, half, own
            self.zfirst = zfirst
            self.s = lambda i: ag_s.at[item, q, i]
            self.r = lambda i: ag_r.at[item, q, i]
            self.dev1 = zdev if zfirst else ydev
            self.dev2 = ydev if zfirst else zdev

        def tt(self, ku, kv):
            return tid(kv, ku) if self.zfirst else tid(ku, kv)

        def piece(self, ku, kv):
            return self.piece_t(self.tt(ku, kv))

        def half(self, ku, kv, h):
            return self.half_t(self.tt(ku, kv), h)

        def push(self, src, dst, i, dev):
            send(src, dst, self.s(i), self.r(i), dev)

        def e0(self):
            ref = self.piece(0, 0)
            src = ref if self.own is None else self.own
            self.push(src, ref, 1, self.dev1(1))
            self.push(src, ref, 0, self.dev1(3))

        def s2(self, k):
            i = KS.index(k)
            ref = self.piece(k, 0)
            src = ref if self.own is None or k else self.own
            self.push(src, ref, 4 + 2 * i + 1, self.dev2(1))
            self.push(src, ref, 4 + 2 * i, self.dev2(3))

        def f1(self, k):
            h = k // 2
            recv(self.piece(k, 0), self.r(h), self.s(h), self.dev1(k))
            self.push(self.half(k, 0, h), self.half(k, 0, h), 2 + h, self.dev1(4 - k))

        def f2(self, k, kk):
            i, h = KS.index(k), kk // 2
            recv(self.piece(k, kk), self.r(4 + 2 * i + h), self.s(4 + 2 * i + h), self.dev2(kk))
            self.push(self.half(k, kk, h), self.half(k, kk, h), 12 + 2 * i + h, self.dev2(4 - kk))

        def e3(self):
            recv(self.half(2, 0, 0), self.r(2), self.s(2), self.dev1(1))
            recv(self.half(2, 0, 1), self.r(3), self.s(3), self.dev1(3))

        def done(self):
            for i, k in enumerate(KS):
                recv(self.half(k, 2, 0), self.r(12 + 2 * i), self.s(12 + 2 * i), self.dev2(1))
                recv(self.half(k, 2, 1), self.r(12 + 2 * i + 1), self.s(12 + 2 * i + 1), self.dev2(3))

    def g_cols(q):
        return pl.ds(q * QW, QW)

    def n_cols(q):
        return pl.ds(pl.multiple_of(ring(x, RELS[q]) * 512, 512), 512)

    GA = [
        Gather(
            0, q, MODES['G'][q] == 'z',
            lambda tt, q=q: g_all.at[tt, :, g_cols(q)],
            lambda tt, h, q=q: g_all.at[tt, pl.ds(16 * h, 16), g_cols(q)],
            grad_out.at[:, g_cols(q)],
        )
        for q in range(NQ)
    ]
    NA = [
        Gather(
            1, q, MODES['N'][q] == 'z',
            lambda tt, q=q: n_all.at[:, tt, :, n_cols(q)],
            lambda tt, h, q=q: n_all.at[h, tt, :, n_cols(q)],
            None,
        )
        for q in range(NQ)
    ]

    def normed():
        send(n_send, n_all.at[c, t], c_s.at[0], c_r.at[0], sib)

    def nx():
        recv(n_all.at[oc, t], c_r.at[0], c_s.at[0], sib)

    def prefac():
        local[2].wait()
        local[3].wait()

        @pl.loop(0, F // 64)
        def _(r):
            rows = pl.ds(pl.multiple_of(r * 64, 64), 64)
            gp = vgp[rows, :].astype(F32)
            up = vup[rows, :].astype(F32)
            s = jax.nn.sigmoid(gp)
            gs = gp * s
            a2[rows, :] = gs
            a1[rows, :] = up * (s * (1.0 + gp * (1.0 - s)))
            act_t[0, rows, :] = (gs * up).astype(BF)

        send(act_t.at[0], act_s.at[0], c_s.at[1], c_r.at[1], sib)

    begun = set()

    def gh_add(q):
        if "gh" not in begun:
            local[4].wait()
            local[5].wait()
        v = dot_nt(wd[:, g_cols(q)], g_all[:, :, g_cols(q)].reshape(T, QW))
        gh[...] = v if "gh" not in begun else gh[...] + v
        begun.add("gh")
        for jj in range(2):
            j = 2 * q + jj
            src = g_all.at[:, :, pl.ds(pl.multiple_of((2 * j + oc) * 256, 256), 256)]
            send(src, g_sib.at[:, :, pl.ds(j * 256, 256)], c_s.at[4 + j], c_r.at[4 + j], sib)

    def act_grads():
        @pl.loop(0, F // 64)
        def _(r):
            rows = pl.ds(pl.multiple_of(r * 64, 64), 64)
            v = gh[rows, :]
            act_t[1, rows, :] = (v * a1[rows, :]).astype(BF)
            act_t[2, rows, :] = (v * a2[rows, :]).astype(BF)

        for i in (1, 2):
            send(act_t.at[i], act_s.at[i], c_s.at[1 + i], c_r.at[1 + i], sib)

    def turn():
        @pl.loop(0, 4)
        def _(r):
            rows = pl.ds(pl.multiple_of(r * 128, 128), 128)
            for i in (1, 2):
                acts[i - 1, rows, :] = act_t[i, :, rows].T

    def d_ready():
        recv(act_s.at[0], c_r.at[1], c_s.at[1], sib)
        for j in range(8):
            recv(g_sib.at[:, :, pl.ds(j * 256, 256)], c_r.at[4 + j], c_s.at[4 + j], sib)

    def w_ready():
        for i in (1, 2):
            recv(act_s.at[i], c_r.at[1 + i], c_s.at[1 + i], sib)

    def add_rows(dst, srcs, rows, step):
        @pl.loop(0, rows // step)
        def _(r):
            rr = pl.ds(pl.multiple_of(r * step, step), step)
            v = dst[rr, :].astype(F32)
            for s_ in srcs:
                v = v + s_[rr, :].astype(F32)
            dst[rr, :] = v.astype(BF)

    oz = 1 - zl

    class DownSum:
        def push(self, src, dst, i, dev):
            send(src, dst, x_s.at[i], x_r.at[i], dev)

        def part(self, rel):
            xr = ring(x, rel)

            @pl.loop(0, 2)
            def _(z):
                j = xr * 2 + z
                mine = g_all[:, :, pl.ds(pl.multiple_of((2 * j + c) * 256, 256), 256)].reshape(T, 256)
                his = g_sib[:, :, pl.ds(pl.multiple_of(j * 256, 256), 256)].reshape(T, 256)
                xp_d[xr, z] = (dot_nn(act_t[0], mine) + dot_nn(act_s[0], his)).astype(BF)

        def x2(self):
            xr = ring(x, 2)
            self.push(xp_d.at[xr, 0], xh_d.at[0], 0, xdev(1))
            self.push(xp_d.at[xr, 1], xh_d.at[1], 1, xdev(3))

        def x1(self):
            xr = ring(x, 1)
            recv(xh_d.at[0], x_r.at[0], x_s.at[0], xdev(3))
            add_rows(xp_d.at[xr, 0], [xh_d.at[0]], F, 64)
            self.push(xp_d.at[xr], xf_d.at[0], 2, xdev(1))

        def x3(self):
            xr = ring(x, 3)
            recv(xh_d.at[1], x_r.at[1], x_s.at[1], xdev(1))
            add_rows(xp_d.at[xr, 1], [xh_d.at[1]], F, 64)
            self.push(xp_d.at[xr], xf_d.at[1], 3, xdev(3))

        def cross(self):
            recv(xf_d.at[0], x_r.at[2], x_s.at[2], xdev(3))
            recv(xf_d.at[1], x_r.at[3], x_s.at[3], xdev(1))
            add_rows(xp_d.at[x, oz], [xf_d.at[0, oz], xf_d.at[1, oz]], F, 64)
            self.push(xp_d.at[x, oz], xz_d, 4, zsib)

        def fin(self):
            recv(xz_d, x_r.at[4], x_s.at[4], zsib)

            @pl.loop(0, F // 64)
            def _(r):
                rr = pl.ds(pl.multiple_of(r * 64, 64), 64)
                v = xp_d[x, zl, rr, :].astype(F32) + xf_d[0, zl, rr, :].astype(F32)
                v = v + xf_d[1, zl, rr, :].astype(F32) + xz_d[rr, :].astype(F32)
                o_down[rr, :] = v.astype(BF)

    blk = pl.ds(pl.multiple_of(p * 256, 256), 256)

    class WeightSum:
        def push(self, src, dst, i, dev):
            send(src, dst, x_s.at[5 + i], x_r.at[5 + i], dev)

        def get(self, dst, i, dev):
            recv(dst, x_r.at[5 + i], x_s.at[5 + i], dev)

        def part(self, rel):
            xr = ring(x, rel)

            @pl.loop(0, 4)
            def _(i):
                z, k = i // 2, lax.rem(i, 2)
                cols = pl.ds(pl.multiple_of((xr * 2 + z) * 256, 256), 256)
                mine = n_all[c, :, :, cols].reshape(T, 256)
                his = n_all[oc, :, :, cols].reshape(T, 256)
                v = dot_nn(act_t[1 + k], mine) + dot_nn(act_s[1 + k], his)
                xp_w[xr, k, z] = v.astype(BF)

        def x2(self):
            xr = ring(x, 2)
            self.push(xp_w.at[xr, 0], xh_w.at[0], 0, xdev(1))
            self.push(xp_w.at[xr, 1], xh_w.at[1], 1, xdev(3))

        def x1i(self):
            self.push(xp_w.at[ring(x, 1), 1], xf_w.at[0, 1], 2, xdev(1))

        def x3i(self):
            self.push(xp_w.at[ring(x, 3), 0], xf_w.at[1, 0], 3, xdev(3))

        def x1d(self):
            xr = ring(x, 1)
            self.get(xh_w.at[0], 0, xdev(3))
            for z in (oz, zl):
                add_rows(xp_w.at[xr, 0, z], [xh_w.at[0, z]], F, 64)
                self.push(xp_w.at[xr, 0, z], xf_w.at[0, 0, z], 4 if z is oz else 5, xdev(1))

        def x3d(self):
            xr = ring(x, 3)
            self.get(xh_w.at[1], 1, xdev(1))
            for z in (oz, zl):
                add_rows(xp_w.at[xr, 1, z], [xh_w.at[1, z]], F, 64)
                self.push(xp_w.at[xr, 1, z], xf_w.at[1, 1, z], 6 if z is oz else 7, xdev(3))

        def cross(self):
            self.get(xf_w.at[0, 1], 2, xdev(3))
            self.get(xf_w.at[1, 0], 3, xdev(1))
            self.get(xf_w.at[0, 0, oz], 4, xdev(3))
            self.get(xf_w.at[1, 1, oz], 6, xdev(1))
            for k in (0, 1):
                add_rows(xp_w.at[x, k, oz], [xf_w.at[0, k, oz], xf_w.at[1, k, oz]], F, 64)
            self.push(xp_w.at[x, :, oz], xz_w, 8, zsib)

        def fin(self):
            self.get(xf_w.at[0, 0, zl], 5, xdev(3))
            self.get(xf_w.at[1, 1, zl], 7, xdev(1))
            self.get(xz_w, 8, zsib)
            gsum = jnp.zeros((8, 256), F32)
            for k, (o_ref, w_ref) in enumerate(((o_gate, wg), (o_up, wu))):
                def step(r, acc):
                    rr = pl.ds(pl.multiple_of(r * 64, 64), 64)
                    v = xp_w[x, k, zl, rr, :].astype(F32) + xf_w[0, k, zl, rr, :].astype(F32)
                    v = v + xf_w[1, k, zl, rr, :].astype(F32) + xz_w[k, rr, :].astype(F32)
                    o_ref[rr, :] = v.astype(BF)
                    return acc + jnp.sum((v * w_ref[rr, blk].astype(F32)).reshape(8, 8, 256), axis=0)

                gsum = lax.fori_loop(0, F // 64, step, gsum)
            gt[t] = jnp.broadcast_to(jnp.sum(gsum, axis=0, keepdims=True) / vgain[:, blk], (8, 256))
            for k in range(1, 16):
                send(gt.at[t], gt.at[t], g_s.at[0, k], g_r.at[0, k], tdev(k))

    def gain1():
        for k in range(1, 16):
            recv(gt.at[lax.rem(t + 16 - k, 16)], g_r.at[0, k], g_s.at[0, k], tdev(16 - k))
        og[p] = jnp.sum(gt[...], axis=0)
        for k in range(1, 16):
            send(og.at[p], og.at[p], g_s.at[1, k], g_r.at[1, k], pdev(k))

    def gain2():
        for k in range(1, 16):
            recv(og.at[lax.rem(p + 16 - k, 16)], g_r.at[1, k], g_s.at[1, k], pdev(16 - k))
        for k in range(16):
            o_gain[:, pl.ds(k * 256, 256)] = og[k, 0:1, :]

    def p_part(i):
        if "pp" not in begun:
            local[6].wait()
            local[7].wait()
            begun.add("pp")
        cols = pl.ds(i * 512, 512)
        v = dot_nn(acts[0], wg[:, cols]) + dot_nn(acts[1], wu[:, cols])
        part[:, :, cols] = v.astype(BF).reshape(16, 32, 512)

    class Scatter:
        def __init__(self, q, zlast):
            self.cols = pl.ds(q * QW, QW)
            self.zlast = zlast
            self.dev1 = ydev if zlast else zdev
            self.dev2 = zdev if zlast else ydev
            self.s = lambda i: r_s.at[q, i]
            self.r = lambda i: r_r.at[q, i]

        def push(self, src, dst, i, dev):
            send(src, dst, self.s(i), self.r(i), dev)

        def tt(self, k1, k2):
            return tid(k1, k2) if self.zlast else tid(k2, k1)

        def blk(self, k1, k2):
            return part.at[self.tt(k1, k2), :, self.cols]

        def hblk(self, k1, k2, h):
            return part.at[self.tt(k1, k2), pl.ds(16 * h, 16), self.cols]

        def r0(self, k):
            i = KS.index(k)
            self.push(self.hblk(2, k, 0), rh.at[i, 0, :, self.cols], 2 * i, self.dev1(1))
            self.push(self.hblk(2, k, 1), rh.at[i, 1, :, self.cols], 2 * i + 1, self.dev1(3))

        def r1(self, k, h):
            i, k1 = KS.index(k), 1 + 2 * h
            src = rh.at[i, h, :, self.cols]
            recv(src, self.r(2 * i + h), self.s(2 * i + h), self.dev1(4 - k1))
            dst = self.hblk(k1, k, h)
            dst[...] = (dst[...].astype(F32) + src[...].astype(F32)).astype(BF)
            self.push(self.blk(k1, k), rf.at[i, h, :, self.cols], 8 + 2 * i + h, self.dev1(k1))

        def r2(self, k):
            i = KS.index(k)
            for h, k1 in ((0, 3), (1, 1)):
                recv(rf.at[i, h, :, self.cols], self.r(8 + 2 * i + h), self.s(8 + 2 * i + h), self.dev1(k1))
            v = self.blk(0, k)[...].astype(F32) + rf[i, 0, :, self.cols].astype(F32)
            v = v + rf[i, 1, :, self.cols].astype(F32)
            rs[i, :, self.cols] = v.astype(BF)
            if k == 2:
                for h, k2 in ((0, 1), (1, 3)):
                    src = rs.at[i, pl.ds(16 * h, 16), self.cols]
                    self.push(src, zh_buf.at[h, :, self.cols], 16 + h, self.dev2(k2))

        def r4(self, h):
            k2 = 1 + 2 * h
            src = zh_buf.at[h, :, self.cols]
            recv(src, self.r(16 + h), self.s(16 + h), self.dev2(4 - k2))
            i = KS.index(k2)
            dst = rs.at[i, pl.ds(16 * h, 16), self.cols]
            dst[...] = (dst[...].astype(F32) + src[...].astype(F32)).astype(BF)
            self.push(rs.at[i, :, self.cols], zf_buf.at[h, :, self.cols], 18 + h, self.dev2(k2))

        def r5(self):
            for h, k2 in ((0, 3), (1, 1)):
                recv(zf_buf.at[h, :, self.cols], self.r(18 + h), self.s(18 + h), self.dev2(k2))
            v = rs[0, :, self.cols].astype(F32) + zf_buf[0, :, self.cols].astype(F32)
            gn[:, self.cols] = v + zf_buf[1, :, self.cols].astype(F32)

    def finish():
        xin = vin[...].astype(F32)
        inv = lax.rsqrt(jnp.mean(xin * xin, axis=1, keepdims=True) + 1e-05)
        dotp = jnp.zeros((32, 1), F32)
        for q in range(NQ):
            cols = pl.ds(q * QW, QW)
            unit = vin[:, cols].astype(F32) * inv
            dotp = dotp + jnp.sum(gn[:, cols] * vgain[:, cols] * unit, axis=1, keepdims=True)
        dotp = dotp * (1.0 / D)
        for q in range(NQ):
            cols = pl.ds(q * QW, QW)
            unit = vin[:, cols].astype(F32) * inv
            res = g_all[t, :, cols].astype(F32) + inv * (gn[:, cols] * vgain[:, cols] - unit * dotp)
            o_in[:, cols] = res.astype(BF)

    RA = [Scatter(q, MODES["R"][q] == "z") for q in range(NQ)]
    per_quarter = {"G": GA, "N": NA, "R": RA}
    whole = {"D": DownSum(), "W": WeightSum()}
    single = {
        "normed": normed, "nx": nx, "prefac": prefac, "gh": gh_add, "acts": act_grads, "tr": turn, "dready": d_ready,
        "wready": w_ready, "pp": p_part, "gain1": gain1, "gain2": gain2, "fin": finish,
    }
    for name, *rest in ORDER:
        if name in per_quarter:
            step, q, *ks = rest
            getattr(per_quarter[name][q], step)(*ks)
        elif name in whole:
            step, *ks = rest
            getattr(whole[name], step)(*ks)
        else:
            single[name](*rest)
    for cp in sent:
        cp.wait_send()


def deliver(*refs):
    for i in range(5):
        refs[5 + i][...] = refs[i][...]


def body(inputs, gate_pre, up_pre, grad_out, gain, w_gate, w_up, w_down):
    V = pltpu.VMEM
    DMA = pltpu.SemaphoreType.DMA
    any_spec = pl.BlockSpec(memory_space=pl.ANY)
    vm_spec = pl.BlockSpec(memory_space=pltpu.VMEM)
    outs = pl.pallas_call(
        kernel,
        out_shape=(
            jax.ShapeDtypeStruct((32, D), BF),
            jax.ShapeDtypeStruct((F, 256), BF),
            jax.ShapeDtypeStruct((F, 256), BF),
            jax.ShapeDtypeStruct((F, 256), BF),
            jax.ShapeDtypeStruct((1, D), F32),
        ),
        in_specs=[any_spec] * 8,
        out_specs=(vm_spec,) * 5,
        scratch_shapes=[
            V((32, D), BF), V((1, D), F32), V((F, T), BF), V((F, T), BF),
            V((F, D), BF), V((F, D), BF), V((F, D), BF),
            V((16, 32, D), BF), V((16, 32, D // 2), BF), V((2, 16, 32, D // 2), BF), V((32, D // 2), BF),
            V((F, T), F32), V((F, T), F32), V((F, T), F32),
            V((2, T, F), BF), V((3, F, T), BF), V((3, F, T), BF),
            V((16, 32, D), BF), V((4, 2, 16, D), BF), V((4, 2, 32, D), BF), V((4, 32, D), BF),
            V((2, 16, D), BF), V((2, 32, D), BF), V((32, D), F32),
            V((4, 2, F, 256), BF), V((2, F, 256), BF), V((2, 2, F, 256), BF), V((F, 256), BF),
            V((4, 2, 2, F, 256), BF), V((2, 2, F, 256), BF), V((2, 2, 2, F, 256), BF), V((2, F, 256), BF),
            V((16, 8, 256), F32), V((16, 8, 256), F32),
            DMA((8,)), DMA((2, NQ, 20)), DMA((2, NQ, 20)), DMA((NQ, 20)), DMA((NQ, 20)),
            DMA((14,)), DMA((14,)), DMA((12,)), DMA((12,)), DMA((2, 16)), DMA((2, 16)),
        ],
        compiler_params=pltpu.CompilerParams(
            collective_id=0, has_side_effects=True, vmem_limit_bytes=60 * 2**20
        ),
    )(inputs, gate_pre.T, up_pre.T, grad_out, gain.reshape(1, D), w_gate.T, w_up.T, w_down)
    outs = pl.pallas_call(
        deliver,
        out_shape=tuple(jax.ShapeDtypeStruct(o.shape, o.dtype) for o in outs),
        in_specs=[vm_spec] * 5,
        out_specs=(vm_spec,) * 5,
        compiler_params=pltpu.CompilerParams(vmem_limit_bytes=60 * 2**20),
    )(*outs)
    return outs[0], outs[1].T, outs[2].T, outs[3], outs[4].reshape(D)


def solution(mesh):
    return jax.shard_map(
        body,
        mesh=mesh,
        in_specs=(
            P(("dp", "tensor"), None),
            P("dp", "tensor"),
            P("dp", "tensor"),
            P(("dp", "tensor"), None),
            P(),
            P(None, "tensor"),
            P(None, "tensor"),
            P("tensor", None),
        ),
        out_specs=(
            P(("dp", "tensor"), None),
            P("dp", "tensor"),
            P("dp", "tensor"),
            P("tensor", "dp"),
            P(),
        ),
        check_vma=False,
    )
```

```python
import functools

import jax
import jax.numpy as jnp
from jax import lax
from jax.experimental import pallas as pl
from jax.experimental.pallas import tpu as pltpu
from jax.sharding import PartitionSpec as P

MESH = pl.DeviceIdType.MESH
BF = jnp.bfloat16
F32 = jnp.float32
D = 4096
F = 448
T = 512
NQ = 4
QW = D // NQ
KS = (0, 1, 3, 2)
MODES = {'G': 'zzzz', 'N': 'zzyz', 'R': 'zzzy'}
ORDER = (
    ('G', 'e0', 0), ('G', 'e0', 2), ('G', 's2', 2, 0), ('G', 's2', 0, 0), ('G', 'e0', 1), ('G', 's2', 1, 0),
    ('prefac',), ('normed',), ('hx',), ('nx',), ('N', 'e0', 2), ('G', 'e0', 3), ('G', 's2', 3, 0),
    ('G', 'f2', 2, 0, 3), ('G', 'f2', 2, 0, 1), ('G', 'f1', 0, 3), ('G', 'f1', 0, 1), ('G', 's2', 0, 3),
    ('G', 's2', 0, 1), ('G', 'f2', 0, 0, 3), ('G', 'f2', 0, 0, 1), ('G', 'f2', 1, 0, 3), ('G', 'f2', 1, 0, 1),
    ('G', 'f1', 2, 3), ('G', 's2', 2, 3), ('G', 'f1', 2, 1), ('N', 'f1', 2, 3), ('N', 'f1', 2, 1),
    ('G', 'f2', 3, 0, 3), ('G', 'f2', 3, 0, 1), ('G', 's2', 2, 1), ('G', 'f1', 1, 3), ('G', 'f1', 1, 1),
    ('G', 'f2', 0, 3, 3), ('G', 'f2', 0, 3, 1), ('N', 'e0', 3), ('G', 's2', 1, 3), ('G', 'f2', 0, 1, 3),
    ('G', 'f2', 0, 1, 1), ('G', 'f1', 3, 3), ('G', 'f1', 3, 1), ('G', 's2', 1, 1), ('G', 'e3', 0), ('G', 's2', 0, 2),
    ('G', 'f2', 2, 3, 3), ('G', 'f2', 2, 3, 1), ('N', 'e0', 1), ('G', 'e3', 2), ('N', 'e3', 2), ('G', 'e3', 1),
    ('G', 's2', 1, 2), ('G', 'f2', 2, 1, 3), ('G', 'f2', 2, 1, 1), ('N', 'e0', 0), ('G', 's2', 2, 2),
    ('N', 'f1', 3, 3), ('N', 'f1', 3, 1), ('G', 'f2', 1, 3, 3), ('G', 'f2', 1, 3, 1), ('G', 'e3', 3),
    ('G', 's2', 3, 3), ('G', 'f2', 1, 1, 3), ('G', 'f2', 1, 1, 1), ('N', 's2', 2, 0), ('G', 'f2', 0, 2, 3),
    ('G', 'f2', 0, 2, 1), ('N', 'f1', 1, 3), ('N', 'f1', 1, 1), ('G', 's2', 3, 1), ('G', 'f2', 1, 2, 3),
    ('G', 'f2', 1, 2, 1), ('G', 's2', 3, 2), ('N', 'f1', 0, 3), ('N', 'f1', 0, 1), ('G', 'f2', 2, 2, 3),
    ('G', 'f2', 2, 2, 1), ('N', 's2', 2, 3), ('N', 'e3', 3), ('N', 's2', 0, 0), ('G', 'f2', 3, 3, 3),
    ('G', 'f2', 3, 3, 1), ('N', 'f2', 2, 0, 3), ('N', 'f2', 2, 0, 1), ('N', 's2', 0, 3), ('G', 'done', 0), ('gh', 0),
    ('N', 's2', 2, 1), ('N', 'e3', 1), ('N', 's2', 0, 1), ('G', 'f2', 3, 1, 3), ('G', 'f2', 3, 1, 1),
    ('G', 'done', 1), ('gh', 1), ('dr', 0), ('D', 'part', 2), ('G', 'f2', 3, 2, 3), ('G', 'f2', 3, 2, 1), ('D', 'x2'),
    ('G', 'done', 2), ('N', 's2', 1, 0), ('N', 'e3', 0), ('N', 's2', 2, 2), ('gh', 2), ('dr', 1), ('D', 'part', 1),
    ('N', 's2', 0, 2), ('N', 'f2', 0, 0, 3), ('N', 'f2', 0, 0, 1), ('N', 'f2', 2, 3, 3), ('N', 'f2', 2, 3, 1),
    ('dr', 2), ('D', 'part', 3), ('N', 'f2', 0, 3, 3), ('N', 'f2', 0, 3, 1), ('N', 's2', 1, 3), ('N', 'f2', 0, 1, 3),
    ('N', 'f2', 0, 1, 1), ('N', 'f2', 2, 1, 3), ('N', 'f2', 2, 1, 1), ('N', 's2', 1, 1), ('G', 'done', 3), ('gh', 3),
    ('acts',), ('tr',), ('pp', 6), ('D', 'x1'), ('D', 'x3'), ('pp', 7), ('N', 'f2', 0, 2, 3), ('N', 'f2', 0, 2, 1),
    ('N', 's2', 1, 2), ('N', 'f2', 2, 2, 3), ('N', 'f2', 2, 2, 1), ('pp', 2), ('wready',), ('N', 'f2', 1, 0, 3),
    ('N', 'f2', 1, 0, 1), ('pp', 1), ('N', 'f2', 1, 3, 3), ('N', 'f2', 1, 3, 1), ('R', 'r0', 3, 2), ('R', 'r0', 3, 1),
    ('R', 'r0', 3, 3), ('R', 'r0', 3, 0), ('N', 's2', 3, 0), ('pp', 0), ('N', 's2', 3, 3), ('R', 'r0', 0, 2),
    ('pp', 3), ('N', 'f2', 1, 1, 3), ('N', 'f2', 1, 1, 1), ('dr', 3), ('D', 'part', 0), ('N', 'done', 0),
    ('W', 'part', 2), ('W', 'x2'), ('N', 'f2', 1, 2, 3), ('N', 'f2', 1, 2, 1), ('R', 'r1', 3, 2, 0),
    ('R', 'r1', 3, 2, 1), ('N', 's2', 3, 1), ('N', 's2', 3, 2), ('N', 'done', 2), ('W', 'part', 3), ('W', 'x3i'),
    ('N', 'f2', 3, 0, 3), ('N', 'f2', 3, 0, 1), ('R', 'r1', 3, 1, 0), ('R', 'r1', 3, 1, 1), ('R', 'r1', 3, 3, 0),
    ('R', 'r1', 3, 3, 1), ('R', 'r0', 0, 1), ('N', 'f2', 3, 3, 3), ('N', 'f2', 3, 3, 1), ('R', 'r0', 0, 3), ('pp', 4),
    ('R', 'r1', 3, 0, 0), ('R', 'r1', 3, 0, 1), ('R', 'r0', 0, 0), ('R', 'r0', 1, 2), ('R', 'r1', 0, 2, 0),
    ('R', 'r1', 0, 2, 1), ('D', 'cross'), ('pp', 5), ('N', 'done', 1), ('W', 'part', 1), ('N', 'f2', 3, 1, 3),
    ('N', 'f2', 3, 1, 1), ('R', 'r2', 3, 2), ('R', 'r0', 2, 2), ('W', 'x1i'), ('N', 'f2', 3, 2, 3),
    ('N', 'f2', 3, 2, 1), ('R', 'r2', 3, 1), ('R', 'r0', 2, 1), ('R', 'r1', 0, 1, 0), ('R', 'r1', 0, 1, 1),
    ('R', 'r1', 0, 3, 0), ('R', 'r1', 0, 3, 1), ('R', 'r1', 0, 0, 0), ('R', 'r1', 0, 0, 1), ('R', 'r2', 3, 3),
    ('R', 'r1', 1, 2, 0), ('R', 'r1', 1, 2, 1), ('R', 'r2', 0, 2), ('W', 'x1d'), ('W', 'x3d'), ('R', 'r2', 3, 0),
    ('R', 'r4', 3, 0), ('R', 'r4', 3, 1), ('R', 'r1', 2, 2, 0), ('R', 'r1', 2, 2, 1), ('N', 'done', 3),
    ('W', 'part', 0), ('R', 'r0', 2, 3), ('R', 'r1', 2, 1, 0), ('R', 'r1', 2, 1, 1), ('R', 'r2', 0, 1), ('D', 'fin'),
    ('R', 'r2', 0, 3), ('R', 'r0', 2, 0), ('R', 'r4', 0, 0), ('R', 'r4', 0, 1), ('R', 'r0', 1, 1), ('R', 'r2', 0, 0),
    ('R', 'r0', 1, 3), ('R', 'r0', 1, 0), ('R', 'r2', 1, 2), ('R', 'r5', 3), ('W', 'cross'), ('R', 'r2', 2, 2),
    ('R', 'r1', 2, 3, 0), ('R', 'r1', 2, 3, 1), ('R', 'r5', 0), ('R', 'r2', 2, 1), ('R', 'r1', 2, 0, 0),
    ('R', 'r1', 2, 0, 1), ('R', 'r1', 1, 1, 0), ('R', 'r1', 1, 1, 1), ('R', 'r1', 1, 3, 0), ('R', 'r1', 1, 3, 1),
    ('R', 'r1', 1, 0, 0), ('R', 'r1', 1, 0, 1), ('R', 'r2', 2, 3), ('R', 'r2', 2, 0), ('W', 'own'), ('R', 'r2', 1, 1),
    ('R', 'r4', 1, 0), ('R', 'r2', 1, 3), ('R', 'r4', 1, 1), ('R', 'r2', 1, 0), ('W', 'fin'), ('R', 'r4', 2, 0),
    ('R', 'r4', 2, 1), ('gain1',), ('R', 'r5', 1), ('R', 'r5', 2), ('fin',), ('gain2',),
)
RELS = (2, 1, 3, 0)


def dot_nt(a, b):
    return lax.dot_general(a, b, (((1,), (1,)), ((), ())), preferred_element_type=F32)


def dot_nn(a, b):
    return lax.dot_general(a, b, (((1,), (0,)), ((), ())), preferred_element_type=F32)


def kernel(
    inputs, gate_pre, up_pre, grad_out, gain, w_gate, w_up, w_down,
    o_in, o_gate, o_up, o_down, o_gain,
    vin, vgain, vgp, vup, wg, wu, wd,
    g_all, g_sib, n_all, n_send, a1, a2, gh, acts, act_t, act_s,
    part, rh, rf, rs, zh_buf, zf_buf, gn,
    xp_d, xh_d, xf_d, xz_d, xp_w, xh_w, xf_w, xz_w,
    gt, og,
    loc, ag_s, ag_r, r_s, r_r, x_s, x_r, c_s, c_r, g_s, g_r,
):
    p = lax.axis_index("dp")
    t = lax.axis_index("tensor")
    x, zl, c = p // 4, lax.rem(p // 2, 2), lax.rem(p, 2)
    y, zh = t // 4, lax.rem(t, 4)
    oc = 1 - c
    sib = (x * 4 + zl * 2 + oc, t)
    zsib = (x * 4 + (1 - zl) * 2 + c, t)

    def ring(v, k):
        return lax.rem(v + k, 4)

    def ydev(k):
        return (p, ring(y, k) * 4 + zh)

    def zdev(k):
        return (p, y * 4 + ring(zh, k))

    def xdev(k):
        return (ring(x, k) * 4 + zl * 2 + c, t)

    def tdev(k):
        return (p, lax.rem(t + k, 16))

    def pdev(k):
        return (lax.rem(p + k, 16), t)

    def tid(ky, kz):
        return ring(y, ky) * 4 + ring(zh, kz)

    sent = []

    def send(src, dst, ss, rs_, dev):
        cp = pltpu.make_async_remote_copy(
            src_ref=src, dst_ref=dst, send_sem=ss, recv_sem=rs_, device_id=dev, device_id_type=MESH
        )
        cp.start()
        return cp

    def wait_sent(ref, sem, dev):
        pltpu.make_async_remote_copy(
            src_ref=ref, dst_ref=ref, send_sem=sem, recv_sem=sem, device_id=dev, device_id_type=MESH
        ).wait_send()

    def recv(dst, sem, ss, dev):
        pltpu.make_async_remote_copy(
            src_ref=dst, dst_ref=dst, send_sem=ss, recv_sem=sem, device_id=dev, device_id_type=MESH
        ).wait_recv()

    barrier = pltpu.get_barrier_semaphore()
    partners = [f(k) for f in (ydev, zdev, xdev) for k in (1, 3)] + [sib, zsib]
    for dev in partners:
        pl.semaphore_signal(barrier, inc=1, device_id=dev, device_id_type=MESH)
    local = []
    for i, (src, dst) in enumerate((
        (inputs, vin), (gain, vgain), (gate_pre, vgp), (up_pre, vup),
        (grad_out, g_all.at[t]), (w_down, wd), (w_gate, wg), (w_up, wu),
    )):
        cp = pltpu.make_async_copy(src, dst, loc.at[i])
        cp.start()
        local.append(cp)

    local[0].wait()
    local[1].wait()
    xin = vin[...].astype(F32)
    inv = lax.rsqrt(jnp.mean(xin * xin, axis=1, keepdims=True) + 1e-05)

    @pl.loop(0, 8)
    def _(j):
        own = pl.ds(pl.multiple_of((2 * j + c) * 256, 256), 256)
        oth = pl.ds(pl.multiple_of((2 * j + oc) * 256, 256), 256)
        col = pl.ds(pl.multiple_of(j * 256, 256), 256)
        n_all[c, t, :, col] = (vin[:, own].astype(F32) * inv * vgain[:, own]).astype(BF)
        n_send[:, col] = (vin[:, oth].astype(F32) * inv * vgain[:, oth]).astype(BF)
    pl.semaphore_wait(barrier, len(partners))

    class Gather:
        def __init__(self, item, q, zfirst, piece, half, group, own):
            self.piece_t, self.half_t, self.group_t, self.own = piece, half, group, own
            self.zfirst = zfirst
            self.sem = ag_s.at[item, q]
            self.s = lambda i: self.sem
            self.r = lambda i: ag_r.at[item, q, i]
            self.dev1 = zdev if zfirst else ydev
            self.dev2 = ydev if zfirst else zdev

        def tt(self, ku, kv):
            return tid(kv, ku) if self.zfirst else tid(ku, kv)

        def piece(self, ku, kv):
            return self.piece_t(self.tt(ku, kv))

        def half(self, ku, kv, h):
            return self.half_t(self.tt(ku, kv), h)

        def push(self, src, dst, i, dev):
            send(src, dst, self.s(i), self.r(i), dev)

        def e0(self):
            ref = self.piece(0, 0)
            src = ref if self.own is None else self.own
            self.push(src, ref, 1, self.dev1(1))
            self.push(src, ref, 0, self.dev1(3))

        def s2(self, k):
            i = KS.index(k)
            ref = self.piece(k, 0)
            src = ref if self.own is None or k else self.own
            self.push(src, ref, 3 + 2 * i + 1, self.dev2(1))
            self.push(src, ref, 3 + 2 * i, self.dev2(3))

        def f1(self, k):
            h = k // 2
            recv(self.piece(k, 0), self.r(h), self.s(h), self.dev1(k))
            self.push(self.half(k, 0, h), self.half(k, 0, h), 2, self.dev1(4 - k))

        def f2(self, k, kk):
            i, h = KS.index(k), kk // 2
            recv(self.piece(k, kk), self.r(3 + 2 * i + h), self.sem, self.dev2(kk))
            self.push(self.half(k, kk, h), self.half(k, kk, h), 11, self.dev2(4 - kk))

        def e3(self):
            recv(self.piece(2, 0), self.r(2), self.sem, self.dev1(1))

        def done(self):
            recv(self.group_t(4), self.r(11), self.sem, self.dev2(1))

        def settle(self):
            wait_sent(self.group_t(15), self.sem, self.dev1(1))

    def g_cols(q):
        return pl.ds(pl.multiple_of(ring(x, RELS[q]) * QW, QW), QW)

    def n_cols(q):
        return pl.ds(pl.multiple_of(ring(x, RELS[q]) * 512, 512), 512)

    GA = [
        Gather(
            0, q, MODES['G'][q] == 'z',
            lambda tt, q=q: g_all.at[tt, :, g_cols(q)],
            lambda tt, h, q=q: g_all.at[tt, pl.ds(16 * h, 16), g_cols(q)],
            lambda n, q=q: g_all.at[pl.ds(0, n), :, g_cols(q)],
            grad_out.at[:, g_cols(q)],
        )
        for q in range(NQ)
    ]
    NA = [
        Gather(
            1, q, MODES['N'][q] == 'z',
            lambda tt, q=q: n_all.at[:, tt, :, n_cols(q)],
            lambda tt, h, q=q: n_all.at[h, tt, :, n_cols(q)],
            lambda n, q=q: n_all.at[:, pl.ds(0, n), :, n_cols(q)],
            None,
        )
        for q in range(NQ)
    ]

    def normed():
        sent.append(send(n_send, n_all.at[c, t], c_s.at[0], c_r.at[0], sib))

    def nx():
        recv(n_all.at[oc, t], c_r.at[0], c_s.at[0], sib)

    def prefac():
        local[2].wait()
        local[3].wait()

        @pl.loop(0, F // 64)
        def _(r):
            rows = pl.ds(pl.multiple_of(r * 64, 64), 64)
            gp = vgp[rows, :].astype(F32)
            up = vup[rows, :].astype(F32)
            s = jax.nn.sigmoid(gp)
            gs = gp * s
            a2[rows, :] = gs
            a1[rows, :] = up * (s * (1.0 + gp * (1.0 - s)))
            act_t[0, rows, :] = (gs * up).astype(BF)

        sent.append(send(act_t.at[0], act_s.at[0], c_s.at[1], c_r.at[1], sib))

    begun = set()

    def gh_add(q):
        if "gh" not in begun:
            local[4].wait()
            local[5].wait()
        v = dot_nt(wd[:, g_cols(q)], g_all[:, :, g_cols(q)].reshape(T, QW))
        gh[...] = v if "gh" not in begun else gh[...] + v
        begun.add("gh")
        for i in range(2):
            j = 2 * ring(x, RELS[q]) + i
            src = g_all.at[:, :, pl.ds(pl.multiple_of((2 * j + oc) * 256, 256), 256)]
            dst = g_sib.at[:, :, pl.ds(pl.multiple_of(j * 256, 256), 256)]
            sent.append(send(src, dst, c_s.at[4 + 2 * q + i], c_r.at[4 + 2 * q + i], sib))

    def act_grads():
        @pl.loop(0, F // 64)
        def _(r):
            rows = pl.ds(pl.multiple_of(r * 64, 64), 64)
            v = gh[rows, :]
            act_t[1, rows, :] = (v * a1[rows, :]).astype(BF)
            act_t[2, rows, :] = (v * a2[rows, :]).astype(BF)

        for i in (1, 2):
            sent.append(send(act_t.at[i], act_s.at[i], c_s.at[1 + i], c_r.at[1 + i], sib))

    def turn():
        @pl.loop(0, 4)
        def _(r):
            rows = pl.ds(pl.multiple_of(r * 128, 128), 128)
            for i in (1, 2):
                acts[i - 1, rows, :] = act_t[i, :, rows].T

    def h_ready():
        recv(act_s.at[0], c_r.at[1], c_s.at[1], sib)

    def d_ready(q):
        for i in range(2):
            j = 2 * ring(x, RELS[q]) + i
            dst = g_sib.at[:, :, pl.ds(pl.multiple_of(j * 256, 256), 256)]
            recv(dst, c_r.at[4 + 2 * q + i], c_s.at[4 + 2 * q + i], sib)

    def w_ready():
        for i in (1, 2):
            recv(act_s.at[i], c_r.at[1 + i], c_s.at[1 + i], sib)

    def add_rows(dst, srcs, rows, step):
        @pl.loop(0, rows // step)
        def _(r):
            rr = pl.ds(pl.multiple_of(r * step, step), step)
            v = dst[rr, :].astype(F32)
            for s_ in srcs:
                v = v + s_[rr, :].astype(F32)
            dst[rr, :] = v.astype(BF)

    oz = 1 - zl

    class DownSum:
        def push(self, src, dst, i, dev):
            sent.append(send(src, dst, x_s.at[i], x_r.at[i], dev))

        def part(self, rel):
            xr = ring(x, rel)

            @pl.loop(0, 2)
            def _(z):
                j = xr * 2 + z
                mine = g_all[:, :, pl.ds(pl.multiple_of((2 * j + c) * 256, 256), 256)].reshape(T, 256)
                his = g_sib[:, :, pl.ds(pl.multiple_of(j * 256, 256), 256)].reshape(T, 256)
                xp_d[xr, z] = (dot_nn(act_t[0], mine) + dot_nn(act_s[0], his)).astype(BF)

        def x2(self):
            xr = ring(x, 2)
            self.push(xp_d.at[xr, 0], xh_d.at[0], 0, xdev(1))
            self.push(xp_d.at[xr, 1], xh_d.at[1], 1, xdev(3))

        def x1(self):
            xr = ring(x, 1)
            recv(xh_d.at[0], x_r.at[0], x_s.at[0], xdev(3))
            add_rows(xp_d.at[xr, 0], [xh_d.at[0]], F, 64)
            self.push(xp_d.at[xr], xf_d.at[0], 2, xdev(1))

        def x3(self):
            xr = ring(x, 3)
            recv(xh_d.at[1], x_r.at[1], x_s.at[1], xdev(1))
            add_rows(xp_d.at[xr, 1], [xh_d.at[1]], F, 64)
            self.push(xp_d.at[xr], xf_d.at[1], 3, xdev(3))

        def cross(self):
            recv(xf_d.at[0], x_r.at[2], x_s.at[2], xdev(3))
            recv(xf_d.at[1], x_r.at[3], x_s.at[3], xdev(1))
            add_rows(xp_d.at[x, oz], [xf_d.at[0, oz], xf_d.at[1, oz]], F, 64)
            self.push(xp_d.at[x, oz], xz_d, 4, zsib)

        def fin(self):
            recv(xz_d, x_r.at[4], x_s.at[4], zsib)

            @pl.loop(0, F // 64)
            def _(r):
                rr = pl.ds(pl.multiple_of(r * 64, 64), 64)
                v = xp_d[x, zl, rr, :].astype(F32) + xf_d[0, zl, rr, :].astype(F32)
                v = v + xf_d[1, zl, rr, :].astype(F32) + xz_d[rr, :].astype(F32)
                o_down[rr, :] = v.astype(BF)


    class WeightSum:
        def push(self, src, dst, i, dev):
            sent.append(send(src, dst, x_s.at[5 + i], x_r.at[5 + i], dev))

        def get(self, dst, i, dev):
            recv(dst, x_r.at[5 + i], x_s.at[5 + i], dev)

        def part(self, rel):
            xr = ring(x, rel)

            @pl.loop(0, 4)
            def _(i):
                z, k = i // 2, lax.rem(i, 2)
                cols = pl.ds(pl.multiple_of((xr * 2 + z) * 256, 256), 256)
                mine = n_all[c, :, :, cols].reshape(T, 256)
                his = n_all[oc, :, :, cols].reshape(T, 256)
                v = dot_nn(act_t[1 + k], mine) + dot_nn(act_s[1 + k], his)
                xp_w[xr, k, z] = v.astype(BF)

        def x2(self):
            xr = ring(x, 2)
            self.push(xp_w.at[xr, 0], xh_w.at[0], 0, xdev(1))
            self.push(xp_w.at[xr, 1], xh_w.at[1], 1, xdev(3))

        def x1i(self):
            self.push(xp_w.at[ring(x, 1), 1, oz], xf_w.at[0, 1, oz], 2, xdev(1))

        def x3i(self):
            self.push(xp_w.at[ring(x, 3), 0, oz], xf_w.at[1, 0, oz], 3, xdev(3))

        def x1d(self):
            xr = ring(x, 1)
            self.get(xh_w.at[0], 0, xdev(3))
            add_rows(xp_w.at[xr, 0, oz], [xh_w.at[0, oz]], F, 64)
            self.push(xp_w.at[xr, 0, oz], xf_w.at[0, 0, oz], 4, xdev(1))
            self.push(xp_w.at[xr, 1, zl], xf_w.at[0, 1, zl], 9, xdev(1))
            add_rows(xp_w.at[xr, 0, zl], [xh_w.at[0, zl]], F, 64)
            self.push(xp_w.at[xr, 0, zl], xf_w.at[0, 0, zl], 5, xdev(1))

        def x3d(self):
            xr = ring(x, 3)
            self.get(xh_w.at[1], 1, xdev(1))
            add_rows(xp_w.at[xr, 1, oz], [xh_w.at[1, oz]], F, 64)
            self.push(xp_w.at[xr, 1, oz], xf_w.at[1, 1, oz], 6, xdev(3))
            self.push(xp_w.at[xr, 0, zl], xf_w.at[1, 0, zl], 10, xdev(3))
            add_rows(xp_w.at[xr, 1, zl], [xh_w.at[1, zl]], F, 64)
            self.push(xp_w.at[xr, 1, zl], xf_w.at[1, 1, zl], 7, xdev(3))

        def gather_sum(self, z):
            cols = pl.ds(pl.multiple_of((x * 4 + z * 2 + c) * 256, 256), 256)
            gsum = jnp.zeros((8, 256), F32)
            for k, w_ref in enumerate((wg, wu)):
                def step(r, acc):
                    rr = pl.ds(pl.multiple_of(r * 64, 64), 64)
                    v = xp_w[x, k, z, rr, :].astype(F32) + xf_w[0, k, z, rr, :].astype(F32)
                    v = v + xf_w[1, k, z, rr, :].astype(F32)
                    xp_w[x, k, z, rr, :] = v.astype(BF)
                    return acc + jnp.sum((v * w_ref[rr, cols].astype(F32)).reshape(8, 8, 256), axis=0)

                gsum = lax.fori_loop(0, F // 64, step, gsum)
            gt[t, pl.ds(z, 1), :] = jnp.sum(gsum, axis=0, keepdims=True) / vgain[:, cols]

        def cross(self):
            self.get(xf_w.at[0, 1, oz], 2, xdev(3))
            self.get(xf_w.at[1, 0, oz], 3, xdev(1))
            self.get(xf_w.at[0, 0, oz], 4, xdev(3))
            self.get(xf_w.at[1, 1, oz], 6, xdev(1))
            gt[t] = jnp.zeros((8, 256), F32)
            self.gather_sum(oz)
            self.push(xp_w.at[x, :, oz], xz_w, 8, zsib)

        def own(self):
            self.get(xf_w.at[0, 1, zl], 9, xdev(3))
            self.get(xf_w.at[1, 0, zl], 10, xdev(1))
            self.get(xf_w.at[0, 0, zl], 5, xdev(3))
            self.get(xf_w.at[1, 1, zl], 7, xdev(1))
            self.gather_sum(zl)
            for k in range(1, 16):
                send(gt.at[t], gt.at[t], g_s.at[0], g_r.at[0], tdev(k))

        def fin(self):
            self.get(xz_w, 8, zsib)
            for k, o_ref in enumerate((o_gate, o_up)):
                @pl.loop(0, F // 64)
                def _(r):
                    rr = pl.ds(pl.multiple_of(r * 64, 64), 64)
                    o_ref[rr, :] = (xp_w[x, k, zl, rr, :].astype(F32) + xz_w[k, rr, :].astype(F32)).astype(BF)


    def gain1():
        recv(gt.at[pl.ds(0, 15)], g_r.at[0], g_s.at[0], tdev(1))
        og[p] = jnp.sum(gt[...], axis=0)
        for k in range(1, 16):
            send(og.at[p], og.at[p], g_s.at[1], g_r.at[1], pdev(k))

    def gain2():
        recv(og.at[pl.ds(0, 15)], g_r.at[1], g_s.at[1], pdev(1))
        for k in range(16):
            z, k0 = (k // 2) % 2, k - k % 4 + k % 2
            o_gain[:, pl.ds(k * 256, 256)] = og[k0, z : z + 1, :] + og[k0 + 2, z : z + 1, :]

    def p_part(i):
        if "pp" not in begun:
            local[6].wait()
            local[7].wait()
            begun.add("pp")
        cols = pl.ds(i * 512, 512)
        v = dot_nn(acts[0], wg[:, cols]) + dot_nn(acts[1], wu[:, cols])
        part[:, :, cols] = v.astype(BF).reshape(16, 32, 512)

    class Scatter:
        def __init__(self, q, zlast):
            self.cols = pl.ds(q * QW, QW)
            self.zlast = zlast
            self.dev1 = ydev if zlast else zdev
            self.dev2 = zdev if zlast else ydev
            self.sem = r_s.at[q]
            self.s = lambda i: self.sem
            self.r = lambda i: r_r.at[q, i]

        def push(self, src, dst, i, dev):
            send(src, dst, self.s(i), self.r(i), dev)

        def tt(self, k1, k2):
            return tid(k1, k2) if self.zlast else tid(k2, k1)

        def blk(self, k1, k2):
            return part.at[self.tt(k1, k2), :, self.cols]

        def hblk(self, k1, k2, h):
            return part.at[self.tt(k1, k2), pl.ds(16 * h, 16), self.cols]

        def r0(self, k):
            i = KS.index(k)
            self.push(self.hblk(2, k, 0), rh.at[i, 0, :, self.cols], 2 * i, self.dev1(1))
            self.push(self.hblk(2, k, 1), rh.at[i, 1, :, self.cols], 2 * i + 1, self.dev1(3))

        def r1(self, k, h):
            i, k1 = KS.index(k), 1 + 2 * h
            src = rh.at[i, h, :, self.cols]
            recv(src, self.r(2 * i + h), self.s(2 * i + h), self.dev1(4 - k1))
            dst = self.hblk(k1, k, h)
            dst[...] = (dst[...].astype(F32) + src[...].astype(F32)).astype(BF)
            self.push(self.blk(k1, k), rf.at[i, h, :, self.cols], 8 + i, self.dev1(k1))

        def r2(self, k):
            i = KS.index(k)
            recv(rf.at[i, :, :, self.cols], self.r(8 + i), self.sem, self.dev1(1))
            v = self.blk(0, k)[...].astype(F32) + rf[i, 0, :, self.cols].astype(F32)
            v = v + rf[i, 1, :, self.cols].astype(F32)
            rs[i, :, self.cols] = v.astype(BF)
            if k == 2:
                for h, k2 in ((0, 1), (1, 3)):
                    src = rs.at[i, pl.ds(16 * h, 16), self.cols]
                    self.push(src, zh_buf.at[h, :, self.cols], 12 + h, self.dev2(k2))

        def r4(self, h):
            k2 = 1 + 2 * h
            src = zh_buf.at[h, :, self.cols]
            recv(src, self.r(12 + h), self.sem, self.dev2(4 - k2))
            i = KS.index(k2)
            dst = rs.at[i, pl.ds(16 * h, 16), self.cols]
            dst[...] = (dst[...].astype(F32) + src[...].astype(F32)).astype(BF)
            self.push(rs.at[i, :, self.cols], zf_buf.at[h, :, self.cols], 14, self.dev2(k2))

        def r5(self):
            recv(zf_buf.at[:, :, self.cols], self.r(14), self.sem, self.dev2(1))
            v = rs[0, :, self.cols].astype(F32) + zf_buf[0, :, self.cols].astype(F32)
            gn[:, self.cols] = v + zf_buf[1, :, self.cols].astype(F32)

        def settle(self):
            wait_sent(part.at[pl.ds(0, 15), :, self.cols], self.sem, self.dev1(1))

    def finish():
        xin = vin[...].astype(F32)
        inv = lax.rsqrt(jnp.mean(xin * xin, axis=1, keepdims=True) + 1e-05)
        dotp = jnp.zeros((32, 1), F32)
        for q in range(NQ):
            cols = pl.ds(q * QW, QW)
            unit = vin[:, cols].astype(F32) * inv
            dotp = dotp + jnp.sum(gn[:, cols] * vgain[:, cols] * unit, axis=1, keepdims=True)
        dotp = dotp * (1.0 / D)
        for q in range(NQ):
            cols = pl.ds(q * QW, QW)
            unit = vin[:, cols].astype(F32) * inv
            res = g_all[t, :, cols].astype(F32) + inv * (gn[:, cols] * vgain[:, cols] - unit * dotp)
            o_in[:, cols] = res.astype(BF)

    RA = [Scatter(q, MODES["R"][q] == "z") for q in range(NQ)]
    per_quarter = {"G": GA, "N": NA, "R": RA}
    whole = {"D": DownSum(), "W": WeightSum()}
    single = {
        "normed": normed, "nx": nx, "prefac": prefac, "gh": gh_add, "acts": act_grads, "tr": turn, "hx": h_ready, "dr": d_ready,
        "wready": w_ready, "pp": p_part, "gain1": gain1, "gain2": gain2, "fin": finish,
    }
    for name, *rest in ORDER:
        if name in per_quarter:
            step, q, *ks = rest
            getattr(per_quarter[name][q], step)(*ks)
        elif name in whole:
            step, *ks = rest
            getattr(whole[name], step)(*ks)
        else:
            single[name](*rest)
    for q in range(NQ):
        GA[q].settle()
        NA[q].settle()
        RA[q].settle()
    wait_sent(gt.at[pl.ds(0, 15)], g_s.at[0], tdev(1))
    wait_sent(og.at[pl.ds(0, 15)], g_s.at[1], pdev(1))
    for cp in sent:
        cp.wait_send()


def deliver(*refs):
    copies = [pltpu.make_async_copy(refs[i], refs[5 + i], refs[10].at[i]) for i in range(5)]
    for cp in copies:
        cp.start()
    for cp in copies:
        cp.wait()


def body(inputs, gate_pre, up_pre, grad_out, gain, w_gate, w_up, w_down):
    V = pltpu.VMEM
    DMA = pltpu.SemaphoreType.DMA
    any_spec = pl.BlockSpec(memory_space=pl.ANY)
    vm_spec = pl.BlockSpec(memory_space=pltpu.VMEM)
    outs = pl.pallas_call(
        kernel,
        out_shape=(
            V((32, D), BF),
            V((F, 256), BF),
            V((F, 256), BF),
            V((F, 256), BF),
            V((1, D), F32),
        ),
        in_specs=[any_spec] * 8,
        out_specs=(vm_spec,) * 5,
        scratch_shapes=[
            V((32, D), BF), V((1, D), F32), V((F, T), BF), V((F, T), BF),
            V((F, D), BF), V((F, D), BF), V((F, D), BF),
            V((16, 32, D), BF), V((16, 32, D // 2), BF), V((2, 16, 32, D // 2), BF), V((32, D // 2), BF),
            V((F, T), F32), V((F, T), F32), V((F, T), F32),
            V((2, T, F), BF), V((3, F, T), BF), V((3, F, T), BF),
            V((16, 32, D), BF), V((4, 2, 16, D), BF), V((4, 2, 32, D), BF), V((4, 32, D), BF),
            V((2, 16, D), BF), V((2, 32, D), BF), V((32, D), F32),
            V((4, 2, F, 256), BF), V((2, F, 256), BF), V((2, 2, F, 256), BF), V((F, 256), BF),
            V((4, 2, 2, F, 256), BF), V((2, 2, F, 256), BF), V((2, 2, 2, F, 256), BF), V((2, F, 256), BF),
            V((16, 8, 256), F32), V((16, 8, 256), F32),
            DMA((8,)), DMA((2, NQ)), DMA((2, NQ, 12)), DMA((NQ,)), DMA((NQ, 15)),
            DMA((16,)), DMA((16,)), DMA((12,)), DMA((12,)), DMA((2,)), DMA((2,)),
        ],
        compiler_params=pltpu.CompilerParams(
            collective_id=0, has_side_effects=True, vmem_limit_bytes=56 * 2**20
        ),
    )(inputs, gate_pre.T, up_pre.T, grad_out, gain.reshape(1, D), w_gate.T, w_up.T, w_down)
    outs = pl.pallas_call(
        deliver,
        out_shape=tuple(jax.ShapeDtypeStruct(o.shape, o.dtype) for o in outs),
        in_specs=[vm_spec] * 5,
        out_specs=(any_spec,) * 5,
        scratch_shapes=[DMA((5,))],
        compiler_params=pltpu.CompilerParams(vmem_limit_bytes=40 * 2**20),
    )(*[pltpu.with_memory_space_constraint(o, pltpu.VMEM) for o in outs])
    return outs[0], outs[1].T, outs[2].T, outs[3], outs[4].reshape(D)


def solution(mesh):
    return jax.shard_map(
        body,
        mesh=mesh,
        in_specs=(
            P(("dp", "tensor"), None),
            P("dp", "tensor"),
            P("dp", "tensor"),
            P(("dp", "tensor"), None),
            P(),
            P(None, "tensor"),
            P(None, "tensor"),
            P("tensor", None),
        ),
        out_specs=(
            P(("dp", "tensor"), None),
            P("dp", "tensor"),
            P("dp", "tensor"),
            P("tensor", "dp"),
            P(),
        ),
        check_vma=False,
    )
```

```python
import functools

import jax
import jax.numpy as jnp
from jax import lax
from jax.experimental import pallas as pl
from jax.experimental.pallas import tpu as pltpu
from jax.sharding import PartitionSpec as P

MESH = pl.DeviceIdType.MESH
BF = jnp.bfloat16
F32 = jnp.float32
D = 4096
F = 448
T = 512
NQ = 4
QW = D // NQ
KS = (0, 1, 3, 2)
MODES = {'G': 'zzzz', 'N': 'zzyz', 'R': 'zzzy'}
RW = (5, 13, 6, 8)
ORDER = (
    ('G', 'e0', 0), ('G', 'e0', 3), ('G', 's2', 3, 0), ('G', 'e0', 1), ('G', 's2', 1, 0), ('G', 'e0', 2),
    ('G', 's2', 2, 0), ('prefac',), ('normed',), ('G', 's2', 0, 0), ('hx',), ('nx',), ('N', 'e0', 2),
    ('G', 'f2', 3, 0, 3), ('G', 'f2', 3, 0, 1), ('G', 'f1', 0, 3), ('G', 'f1', 0, 1), ('G', 's2', 0, 3),
    ('G', 's2', 0, 1), ('G', 'f2', 1, 0, 3), ('G', 'f2', 1, 0, 1), ('G', 'f2', 2, 0, 3), ('G', 'f2', 2, 0, 1),
    ('G', 'f1', 3, 3), ('G', 'f1', 3, 1), ('G', 'f2', 0, 0, 3), ('G', 'f2', 0, 0, 1), ('G', 's2', 3, 3),
    ('N', 'f1', 2, 3), ('N', 'f1', 2, 1), ('G', 'f1', 1, 3), ('G', 'f1', 1, 1), ('G', 's2', 1, 3),
    ('G', 'f2', 0, 3, 3), ('G', 'f2', 0, 3, 1), ('G', 'f2', 0, 1, 3), ('N', 'e0', 3), ('G', 'f2', 0, 1, 1),
    ('G', 'f1', 2, 3), ('G', 'f1', 2, 1), ('G', 's2', 2, 3), ('G', 'e3', 0), ('G', 's2', 0, 2), ('G', 'e3', 3),
    ('G', 'f2', 3, 3, 3), ('G', 'f2', 3, 3, 1), ('N', 'e0', 1), ('N', 'e3', 2), ('G', 's2', 2, 1), ('G', 'e3', 1),
    ('G', 'f2', 1, 3, 3), ('G', 'f2', 1, 3, 1), ('G', 's2', 1, 1), ('N', 'e0', 0), ('N', 'f1', 3, 3),
    ('N', 'f1', 3, 1), ('G', 's2', 1, 2), ('G', 'f2', 2, 3, 3), ('G', 'f2', 2, 3, 1), ('G', 'e3', 2),
    ('G', 'f2', 0, 2, 3), ('G', 'f2', 0, 2, 1), ('G', 's2', 2, 2), ('N', 's2', 2, 0), ('N', 'f1', 1, 3),
    ('N', 'f1', 1, 1), ('G', 'f2', 2, 1, 3), ('G', 'f2', 2, 1, 1), ('G', 's2', 3, 1), ('G', 'f2', 1, 1, 3),
    ('G', 'f2', 1, 1, 1), ('N', 'f1', 0, 3), ('N', 'f1', 0, 1), ('G', 's2', 3, 2), ('G', 'f2', 1, 2, 3),
    ('G', 'f2', 1, 2, 1), ('N', 'e3', 3), ('N', 's2', 2, 3), ('G', 'done', 0), ('gh', 0), ('N', 's2', 0, 0),
    ('G', 'f2', 2, 2, 3), ('G', 'f2', 2, 2, 1), ('N', 'f2', 2, 0, 3), ('N', 'f2', 2, 0, 1), ('dr', 0),
    ('D', 'part', 2), ('G', 'f2', 3, 1, 3), ('G', 'f2', 3, 1, 1), ('D', 'x2'), ('N', 's2', 0, 3), ('N', 'e3', 1),
    ('N', 's2', 2, 1), ('N', 'e3', 0), ('N', 's2', 0, 1), ('G', 'f2', 3, 2, 3), ('G', 'f2', 3, 2, 1),
    ('G', 'done', 1), ('gh', 1), ('N', 's2', 2, 2), ('N', 's2', 0, 2), ('N', 'f2', 2, 3, 3), ('N', 'f2', 2, 3, 1),
    ('N', 'f2', 0, 0, 3), ('N', 'f2', 0, 0, 1), ('G', 'done', 2), ('gh', 2), ('dr', 1), ('D', 'part', 1),
    ('N', 's2', 1, 0), ('N', 'f2', 0, 3, 3), ('N', 'f2', 0, 3, 1), ('dr', 2), ('D', 'part', 3), ('D', 'x1'),
    ('D', 'x3'), ('N', 'f2', 2, 1, 3), ('G', 'done', 3), ('N', 'f2', 2, 1, 1), ('N', 's2', 1, 3), ('gh', 3),
    ('N', 's2', 1, 1), ('acts',), ('N', 'f2', 0, 1, 3), ('N', 'f2', 0, 1, 1), ('N', 'f2', 0, 2, 3),
    ('N', 'f2', 0, 2, 1), ('tr',), ('pp', 6), ('N', 'f2', 2, 2, 3), ('N', 'f2', 2, 2, 1), ('pp', 2),
    ('N', 's2', 1, 2), ('N', 'f2', 1, 0, 3), ('N', 'f2', 1, 0, 1), ('pp', 7), ('wready',), ('R', 'r0', 3, 2),
    ('R', 'r0', 3, 1), ('R', 'r0', 3, 3), ('R', 'r0', 3, 0), ('pp', 4), ('N', 's2', 3, 0), ('N', 'f2', 1, 3, 3),
    ('N', 'f2', 1, 3, 1), ('pp', 1), ('pp', 0), ('N', 's2', 3, 3), ('N', 'f2', 1, 1, 3), ('N', 'f2', 1, 1, 1),
    ('R', 'r0', 0, 2), ('pp', 3), ('N', 'done', 0), ('W', 'part', 2), ('N', 's2', 3, 1), ('R', 'r1', 3, 2, 0),
    ('N', 's2', 3, 2), ('R', 'r1', 3, 2, 1), ('R', 'r1', 3, 1, 0), ('R', 'r1', 3, 1, 1), ('R', 'r1', 3, 3, 0),
    ('R', 'r1', 3, 3, 1), ('N', 'f2', 1, 2, 3), ('N', 'f2', 1, 2, 1), ('R', 'r0', 0, 1), ('R', 'r0', 0, 3),
    ('W', 'x2'), ('dr', 3), ('D', 'part', 0), ('D', 'cross'), ('R', 'r1', 3, 0, 0), ('R', 'r1', 3, 0, 1),
    ('R', 'r0', 0, 0), ('R', 'r0', 1, 2), ('pp', 5), ('R', 'r0', 2, 2), ('R', 'r0', 2, 1), ('N', 'f2', 3, 0, 3),
    ('N', 'f2', 3, 0, 1), ('N', 'f2', 3, 3, 3), ('N', 'f2', 3, 3, 1), ('N', 'done', 2), ('R', 'r1', 0, 2, 0),
    ('R', 'r1', 0, 2, 1), ('W', 'part', 3), ('R', 'r0', 2, 3), ('W', 'x3i'), ('N', 'f2', 3, 1, 3),
    ('N', 'f2', 3, 1, 1), ('N', 'f2', 3, 2, 3), ('N', 'f2', 3, 2, 1), ('R', 'r2', 3, 2), ('N', 'done', 1),
    ('W', 'part', 1), ('R', 'r1', 1, 2, 0), ('R', 'r1', 1, 2, 1), ('R', 'r1', 0, 1, 0), ('R', 'r1', 0, 1, 1),
    ('R', 'r1', 0, 3, 0), ('R', 'r1', 2, 2, 0), ('R', 'r1', 2, 2, 1), ('R', 'r1', 0, 3, 1), ('R', 'r1', 0, 0, 0),
    ('R', 'r1', 2, 1, 0), ('R', 'r1', 2, 1, 1), ('R', 'r1', 0, 0, 1), ('W', 'x1i'), ('R', 'r2', 3, 1),
    ('R', 'r2', 3, 3), ('R', 'r2', 0, 2), ('W', 'x1d'), ('R', 'r1', 2, 3, 0), ('R', 'r1', 2, 3, 1), ('W', 'x3d'),
    ('N', 'done', 3), ('W', 'part', 0), ('D', 'fin'), ('R', 'r0', 2, 0), ('R', 'r0', 1, 1), ('R', 'r4', 3, 0),
    ('R', 'r2', 1, 2), ('R', 'r4', 3, 1), ('gain0',), ('R', 'r2', 0, 1), ('R', 'r2', 3, 0), ('R', 'r4', 0, 0),
    ('R', 'r0', 1, 3), ('R', 'r2', 2, 2), ('R', 'r2', 0, 3), ('R', 'r4', 0, 1), ('R', 'r0', 1, 0), ('R', 'r2', 2, 1),
    ('R', 'r2', 0, 0), ('W', 'cross'), ('R', 'r2', 2, 3), ('R', 'r1', 2, 0, 0), ('R', 'r1', 2, 0, 1),
    ('R', 'r4', 2, 1), ('R', 'r1', 1, 1, 0), ('R', 'r1', 1, 1, 1), ('R', 'r5', 0), ('R', 'r4', 2, 0), ('R', 'r5', 3),
    ('R', 'r1', 1, 3, 1), ('R', 'r1', 1, 3, 0), ('R', 'r1', 1, 0, 1), ('R', 'r1', 1, 0, 0), ('R', 'r2', 2, 0),
    ('gain1',), ('R', 'r2', 1, 1), ('R', 'r4', 1, 0), ('R', 'r2', 1, 3), ('R', 'r4', 1, 1), ('W', 'fin'),
    ('R', 'r2', 1, 0), ('R', 'r5', 2), ('gain2',), ('R', 'r5', 1), ('fin',),
)
RELS = (2, 1, 3, 0)


def dot_nt(a, b):
    return lax.dot_general(a, b, (((1,), (1,)), ((), ())), preferred_element_type=F32)


def dot_nn(a, b):
    return lax.dot_general(a, b, (((1,), (0,)), ((), ())), preferred_element_type=F32)


def kernel(
    inputs, gate_pre, up_pre, grad_out, gain, w_gate, w_up, w_down,
    o_in, o_gate, o_up, o_down, o_gain,
    vin, vgain, vgp, vup, wg, wu, wd,
    g_all, g_sib, n_all, n_send, a1, a2, gh, acts, act_t, act_s,
    part, rh, rf, rs, zh_buf, zf_buf, gn,
    xp_d, xh_d, xf_d, xz_d, xp_w, xh_w, xf_w, xz_w,
    gt, og,
    loc, ag_s, ag_r, r_s, r_r, x_s, x_r, c_s, c_r, g_s, g_r,
):
    p = lax.axis_index("dp")
    t = lax.axis_index("tensor")
    x, zl, c = p // 4, lax.rem(p // 2, 2), lax.rem(p, 2)
    y, zh = t // 4, lax.rem(t, 4)
    oc = 1 - c
    sib = (x * 4 + zl * 2 + oc, t)
    zsib = (x * 4 + (1 - zl) * 2 + c, t)

    def ring(v, k):
        return lax.rem(v + k, 4)

    def ydev(k):
        return (p, ring(y, k) * 4 + zh)

    def zdev(k):
        return (p, y * 4 + ring(zh, k))

    def xdev(k):
        return (ring(x, k) * 4 + zl * 2 + c, t)

    def tdev(k):
        return (p, lax.rem(t + k, 16))

    def pdev(k):
        return (lax.rem(p + k, 16), t)

    def tid(ky, kz):
        return ring(y, ky) * 4 + ring(zh, kz)

    sent = []

    def send(src, dst, ss, rs_, dev):
        cp = pltpu.make_async_remote_copy(
            src_ref=src, dst_ref=dst, send_sem=ss, recv_sem=rs_, device_id=dev, device_id_type=MESH
        )
        cp.start()
        return cp

    def wait_sent(ref, sem, dev):
        pltpu.make_async_remote_copy(
            src_ref=ref, dst_ref=ref, send_sem=sem, recv_sem=sem, device_id=dev, device_id_type=MESH
        ).wait_send()

    def recv(dst, sem, ss, dev):
        pltpu.make_async_remote_copy(
            src_ref=dst, dst_ref=dst, send_sem=ss, recv_sem=sem, device_id=dev, device_id_type=MESH
        ).wait_recv()

    barrier = pltpu.get_barrier_semaphore()
    partners = [f(k) for f in (ydev, zdev, xdev) for k in (1, 3)] + [sib, zsib]
    for dev in partners:
        pl.semaphore_signal(barrier, inc=1, device_id=dev, device_id_type=MESH)
    local = []
    for i, (src, dst) in enumerate((
        (inputs, vin), (gain, vgain), (gate_pre, vgp), (up_pre, vup),
        (grad_out, g_all.at[t]), (w_down, wd), (w_gate, wg), (w_up, wu),
    )):
        cp = pltpu.make_async_copy(src, dst, loc.at[i])
        cp.start()
        local.append(cp)

    local[0].wait()
    local[1].wait()
    xin = vin[...].astype(F32)
    inv = lax.rsqrt(jnp.mean(xin * xin, axis=1, keepdims=True) + 1e-05)

    @pl.loop(0, 8)
    def _(j):
        own = pl.ds(pl.multiple_of((2 * j + c) * 256, 256), 256)
        oth = pl.ds(pl.multiple_of((2 * j + oc) * 256, 256), 256)
        col = pl.ds(pl.multiple_of(j * 256, 256), 256)
        n_all[c, t, :, col] = (vin[:, own].astype(F32) * inv * vgain[:, own]).astype(BF)
        n_send[:, col] = (vin[:, oth].astype(F32) * inv * vgain[:, oth]).astype(BF)
    pl.semaphore_wait(barrier, len(partners))

    class Gather:
        def __init__(self, item, q, zfirst, piece, half, group, own):
            self.piece_t, self.half_t, self.group_t, self.own = piece, half, group, own
            self.zfirst = zfirst
            self.sem = ag_s.at[item, q]
            self.s = lambda i: self.sem
            self.r = lambda i: ag_r.at[item, q, i]
            self.dev1 = zdev if zfirst else ydev
            self.dev2 = ydev if zfirst else zdev

        def tt(self, ku, kv):
            return tid(kv, ku) if self.zfirst else tid(ku, kv)

        def piece(self, ku, kv):
            return self.piece_t(self.tt(ku, kv))

        def half(self, ku, kv, h):
            return self.half_t(self.tt(ku, kv), h)

        def push(self, src, dst, i, dev):
            send(src, dst, self.s(i), self.r(i), dev)

        def e0(self):
            ref = self.piece(0, 0)
            src = ref if self.own is None else self.own
            self.push(src, ref, 1, self.dev1(1))
            self.push(src, ref, 0, self.dev1(3))

        def s2(self, k):
            i = KS.index(k)
            ref = self.piece(k, 0)
            src = ref if self.own is None or k else self.own
            self.push(src, ref, 3 + 2 * i + 1, self.dev2(1))
            self.push(src, ref, 3 + 2 * i, self.dev2(3))

        def f1(self, k):
            h = k // 2
            recv(self.piece(k, 0), self.r(h), self.s(h), self.dev1(k))
            self.push(self.half(k, 0, h), self.half(k, 0, h), 2, self.dev1(4 - k))

        def f2(self, k, kk):
            i, h = KS.index(k), kk // 2
            recv(self.piece(k, kk), self.r(3 + 2 * i + h), self.sem, self.dev2(kk))
            self.push(self.half(k, kk, h), self.half(k, kk, h), 11, self.dev2(4 - kk))

        def e3(self):
            recv(self.piece(2, 0), self.r(2), self.sem, self.dev1(1))

        def done(self):
            recv(self.group_t(4), self.r(11), self.sem, self.dev2(1))

        def settle(self):
            wait_sent(self.group_t(15), self.sem, self.dev1(1))

    def g_cols(q):
        return pl.ds(pl.multiple_of(ring(x, RELS[q]) * QW, QW), QW)

    def n_cols(q):
        return pl.ds(pl.multiple_of(ring(x, RELS[q]) * 512, 512), 512)

    GA = [
        Gather(
            0, q, MODES['G'][q] == 'z',
            lambda tt, q=q: g_all.at[tt, :, g_cols(q)],
            lambda tt, h, q=q: g_all.at[tt, pl.ds(16 * h, 16), g_cols(q)],
            lambda n, q=q: g_all.at[pl.ds(0, n), :, g_cols(q)],
            grad_out.at[:, g_cols(q)],
        )
        for q in range(NQ)
    ]
    NA = [
        Gather(
            1, q, MODES['N'][q] == 'z',
            lambda tt, q=q: n_all.at[:, tt, :, n_cols(q)],
            lambda tt, h, q=q: n_all.at[h, tt, :, n_cols(q)],
            lambda n, q=q: n_all.at[:, pl.ds(0, n), :, n_cols(q)],
            None,
        )
        for q in range(NQ)
    ]

    def normed():
        sent.append(send(n_send, n_all.at[c, t], c_s.at[0], c_r.at[0], sib))

    def nx():
        recv(n_all.at[oc, t], c_r.at[0], c_s.at[0], sib)

    def prefac():
        local[2].wait()
        local[3].wait()

        @pl.loop(0, F // 64)
        def _(r):
            rows = pl.ds(pl.multiple_of(r * 64, 64), 64)
            gp = vgp[rows, :].astype(F32)
            up = vup[rows, :].astype(F32)
            s = jax.nn.sigmoid(gp)
            gs = gp * s
            a2[rows, :] = gs
            a1[rows, :] = up * (s * (1.0 + gp * (1.0 - s)))
            act_t[0, rows, :] = (gs * up).astype(BF)

        sent.append(send(act_t.at[0], act_s.at[0], c_s.at[1], c_r.at[1], sib))

    begun = set()

    def gh_add(q):
        if "gh" not in begun:
            local[4].wait()
            local[5].wait()
        v = dot_nt(wd[:, g_cols(q)], g_all[:, :, g_cols(q)].reshape(T, QW))
        gh[...] = v if "gh" not in begun else gh[...] + v
        begun.add("gh")
        for i in range(2):
            j = 2 * ring(x, RELS[q]) + i
            src = g_all.at[:, :, pl.ds(pl.multiple_of((2 * j + oc) * 256, 256), 256)]
            dst = g_sib.at[:, :, pl.ds(pl.multiple_of(j * 256, 256), 256)]
            sent.append(send(src, dst, c_s.at[4 + 2 * q + i], c_r.at[4 + 2 * q + i], sib))

    def act_grads():
        @pl.loop(0, F // 64)
        def _(r):
            rows = pl.ds(pl.multiple_of(r * 64, 64), 64)
            v = gh[rows, :]
            act_t[1, rows, :] = (v * a1[rows, :]).astype(BF)
            act_t[2, rows, :] = (v * a2[rows, :]).astype(BF)

        for i in (1, 2):
            sent.append(send(act_t.at[i], act_s.at[i], c_s.at[1 + i], c_r.at[1 + i], sib))

    def turn():
        @pl.loop(0, 4)
        def _(r):
            rows = pl.ds(pl.multiple_of(r * 128, 128), 128)
            for i in (1, 2):
                acts[i - 1, rows, :] = act_t[i, :, rows].T

    def h_ready():
        recv(act_s.at[0], c_r.at[1], c_s.at[1], sib)

    def d_ready(q):
        for i in range(2):
            j = 2 * ring(x, RELS[q]) + i
            dst = g_sib.at[:, :, pl.ds(pl.multiple_of(j * 256, 256), 256)]
            recv(dst, c_r.at[4 + 2 * q + i], c_s.at[4 + 2 * q + i], sib)

    def w_ready():
        for i in (1, 2):
            recv(act_s.at[i], c_r.at[1 + i], c_s.at[1 + i], sib)

    def add_rows(dst, srcs, rows, step):
        @pl.loop(0, rows // step)
        def _(r):
            rr = pl.ds(pl.multiple_of(r * step, step), step)
            v = dst[rr, :].astype(F32)
            for s_ in srcs:
                v = v + s_[rr, :].astype(F32)
            dst[rr, :] = v.astype(BF)

    oz = 1 - zl

    class DownSum:
        def push(self, src, dst, i, dev):
            sent.append(send(src, dst, x_s.at[i], x_r.at[i], dev))

        def part(self, rel):
            xr = ring(x, rel)

            @pl.loop(0, 2)
            def _(z):
                j = xr * 2 + z
                mine = g_all[:, :, pl.ds(pl.multiple_of((2 * j + c) * 256, 256), 256)].reshape(T, 256)
                his = g_sib[:, :, pl.ds(pl.multiple_of(j * 256, 256), 256)].reshape(T, 256)
                xp_d[xr, z] = (dot_nn(act_t[0], mine) + dot_nn(act_s[0], his)).astype(BF)

        def x2(self):
            xr = ring(x, 2)
            self.push(xp_d.at[xr, 0], xh_d.at[0], 0, xdev(1))
            self.push(xp_d.at[xr, 1], xh_d.at[1], 1, xdev(3))

        def x1(self):
            xr = ring(x, 1)
            recv(xh_d.at[0], x_r.at[0], x_s.at[0], xdev(3))
            add_rows(xp_d.at[xr, 0], [xh_d.at[0]], F, 64)
            self.push(xp_d.at[xr], xf_d.at[0], 2, xdev(1))

        def x3(self):
            xr = ring(x, 3)
            recv(xh_d.at[1], x_r.at[1], x_s.at[1], xdev(1))
            add_rows(xp_d.at[xr, 1], [xh_d.at[1]], F, 64)
            self.push(xp_d.at[xr], xf_d.at[1], 3, xdev(3))

        def cross(self):
            recv(xf_d.at[0], x_r.at[2], x_s.at[2], xdev(3))
            recv(xf_d.at[1], x_r.at[3], x_s.at[3], xdev(1))
            add_rows(xp_d.at[x, oz], [xf_d.at[0, oz], xf_d.at[1, oz]], F, 64)
            self.push(xp_d.at[x, oz], xz_d, 4, zsib)

        def fin(self):
            recv(xz_d, x_r.at[4], x_s.at[4], zsib)

            @pl.loop(0, F // 64)
            def _(r):
                rr = pl.ds(pl.multiple_of(r * 64, 64), 64)
                v = xp_d[x, zl, rr, :].astype(F32) + xf_d[0, zl, rr, :].astype(F32)
                v = v + xf_d[1, zl, rr, :].astype(F32) + xz_d[rr, :].astype(F32)
                o_down[rr, :] = v.astype(BF)


    class WeightSum:
        def push(self, src, dst, i, dev):
            sent.append(send(src, dst, x_s.at[5 + i], x_r.at[5 + i], dev))

        def get(self, dst, i, dev):
            recv(dst, x_r.at[5 + i], x_s.at[5 + i], dev)

        def part(self, rel):
            xr = ring(x, rel)

            @pl.loop(0, 2)
            def _(z):
                j = xr * 2 + z
                cols = pl.ds(pl.multiple_of(j * 256, 256), 256)
                wcols = pl.ds(pl.multiple_of((2 * j + c) * 256, 256), 256)
                mine = n_all[c, :, :, cols].reshape(T, 256)
                his = n_all[oc, :, :, cols].reshape(T, 256)
                gsum = jnp.zeros((8, 256), F32)
                for k, w_ref in enumerate((wg, wu)):
                    v = dot_nn(act_t[1 + k], mine) + dot_nn(act_s[1 + k], his)
                    xp_w[xr, k, z] = v.astype(BF)
                    gsum = gsum + jnp.sum((v * w_ref[:, wcols].astype(F32)).reshape(F // 8, 8, 256), axis=0)
                gt[t, pl.ds(j, 1), :] = jnp.sum(gsum, axis=0, keepdims=True) / vgain[:, wcols]

        def x2(self):
            xr = ring(x, 2)
            self.push(xp_w.at[xr, 0], xh_w.at[0], 0, xdev(1))
            self.push(xp_w.at[xr, 1], xh_w.at[1], 1, xdev(3))

        def x1i(self):
            self.push(xp_w.at[ring(x, 1), 1, oz], xf_w.at[0, 1, oz], 2, xdev(1))

        def x3i(self):
            self.push(xp_w.at[ring(x, 3), 0, oz], xf_w.at[1, 0, oz], 3, xdev(3))

        def x1d(self):
            xr = ring(x, 1)
            self.get(xh_w.at[0], 0, xdev(3))
            add_rows(xp_w.at[xr, 0, oz], [xh_w.at[0, oz]], F, 64)
            self.push(xp_w.at[xr, 0, oz], xf_w.at[0, 0, oz], 4, xdev(1))
            self.push(xp_w.at[xr, 1, zl], xf_w.at[0, 1, zl], 9, xdev(1))
            add_rows(xp_w.at[xr, 0, zl], [xh_w.at[0, zl]], F, 64)
            self.push(xp_w.at[xr, 0, zl], xf_w.at[0, 0, zl], 5, xdev(1))

        def x3d(self):
            xr = ring(x, 3)
            self.get(xh_w.at[1], 1, xdev(1))
            add_rows(xp_w.at[xr, 1, oz], [xh_w.at[1, oz]], F, 64)
            self.push(xp_w.at[xr, 1, oz], xf_w.at[1, 1, oz], 6, xdev(3))
            self.push(xp_w.at[xr, 0, zl], xf_w.at[1, 0, zl], 10, xdev(3))
            add_rows(xp_w.at[xr, 1, zl], [xh_w.at[1, zl]], F, 64)
            self.push(xp_w.at[xr, 1, zl], xf_w.at[1, 1, zl], 7, xdev(3))

        def cross(self):
            self.get(xf_w.at[0, 1, oz], 2, xdev(3))
            self.get(xf_w.at[1, 0, oz], 3, xdev(1))
            self.get(xf_w.at[0, 0, oz], 4, xdev(3))
            self.get(xf_w.at[1, 1, oz], 6, xdev(1))
            for k in (0, 1):
                add_rows(xp_w.at[x, k, oz], [xf_w.at[0, k, oz], xf_w.at[1, k, oz]], F, 64)
            self.push(xp_w.at[x, :, oz], xz_w, 8, zsib)

        def fin(self):
            self.get(xf_w.at[0, 1, zl], 9, xdev(3))
            self.get(xf_w.at[1, 0, zl], 10, xdev(1))
            self.get(xf_w.at[0, 0, zl], 5, xdev(3))
            self.get(xf_w.at[1, 1, zl], 7, xdev(1))
            self.get(xz_w, 8, zsib)
            for k, o_ref in enumerate((o_gate, o_up)):
                @pl.loop(0, F // 64)
                def _(r):
                    rr = pl.ds(pl.multiple_of(r * 64, 64), 64)
                    v = xp_w[x, k, zl, rr, :].astype(F32) + xf_w[0, k, zl, rr, :].astype(F32)
                    v = v + xf_w[1, k, zl, rr, :].astype(F32) + xz_w[k, rr, :].astype(F32)
                    o_ref[rr, :] = v.astype(BF)

    def gain0():
        for k in range(1, 16):
            send(gt.at[t], gt.at[t], g_s.at[0], g_r.at[0], tdev(k))

    def gain1():
        recv(gt.at[pl.ds(0, 15)], g_r.at[0], g_s.at[0], tdev(1))
        og[p] = jnp.sum(gt[...], axis=0)
        for k in range(1, 16):
            send(og.at[p], og.at[p], g_s.at[1], g_r.at[1], pdev(k))

    def gain2():
        recv(og.at[pl.ds(0, 15)], g_r.at[1], g_s.at[1], pdev(1))
        for k in (0, 1):
            v = og[k]
            for i in range(1, 8):
                v = v + og[2 * i + k]
            for j in range(8):
                o_gain[:, pl.ds((2 * j + k) * 256, 256)] = v[j : j + 1, :]

    def p_part(i):
        if "pp" not in begun:
            local[6].wait()
            local[7].wait()
            begun.add("pp")
        cols = pl.ds(i * 512, 512)
        v = dot_nn(acts[0], wg[:, cols]) + dot_nn(acts[1], wu[:, cols])
        part[:, :, cols] = v.astype(BF).reshape(16, 32, 512)

    class Scatter:
        def __init__(self, q, zlast):
            self.cols = pl.ds(128 * sum(RW[:q]), 128 * RW[q])
            self.zlast = zlast
            self.dev1 = ydev if zlast else zdev
            self.dev2 = zdev if zlast else ydev
            self.sem = r_s.at[q]
            self.s = lambda i: self.sem
            self.r = lambda i: r_r.at[q, i]

        def push(self, src, dst, i, dev):
            send(src, dst, self.s(i), self.r(i), dev)

        def tt(self, k1, k2):
            return tid(k1, k2) if self.zlast else tid(k2, k1)

        def blk(self, k1, k2):
            return part.at[self.tt(k1, k2), :, self.cols]

        def hblk(self, k1, k2, h):
            return part.at[self.tt(k1, k2), pl.ds(16 * h, 16), self.cols]

        def r0(self, k):
            i = KS.index(k)
            self.push(self.hblk(2, k, 0), rh.at[i, 0, :, self.cols], 2 * i, self.dev1(1))
            self.push(self.hblk(2, k, 1), rh.at[i, 1, :, self.cols], 2 * i + 1, self.dev1(3))

        def r1(self, k, h):
            i, k1 = KS.index(k), 1 + 2 * h
            src = rh.at[i, h, :, self.cols]
            recv(src, self.r(2 * i + h), self.s(2 * i + h), self.dev1(4 - k1))
            dst = self.hblk(k1, k, h)
            dst[...] = (dst[...].astype(F32) + src[...].astype(F32)).astype(BF)
            self.push(self.blk(k1, k), rf.at[i, h, :, self.cols], 8 + i, self.dev1(k1))

        def r2(self, k):
            i = KS.index(k)
            recv(rf.at[i, :, :, self.cols], self.r(8 + i), self.sem, self.dev1(1))
            v = self.blk(0, k)[...].astype(F32) + rf[i, 0, :, self.cols].astype(F32)
            v = v + rf[i, 1, :, self.cols].astype(F32)
            rs[i, :, self.cols] = v.astype(BF)
            if k == 2:
                for h, k2 in ((0, 1), (1, 3)):
                    src = rs.at[i, pl.ds(16 * h, 16), self.cols]
                    self.push(src, zh_buf.at[h, :, self.cols], 12 + h, self.dev2(k2))

        def r4(self, h):
            k2 = 1 + 2 * h
            src = zh_buf.at[h, :, self.cols]
            recv(src, self.r(12 + h), self.sem, self.dev2(4 - k2))
            i = KS.index(k2)
            dst = rs.at[i, pl.ds(16 * h, 16), self.cols]
            dst[...] = (dst[...].astype(F32) + src[...].astype(F32)).astype(BF)
            self.push(rs.at[i, :, self.cols], zf_buf.at[h, :, self.cols], 14, self.dev2(k2))

        def r5(self):
            recv(zf_buf.at[:, :, self.cols], self.r(14), self.sem, self.dev2(1))
            v = rs[0, :, self.cols].astype(F32) + zf_buf[0, :, self.cols].astype(F32)
            gn[:, self.cols] = v + zf_buf[1, :, self.cols].astype(F32)

        def settle(self):
            wait_sent(part.at[pl.ds(0, 15), :, self.cols], self.sem, self.dev1(1))

    def finish():
        xin = vin[...].astype(F32)
        inv = lax.rsqrt(jnp.mean(xin * xin, axis=1, keepdims=True) + 1e-05)
        dotp = jnp.zeros((32, 1), F32)
        for q in range(NQ):
            cols = pl.ds(q * QW, QW)
            unit = vin[:, cols].astype(F32) * inv
            dotp = dotp + jnp.sum(gn[:, cols] * vgain[:, cols] * unit, axis=1, keepdims=True)
        dotp = dotp * (1.0 / D)
        for q in range(NQ):
            cols = pl.ds(q * QW, QW)
            unit = vin[:, cols].astype(F32) * inv
            res = g_all[t, :, cols].astype(F32) + inv * (gn[:, cols] * vgain[:, cols] - unit * dotp)
            o_in[:, cols] = res.astype(BF)

    RA = [Scatter(q, MODES["R"][q] == "z") for q in range(NQ)]
    per_quarter = {"G": GA, "N": NA, "R": RA}
    whole = {"D": DownSum(), "W": WeightSum()}
    single = {
        "normed": normed, "nx": nx, "prefac": prefac, "gh": gh_add, "acts": act_grads, "tr": turn, "hx": h_ready, "dr": d_ready,
        "wready": w_ready, "pp": p_part, "gain0": gain0, "gain1": gain1, "gain2": gain2, "fin": finish,
    }
    for name, *rest in ORDER:
        if name in per_quarter:
            step, q, *ks = rest
            getattr(per_quarter[name][q], step)(*ks)
        elif name in whole:
            step, *ks = rest
            getattr(whole[name], step)(*ks)
        else:
            single[name](*rest)
    for q in range(NQ):
        GA[q].settle()
        NA[q].settle()
        RA[q].settle()
    wait_sent(gt.at[pl.ds(0, 15)], g_s.at[0], tdev(1))
    wait_sent(og.at[pl.ds(0, 15)], g_s.at[1], pdev(1))
    for cp in sent:
        cp.wait_send()


def deliver(*refs):
    copies = [pltpu.make_async_copy(refs[i], refs[5 + i], refs[10].at[i]) for i in range(5)]
    for cp in copies:
        cp.start()
    for cp in copies:
        cp.wait()


def body(inputs, gate_pre, up_pre, grad_out, gain, w_gate, w_up, w_down):
    V = pltpu.VMEM
    DMA = pltpu.SemaphoreType.DMA
    any_spec = pl.BlockSpec(memory_space=pl.ANY)
    vm_spec = pl.BlockSpec(memory_space=pltpu.VMEM)
    outs = pl.pallas_call(
        kernel,
        out_shape=(
            V((32, D), BF),
            V((F, 256), BF),
            V((F, 256), BF),
            V((F, 256), BF),
            V((1, D), F32),
        ),
        in_specs=[any_spec] * 8,
        out_specs=(vm_spec,) * 5,
        scratch_shapes=[
            V((32, D), BF), V((1, D), F32), V((F, T), BF), V((F, T), BF),
            V((F, D), BF), V((F, D), BF), V((F, D), BF),
            V((16, 32, D), BF), V((16, 32, D // 2), BF), V((2, 16, 32, D // 2), BF), V((32, D // 2), BF),
            V((F, T), F32), V((F, T), F32), V((F, T), F32),
            V((2, T, F), BF), V((3, F, T), BF), V((3, F, T), BF),
            V((16, 32, D), BF), V((4, 2, 16, D), BF), V((4, 2, 32, D), BF), V((4, 32, D), BF),
            V((2, 16, D), BF), V((2, 32, D), BF), V((32, D), F32),
            V((4, 2, F, 256), BF), V((2, F, 256), BF), V((2, 2, F, 256), BF), V((F, 256), BF),
            V((4, 2, 2, F, 256), BF), V((2, 2, F, 256), BF), V((2, 2, 2, F, 256), BF), V((2, F, 256), BF),
            V((16, 8, 256), F32), V((16, 8, 256), F32),
            DMA((8,)), DMA((2, NQ)), DMA((2, NQ, 12)), DMA((NQ,)), DMA((NQ, 15)),
            DMA((16,)), DMA((16,)), DMA((12,)), DMA((12,)), DMA((2,)), DMA((2,)),
        ],
        compiler_params=pltpu.CompilerParams(
            collective_id=0, has_side_effects=True, vmem_limit_bytes=56 * 2**20
        ),
    )(inputs, gate_pre.T, up_pre.T, grad_out, gain.reshape(1, D), w_gate.T, w_up.T, w_down)
    outs = pl.pallas_call(
        deliver,
        out_shape=tuple(jax.ShapeDtypeStruct(o.shape, o.dtype) for o in outs),
        in_specs=[vm_spec] * 5,
        out_specs=(any_spec,) * 5,
        scratch_shapes=[DMA((5,))],
        compiler_params=pltpu.CompilerParams(vmem_limit_bytes=40 * 2**20),
    )(*[pltpu.with_memory_space_constraint(o, pltpu.VMEM) for o in outs])
    return outs[0], outs[1].T, outs[2].T, outs[3], outs[4].reshape(D)


def solution(mesh):
    return jax.shard_map(
        body,
        mesh=mesh,
        in_specs=(
            P(("dp", "tensor"), None),
            P("dp", "tensor"),
            P("dp", "tensor"),
            P(("dp", "tensor"), None),
            P(),
            P(None, "tensor"),
            P(None, "tensor"),
            P("tensor", None),
        ),
        out_specs=(
            P(("dp", "tensor"), None),
            P("dp", "tensor"),
            P("dp", "tensor"),
            P("tensor", "dp"),
            P(),
        ),
        check_vma=False,
    )
```

```python
import functools

import jax
import jax.numpy as jnp
from jax import lax
from jax.experimental import pallas as pl
from jax.experimental.pallas import tpu as pltpu
from jax.sharding import PartitionSpec as P

MESH = pl.DeviceIdType.MESH
BF = jnp.bfloat16
F32 = jnp.float32
D = 4096
F = 448
T = 512
NQ = 4
QW = D // NQ
KS = (0, 1, 3, 2)
MODES = {'G': 'zzzz', 'N': 'zzyz', 'R': 'zzzy'}
RW = (9, 10, 6, 7)
ORDER = (
    ('G', 'e0', 0), ('G', 'e0', 3), ('G', 'e0', 1), ('G', 's2', 1, 0), ('G', 's2', 3, 0), ('prefac',), ('normed',),
    ('G', 's2', 0, 0), ('G', 'e0', 2), ('G', 's2', 2, 0), ('nx',), ('N', 'e0', 2), ('G', 'f2', 1, 0, 3),
    ('G', 'f2', 1, 0, 1), ('G', 'f1', 0, 3), ('G', 'f1', 0, 1), ('G', 's2', 0, 3), ('G', 's2', 0, 1),
    ('G', 'f2', 3, 0, 3), ('G', 'f2', 3, 0, 1), ('hx',), ('G', 'f2', 0, 0, 3), ('G', 'f2', 0, 0, 1),
    ('G', 'f1', 3, 3), ('G', 'f1', 3, 1), ('G', 'f2', 2, 0, 3), ('G', 'f2', 2, 0, 1), ('G', 's2', 3, 3),
    ('N', 'f1', 2, 3), ('N', 'f1', 2, 1), ('G', 'f1', 1, 3), ('G', 'f1', 1, 1), ('G', 's2', 1, 3),
    ('G', 'f2', 0, 3, 3), ('G', 'f2', 0, 3, 1), ('G', 'f2', 0, 1, 3), ('G', 'f2', 0, 1, 1), ('N', 'e0', 3),
    ('G', 'f1', 2, 3), ('G', 'f1', 2, 1), ('G', 's2', 2, 3), ('G', 'e3', 0), ('G', 's2', 0, 2), ('G', 'e3', 3),
    ('G', 'f2', 3, 3, 3), ('G', 'f2', 3, 3, 1), ('N', 'e3', 2), ('N', 'e0', 0), ('G', 'e3', 1), ('G', 's2', 2, 1),
    ('G', 'f2', 1, 3, 3), ('G', 'f2', 1, 3, 1), ('G', 's2', 1, 1), ('N', 'e0', 1), ('N', 'f1', 3, 3),
    ('N', 'f1', 3, 1), ('G', 's2', 1, 2), ('G', 'f2', 2, 3, 3), ('G', 'f2', 2, 3, 1), ('G', 'e3', 2),
    ('G', 'f2', 0, 2, 3), ('G', 'f2', 0, 2, 1), ('G', 's2', 2, 2), ('N', 's2', 2, 0), ('N', 'f1', 0, 3),
    ('N', 'f1', 0, 1), ('G', 'f2', 2, 1, 3), ('G', 'f2', 2, 1, 1), ('G', 's2', 3, 1), ('G', 'f2', 1, 1, 3),
    ('G', 'f2', 1, 1, 1), ('N', 'f1', 1, 3), ('N', 'f1', 1, 1), ('G', 's2', 3, 2), ('G', 'f2', 1, 2, 3),
    ('G', 'f2', 1, 2, 1), ('N', 'e3', 3), ('G', 'done', 0), ('gh', 0), ('N', 's2', 0, 0), ('N', 's2', 2, 3),
    ('G', 'f2', 2, 2, 3), ('G', 'f2', 2, 2, 1), ('N', 'f2', 2, 0, 3), ('N', 'f2', 2, 0, 1), ('N', 's2', 0, 3),
    ('dr', 0), ('D', 'part', 2), ('D', 'x2'), ('G', 'f2', 3, 1, 3), ('G', 'f2', 3, 1, 1), ('N', 'e3', 0),
    ('N', 's2', 2, 1), ('N', 'e3', 1), ('N', 's2', 0, 1), ('G', 'f2', 3, 2, 3), ('G', 'f2', 3, 2, 1),
    ('G', 'done', 1), ('gh', 1), ('N', 's2', 0, 2), ('N', 's2', 2, 2), ('N', 'f2', 2, 3, 3), ('N', 'f2', 2, 3, 1),
    ('N', 'f2', 0, 0, 3), ('N', 'f2', 0, 0, 1), ('G', 'done', 2), ('gh', 2), ('N', 's2', 1, 0), ('dr', 1),
    ('D', 'part', 1), ('N', 'f2', 0, 3, 3), ('N', 'f2', 0, 3, 1), ('D', 'x1'), ('dr', 2), ('D', 'part', 3),
    ('N', 'f2', 2, 1, 3), ('N', 'f2', 2, 1, 1), ('D', 'x3'), ('N', 's2', 1, 3), ('G', 'done', 3), ('N', 's2', 1, 1),
    ('N', 'f2', 0, 1, 3), ('N', 'f2', 0, 1, 1), ('gh', 3), ('acts',), ('N', 'f2', 0, 2, 3), ('N', 'f2', 0, 2, 1),
    ('tr',), ('N', 'f2', 2, 2, 3), ('N', 'f2', 2, 2, 1), ('pp', 2), ('pp', 6), ('pp', 7), ('wready',),
    ('R', 'r0', 3, 2), ('R', 'r0', 3, 1), ('pp', 1), ('N', 's2', 1, 2), ('R', 'r0', 3, 3), ('N', 's2', 3, 0),
    ('N', 's2', 3, 3), ('pp', 4), ('N', 'f2', 1, 0, 3), ('N', 'f2', 1, 0, 1), ('N', 'f2', 1, 3, 3),
    ('N', 'f2', 1, 3, 1), ('R', 'r0', 3, 0), ('dr', 3), ('D', 'part', 0), ('N', 'f2', 1, 1, 3), ('N', 'f2', 1, 1, 1),
    ('pp', 3), ('N', 'done', 0), ('W', 'part', 2), ('W', 'x2'), ('N', 's2', 3, 1), ('N', 's2', 3, 2),
    ('N', 'f2', 1, 2, 3), ('N', 'f2', 1, 2, 1), ('R', 'r1', 3, 2, 0), ('R', 'r1', 3, 2, 1), ('R', 'r1', 3, 1, 0),
    ('R', 'r1', 3, 1, 1), ('R', 'r1', 3, 3, 0), ('R', 'r1', 3, 3, 1), ('D', 'cross'), ('R', 'r0', 1, 2),
    ('R', 'r1', 3, 0, 0), ('R', 'r1', 3, 0, 1), ('pp', 0), ('R', 'r0', 0, 2), ('pp', 5), ('R', 'r0', 2, 2),
    ('N', 'f2', 3, 0, 3), ('N', 'f2', 3, 0, 1), ('N', 'f2', 3, 3, 3), ('N', 'f2', 3, 3, 1), ('N', 'done', 2),
    ('W', 'part', 3), ('R', 'r0', 2, 1), ('R', 'r0', 2, 3), ('R', 'r0', 2, 0), ('W', 'x3i'), ('N', 'f2', 3, 1, 3),
    ('N', 'f2', 3, 1, 1), ('N', 'f2', 3, 2, 3), ('N', 'f2', 3, 2, 1), ('R', 'r2', 3, 2), ('N', 'done', 1),
    ('W', 'part', 1), ('R', 'r1', 2, 2, 0), ('R', 'r1', 2, 2, 1), ('R', 'r1', 0, 2, 0), ('R', 'r1', 0, 2, 1),
    ('R', 'r1', 1, 2, 0), ('R', 'r1', 1, 2, 1), ('W', 'x1i'), ('R', 'r2', 3, 1), ('R', 'r2', 3, 3),
    ('R', 'r1', 2, 1, 0), ('R', 'r1', 2, 1, 1), ('R', 'r1', 2, 3, 0), ('R', 'r1', 2, 3, 1), ('R', 'r1', 2, 0, 0),
    ('R', 'r1', 2, 0, 1), ('W', 'x3d'), ('W', 'x1d'), ('N', 'done', 3), ('W', 'part', 0), ('D', 'fin'),
    ('R', 'r2', 2, 2), ('R', 'r0', 0, 1), ('gain0',), ('R', 'r2', 0, 2), ('R', 'r0', 0, 3), ('R', 'r4', 3, 0),
    ('R', 'r4', 3, 1), ('R', 'r2', 3, 0), ('R', 'r2', 1, 2), ('R', 'r0', 0, 0), ('R', 'r2', 2, 1), ('R', 'r0', 1, 1),
    ('R', 'r4', 2, 0), ('R', 'r2', 2, 3), ('R', 'r4', 2, 1), ('R', 'r0', 1, 3), ('R', 'r0', 1, 0), ('R', 'r2', 2, 0),
    ('W', 'cross'), ('R', 'r1', 0, 1, 0), ('R', 'r1', 0, 1, 1), ('R', 'r1', 0, 3, 1), ('R', 'r1', 0, 3, 0),
    ('R', 'r5', 3), ('R', 'r1', 0, 0, 1), ('R', 'r1', 0, 0, 0), ('R', 'r5', 2), ('R', 'r1', 1, 1, 1), ('gain1',),
    ('R', 'r1', 1, 1, 0), ('R', 'r1', 1, 3, 0), ('R', 'r1', 1, 3, 1), ('R', 'r1', 1, 0, 1), ('R', 'r1', 1, 0, 0),
    ('R', 'r2', 0, 1), ('R', 'r4', 0, 0), ('R', 'r2', 0, 3), ('R', 'r4', 0, 1), ('R', 'r2', 0, 0), ('R', 'r2', 1, 1),
    ('R', 'r4', 1, 0), ('R', 'r2', 1, 3), ('R', 'r4', 1, 1), ('W', 'fin'), ('R', 'r2', 1, 0), ('gain2',),
    ('R', 'r5', 0), ('R', 'r5', 1), ('fin',),
)
RELS = (2, 1, 3, 0)


def dot_nt(a, b):
    return lax.dot_general(a, b, (((1,), (1,)), ((), ())), preferred_element_type=F32)


def dot_nn(a, b):
    return lax.dot_general(a, b, (((1,), (0,)), ((), ())), preferred_element_type=F32)


def kernel(
    inputs, gate_pre, up_pre, grad_out, gain, w_gate, w_up, w_down,
    o_in, o_gate, o_up, o_down, o_gain,
    vin, vgain, vgp, vup, wg, wu, wd,
    g_all, g_sib, n_all, n_send, a1, a2, gh, acts, act_t, act_s,
    part, rh, rf, rs, zh_buf, zf_buf, gn,
    xp_d, xh_d, xf_d, xz_d, xp_w, xh_w, xf_w, xz_w,
    gt, og,
    loc, ag_s, ag_r, r_s, r_r, x_s, x_r, c_s, c_r, g_s, g_r,
):
    p = lax.axis_index("dp")
    t = lax.axis_index("tensor")
    x, zl, c = p // 4, lax.rem(p // 2, 2), lax.rem(p, 2)
    y, zh = t // 4, lax.rem(t, 4)
    oc = 1 - c
    sib = (x * 4 + zl * 2 + oc, t)
    zsib = (x * 4 + (1 - zl) * 2 + c, t)

    def ring(v, k):
        return lax.rem(v + k, 4)

    def ydev(k):
        return (p, ring(y, k) * 4 + zh)

    def zdev(k):
        return (p, y * 4 + ring(zh, k))

    def xdev(k):
        return (ring(x, k) * 4 + zl * 2 + c, t)

    def tdev(k):
        return (p, lax.rem(t + k, 16))

    def pdev(k):
        return (lax.rem(p + k, 16), t)

    def tid(ky, kz):
        return ring(y, ky) * 4 + ring(zh, kz)

    sent = []

    def send(src, dst, ss, rs_, dev):
        cp = pltpu.make_async_remote_copy(
            src_ref=src, dst_ref=dst, send_sem=ss, recv_sem=rs_, device_id=dev, device_id_type=MESH
        )
        cp.start()
        return cp

    def wait_sent(ref, sem, dev):
        pltpu.make_async_remote_copy(
            src_ref=ref, dst_ref=ref, send_sem=sem, recv_sem=sem, device_id=dev, device_id_type=MESH
        ).wait_send()

    def recv(dst, sem, ss, dev):
        pltpu.make_async_remote_copy(
            src_ref=dst, dst_ref=dst, send_sem=ss, recv_sem=sem, device_id=dev, device_id_type=MESH
        ).wait_recv()

    barrier = pltpu.get_barrier_semaphore()
    partners = [f(k) for f in (ydev, zdev, xdev) for k in (1, 3)] + [sib, zsib]
    for dev in partners:
        pl.semaphore_signal(barrier, inc=1, device_id=dev, device_id_type=MESH)
    local = []
    for i, (src, dst) in enumerate((
        (inputs, vin), (gain, vgain), (gate_pre, vgp), (up_pre, vup),
        (grad_out, g_all.at[t]), (w_down, wd), (w_gate, wg), (w_up, wu),
    )):
        cp = pltpu.make_async_copy(src, dst, loc.at[i])
        cp.start()
        local.append(cp)

    pl.semaphore_wait(barrier, len(partners))

    class Gather:
        def __init__(self, item, q, zfirst, piece, half, group, own):
            self.piece_t, self.half_t, self.group_t, self.own = piece, half, group, own
            self.zfirst = zfirst
            self.sem = ag_s.at[item, q]
            self.s = lambda i: self.sem
            self.r = lambda i: ag_r.at[item, q, i]
            self.dev1 = zdev if zfirst else ydev
            self.dev2 = ydev if zfirst else zdev

        def tt(self, ku, kv):
            return tid(kv, ku) if self.zfirst else tid(ku, kv)

        def piece(self, ku, kv):
            return self.piece_t(self.tt(ku, kv))

        def half(self, ku, kv, h):
            return self.half_t(self.tt(ku, kv), h)

        def push(self, src, dst, i, dev):
            send(src, dst, self.s(i), self.r(i), dev)

        def e0(self):
            ref = self.piece(0, 0)
            src = ref if self.own is None else self.own
            self.push(src, ref, 1, self.dev1(1))
            self.push(src, ref, 0, self.dev1(3))

        def s2(self, k):
            i = KS.index(k)
            ref = self.piece(k, 0)
            src = ref if self.own is None or k else self.own
            self.push(src, ref, 3 + 2 * i + 1, self.dev2(1))
            self.push(src, ref, 3 + 2 * i, self.dev2(3))

        def f1(self, k):
            h = k // 2
            recv(self.piece(k, 0), self.r(h), self.s(h), self.dev1(k))
            self.push(self.half(k, 0, h), self.half(k, 0, h), 2, self.dev1(4 - k))

        def f2(self, k, kk):
            i, h = KS.index(k), kk // 2
            recv(self.piece(k, kk), self.r(3 + 2 * i + h), self.sem, self.dev2(kk))
            self.push(self.half(k, kk, h), self.half(k, kk, h), 11, self.dev2(4 - kk))

        def e3(self):
            recv(self.piece(2, 0), self.r(2), self.sem, self.dev1(1))

        def done(self):
            recv(self.group_t(4), self.r(11), self.sem, self.dev2(1))

        def settle(self):
            wait_sent(self.group_t(15), self.sem, self.dev1(1))

    def g_cols(q):
        return pl.ds(pl.multiple_of(ring(x, RELS[q]) * QW, QW), QW)

    def n_cols(q):
        return pl.ds(pl.multiple_of(ring(x, RELS[q]) * 512, 512), 512)

    GA = [
        Gather(
            0, q, MODES['G'][q] == 'z',
            lambda tt, q=q: g_all.at[tt, :, g_cols(q)],
            lambda tt, h, q=q: g_all.at[tt, pl.ds(16 * h, 16), g_cols(q)],
            lambda n, q=q: g_all.at[pl.ds(0, n), :, g_cols(q)],
            grad_out.at[:, g_cols(q)],
        )
        for q in range(NQ)
    ]
    NA = [
        Gather(
            1, q, MODES['N'][q] == 'z',
            lambda tt, q=q: n_all.at[:, tt, :, n_cols(q)],
            lambda tt, h, q=q: n_all.at[h, tt, :, n_cols(q)],
            lambda n, q=q: n_all.at[:, pl.ds(0, n), :, n_cols(q)],
            None,
        )
        for q in range(NQ)
    ]

    def normed():
        local[0].wait()
        local[1].wait()
        xin = vin[...].astype(F32)
        inv = lax.rsqrt(jnp.mean(xin * xin, axis=1, keepdims=True) + 1e-05)

        @pl.loop(0, 8)
        def _(j):
            own = pl.ds(pl.multiple_of((2 * j + c) * 256, 256), 256)
            oth = pl.ds(pl.multiple_of((2 * j + oc) * 256, 256), 256)
            col = pl.ds(pl.multiple_of(j * 256, 256), 256)
            n_all[c, t, :, col] = (vin[:, own].astype(F32) * inv * vgain[:, own]).astype(BF)
            n_send[:, col] = (vin[:, oth].astype(F32) * inv * vgain[:, oth]).astype(BF)

        sent.append(send(n_send, n_all.at[c, t], c_s.at[0], c_r.at[0], sib))

    def nx():
        recv(n_all.at[oc, t], c_r.at[0], c_s.at[0], sib)

    def prefac():
        local[2].wait()
        local[3].wait()

        @pl.loop(0, F // 64)
        def _(r):
            rows = pl.ds(pl.multiple_of(r * 64, 64), 64)
            gp = vgp[rows, :].astype(F32)
            up = vup[rows, :].astype(F32)
            s = jax.nn.sigmoid(gp)
            gs = gp * s
            a2[rows, :] = gs
            a1[rows, :] = up * (s * (1.0 + gp * (1.0 - s)))
            act_t[0, rows, :] = (gs * up).astype(BF)

        sent.append(send(act_t.at[0], act_s.at[0], c_s.at[1], c_r.at[1], sib))

    begun = set()

    def gh_add(q):
        if "gh" not in begun:
            local[4].wait()
            local[5].wait()
        v = dot_nt(wd[:, g_cols(q)], g_all[:, :, g_cols(q)].reshape(T, QW))
        gh[...] = v if "gh" not in begun else gh[...] + v
        begun.add("gh")
        for i in range(2):
            j = 2 * ring(x, RELS[q]) + i
            src = g_all.at[:, :, pl.ds(pl.multiple_of((2 * j + oc) * 256, 256), 256)]
            dst = g_sib.at[:, :, pl.ds(pl.multiple_of(j * 256, 256), 256)]
            sent.append(send(src, dst, c_s.at[4 + 2 * q + i], c_r.at[4 + 2 * q + i], sib))

    def act_grads():
        @pl.loop(0, F // 64)
        def _(r):
            rows = pl.ds(pl.multiple_of(r * 64, 64), 64)
            v = gh[rows, :]
            act_t[1, rows, :] = (v * a1[rows, :]).astype(BF)
            act_t[2, rows, :] = (v * a2[rows, :]).astype(BF)

        for i in (1, 2):
            sent.append(send(act_t.at[i], act_s.at[i], c_s.at[1 + i], c_r.at[1 + i], sib))

    def turn():
        @pl.loop(0, 4)
        def _(r):
            rows = pl.ds(pl.multiple_of(r * 128, 128), 128)
            for i in (1, 2):
                acts[i - 1, rows, :] = act_t[i, :, rows].T

    def h_ready():
        recv(act_s.at[0], c_r.at[1], c_s.at[1], sib)

    def d_ready(q):
        for i in range(2):
            j = 2 * ring(x, RELS[q]) + i
            dst = g_sib.at[:, :, pl.ds(pl.multiple_of(j * 256, 256), 256)]
            recv(dst, c_r.at[4 + 2 * q + i], c_s.at[4 + 2 * q + i], sib)

    def w_ready():
        for i in (1, 2):
            recv(act_s.at[i], c_r.at[1 + i], c_s.at[1 + i], sib)

    def add_rows(dst, srcs, rows, step):
        @pl.loop(0, rows // step)
        def _(r):
            rr = pl.ds(pl.multiple_of(r * step, step), step)
            v = dst[rr, :].astype(F32)
            for s_ in srcs:
                v = v + s_[rr, :].astype(F32)
            dst[rr, :] = v.astype(BF)

    oz = 1 - zl

    class DownSum:
        def push(self, src, dst, i, dev):
            sent.append(send(src, dst, x_s.at[i], x_r.at[i], dev))

        def part(self, rel):
            xr = ring(x, rel)

            @pl.loop(0, 2)
            def _(z):
                j = xr * 2 + z
                mine = g_all[:, :, pl.ds(pl.multiple_of((2 * j + c) * 256, 256), 256)].reshape(T, 256)
                his = g_sib[:, :, pl.ds(pl.multiple_of(j * 256, 256), 256)].reshape(T, 256)
                xp_d[xr, z] = (dot_nn(act_t[0], mine) + dot_nn(act_s[0], his)).astype(BF)

        def x2(self):
            xr = ring(x, 2)
            self.push(xp_d.at[xr, 0], xh_d.at[0], 0, xdev(1))
            self.push(xp_d.at[xr, 1], xh_d.at[1], 1, xdev(3))

        def x1(self):
            xr = ring(x, 1)
            recv(xh_d.at[0], x_r.at[0], x_s.at[0], xdev(3))
            add_rows(xp_d.at[xr, 0], [xh_d.at[0]], F, 64)
            self.push(xp_d.at[xr], xf_d.at[0], 2, xdev(1))

        def x3(self):
            xr = ring(x, 3)
            recv(xh_d.at[1], x_r.at[1], x_s.at[1], xdev(1))
            add_rows(xp_d.at[xr, 1], [xh_d.at[1]], F, 64)
            self.push(xp_d.at[xr], xf_d.at[1], 3, xdev(3))

        def cross(self):
            recv(xf_d.at[0], x_r.at[2], x_s.at[2], xdev(3))
            recv(xf_d.at[1], x_r.at[3], x_s.at[3], xdev(1))
            add_rows(xp_d.at[x, oz], [xf_d.at[0, oz], xf_d.at[1, oz]], F, 64)
            self.push(xp_d.at[x, oz], xz_d, 4, zsib)

        def fin(self):
            recv(xz_d, x_r.at[4], x_s.at[4], zsib)

            @pl.loop(0, F // 64)
            def _(r):
                rr = pl.ds(pl.multiple_of(r * 64, 64), 64)
                v = xp_d[x, zl, rr, :].astype(F32) + xf_d[0, zl, rr, :].astype(F32)
                v = v + xf_d[1, zl, rr, :].astype(F32) + xz_d[rr, :].astype(F32)
                o_down[rr, :] = v.astype(BF)


    class WeightSum:
        def push(self, src, dst, i, dev):
            sent.append(send(src, dst, x_s.at[5 + i], x_r.at[5 + i], dev))

        def get(self, dst, i, dev):
            recv(dst, x_r.at[5 + i], x_s.at[5 + i], dev)

        def part(self, rel):
            xr = ring(x, rel)

            @pl.loop(0, 2)
            def _(z):
                j = xr * 2 + z
                cols = pl.ds(pl.multiple_of(j * 256, 256), 256)
                wcols = pl.ds(pl.multiple_of((2 * j + c) * 256, 256), 256)
                mine = n_all[c, :, :, cols].reshape(T, 256)
                his = n_all[oc, :, :, cols].reshape(T, 256)
                gsum = jnp.zeros((8, 256), F32)
                for k, w_ref in enumerate((wg, wu)):
                    v = dot_nn(act_t[1 + k], mine) + dot_nn(act_s[1 + k], his)
                    xp_w[xr, k, z] = v.astype(BF)
                    gsum = gsum + jnp.sum((v * w_ref[:, wcols].astype(F32)).reshape(F // 8, 8, 256), axis=0)
                gt[t, pl.ds(j, 1), :] = jnp.sum(gsum, axis=0, keepdims=True) / vgain[:, wcols]

        def x2(self):
            xr = ring(x, 2)
            self.push(xp_w.at[xr, 0], xh_w.at[0], 0, xdev(1))
            self.push(xp_w.at[xr, 1], xh_w.at[1], 1, xdev(3))

        def x1i(self):
            self.push(xp_w.at[ring(x, 1), 1, oz], xf_w.at[0, 1, oz], 2, xdev(1))

        def x3i(self):
            self.push(xp_w.at[ring(x, 3), 0, oz], xf_w.at[1, 0, oz], 3, xdev(3))

        def x1d(self):
            xr = ring(x, 1)
            self.get(xh_w.at[0], 0, xdev(3))
            add_rows(xp_w.at[xr, 0, oz], [xh_w.at[0, oz]], F, 64)
            self.push(xp_w.at[xr, 0, oz], xf_w.at[0, 0, oz], 4, xdev(1))
            self.push(xp_w.at[xr, 1, zl], xf_w.at[0, 1, zl], 9, xdev(1))
            add_rows(xp_w.at[xr, 0, zl], [xh_w.at[0, zl]], F, 64)
            self.push(xp_w.at[xr, 0, zl], xf_w.at[0, 0, zl], 5, xdev(1))

        def x3d(self):
            xr = ring(x, 3)
            self.get(xh_w.at[1], 1, xdev(1))
            add_rows(xp_w.at[xr, 1, oz], [xh_w.at[1, oz]], F, 64)
            self.push(xp_w.at[xr, 1, oz], xf_w.at[1, 1, oz], 6, xdev(3))
            self.push(xp_w.at[xr, 0, zl], xf_w.at[1, 0, zl], 10, xdev(3))
            add_rows(xp_w.at[xr, 1, zl], [xh_w.at[1, zl]], F, 64)
            self.push(xp_w.at[xr, 1, zl], xf_w.at[1, 1, zl], 7, xdev(3))

        def cross(self):
            self.get(xf_w.at[0, 1, oz], 2, xdev(3))
            self.get(xf_w.at[1, 0, oz], 3, xdev(1))
            self.get(xf_w.at[0, 0, oz], 4, xdev(3))
            self.get(xf_w.at[1, 1, oz], 6, xdev(1))
            for k in (0, 1):
                add_rows(xp_w.at[x, k, oz], [xf_w.at[0, k, oz], xf_w.at[1, k, oz]], F, 64)
            self.push(xp_w.at[x, :, oz], xz_w, 8, zsib)

        def fin(self):
            self.get(xf_w.at[0, 1, zl], 9, xdev(3))
            self.get(xf_w.at[1, 0, zl], 10, xdev(1))
            self.get(xf_w.at[0, 0, zl], 5, xdev(3))
            self.get(xf_w.at[1, 1, zl], 7, xdev(1))
            self.get(xz_w, 8, zsib)
            for k, o_ref in enumerate((o_gate, o_up)):
                @pl.loop(0, F // 64)
                def _(r):
                    rr = pl.ds(pl.multiple_of(r * 64, 64), 64)
                    v = xp_w[x, k, zl, rr, :].astype(F32) + xf_w[0, k, zl, rr, :].astype(F32)
                    v = v + xf_w[1, k, zl, rr, :].astype(F32) + xz_w[k, rr, :].astype(F32)
                    o_ref[rr, :] = v.astype(BF)

    def gain0():
        for k in range(1, 16):
            send(gt.at[t], gt.at[t], g_s.at[0], g_r.at[0], tdev(k))

    def gain1():
        recv(gt.at[pl.ds(0, 15)], g_r.at[0], g_s.at[0], tdev(1))
        og[p] = jnp.sum(gt[...], axis=0)
        for k in range(1, 16):
            send(og.at[p], og.at[p], g_s.at[1], g_r.at[1], pdev(k))

    def gain2():
        recv(og.at[pl.ds(0, 15)], g_r.at[1], g_s.at[1], pdev(1))
        for k in (0, 1):
            v = og[k]
            for i in range(1, 8):
                v = v + og[2 * i + k]
            for j in range(8):
                o_gain[:, pl.ds((2 * j + k) * 256, 256)] = v[j : j + 1, :]

    def p_part(i):
        if "pp" not in begun:
            local[6].wait()
            local[7].wait()
            begun.add("pp")
        cols = pl.ds(i * 512, 512)
        v = dot_nn(acts[0], wg[:, cols]) + dot_nn(acts[1], wu[:, cols])
        part[:, :, cols] = v.astype(BF).reshape(16, 32, 512)

    class Scatter:
        def __init__(self, q, zlast):
            self.cols = pl.ds(128 * sum(RW[:q]), 128 * RW[q])
            self.zlast = zlast
            self.dev1 = ydev if zlast else zdev
            self.dev2 = zdev if zlast else ydev
            self.sem = r_s.at[q]
            self.s = lambda i: self.sem
            self.r = lambda i: r_r.at[q, i]

        def push(self, src, dst, i, dev):
            send(src, dst, self.s(i), self.r(i), dev)

        def tt(self, k1, k2):
            return tid(k1, k2) if self.zlast else tid(k2, k1)

        def blk(self, k1, k2):
            return part.at[self.tt(k1, k2), :, self.cols]

        def hblk(self, k1, k2, h):
            return part.at[self.tt(k1, k2), pl.ds(16 * h, 16), self.cols]

        def r0(self, k):
            i = KS.index(k)
            self.push(self.hblk(2, k, 0), rh.at[i, 0, :, self.cols], 2 * i, self.dev1(1))
            self.push(self.hblk(2, k, 1), rh.at[i, 1, :, self.cols], 2 * i + 1, self.dev1(3))

        def r1(self, k, h):
            i, k1 = KS.index(k), 1 + 2 * h
            src = rh.at[i, h, :, self.cols]
            recv(src, self.r(2 * i + h), self.s(2 * i + h), self.dev1(4 - k1))
            dst = self.hblk(k1, k, h)
            dst[...] = (dst[...].astype(F32) + src[...].astype(F32)).astype(BF)
            self.push(self.blk(k1, k), rf.at[i, h, :, self.cols], 8 + i, self.dev1(k1))

        def r2(self, k):
            i = KS.index(k)
            recv(rf.at[i, :, :, self.cols], self.r(8 + i), self.sem, self.dev1(1))
            v = self.blk(0, k)[...].astype(F32) + rf[i, 0, :, self.cols].astype(F32)
            v = v + rf[i, 1, :, self.cols].astype(F32)
            rs[i, :, self.cols] = v.astype(BF)
            if k == 2:
                for h, k2 in ((0, 1), (1, 3)):
                    src = rs.at[i, pl.ds(16 * h, 16), self.cols]
                    self.push(src, zh_buf.at[h, :, self.cols], 12 + h, self.dev2(k2))

        def r4(self, h):
            k2 = 1 + 2 * h
            src = zh_buf.at[h, :, self.cols]
            recv(src, self.r(12 + h), self.sem, self.dev2(4 - k2))
            i = KS.index(k2)
            dst = rs.at[i, pl.ds(16 * h, 16), self.cols]
            dst[...] = (dst[...].astype(F32) + src[...].astype(F32)).astype(BF)
            self.push(rs.at[i, :, self.cols], zf_buf.at[h, :, self.cols], 14, self.dev2(k2))

        def r5(self):
            recv(zf_buf.at[:, :, self.cols], self.r(14), self.sem, self.dev2(1))
            v = rs[0, :, self.cols].astype(F32) + zf_buf[0, :, self.cols].astype(F32)
            gn[:, self.cols] = v + zf_buf[1, :, self.cols].astype(F32)

        def settle(self):
            wait_sent(part.at[pl.ds(0, 15), :, self.cols], self.sem, self.dev1(1))

    def finish():
        xin = vin[...].astype(F32)
        inv = lax.rsqrt(jnp.mean(xin * xin, axis=1, keepdims=True) + 1e-05)
        dotp = jnp.zeros((32, 1), F32)
        for q in range(NQ):
            cols = pl.ds(q * QW, QW)
            unit = vin[:, cols].astype(F32) * inv
            dotp = dotp + jnp.sum(gn[:, cols] * vgain[:, cols] * unit, axis=1, keepdims=True)
        dotp = dotp * (1.0 / D)
        for q in range(NQ):
            cols = pl.ds(q * QW, QW)
            unit = vin[:, cols].astype(F32) * inv
            res = g_all[t, :, cols].astype(F32) + inv * (gn[:, cols] * vgain[:, cols] - unit * dotp)
            o_in[:, cols] = res.astype(BF)

    RA = [Scatter(q, MODES["R"][q] == "z") for q in range(NQ)]
    per_quarter = {"G": GA, "N": NA, "R": RA}
    whole = {"D": DownSum(), "W": WeightSum()}
    single = {
        "normed": normed, "nx": nx, "prefac": prefac, "gh": gh_add, "acts": act_grads, "tr": turn, "hx": h_ready, "dr": d_ready,
        "wready": w_ready, "pp": p_part, "gain0": gain0, "gain1": gain1, "gain2": gain2, "fin": finish,
    }
    for name, *rest in ORDER:
        if name in per_quarter:
            step, q, *ks = rest
            getattr(per_quarter[name][q], step)(*ks)
        elif name in whole:
            step, *ks = rest
            getattr(whole[name], step)(*ks)
        else:
            single[name](*rest)
    for q in range(NQ):
        GA[q].settle()
        NA[q].settle()
        RA[q].settle()
    wait_sent(gt.at[pl.ds(0, 15)], g_s.at[0], tdev(1))
    wait_sent(og.at[pl.ds(0, 15)], g_s.at[1], pdev(1))
    for cp in sent:
        cp.wait_send()


def deliver(*refs):
    copies = [pltpu.make_async_copy(refs[i], refs[5 + i], refs[10].at[i]) for i in range(5)]
    for cp in copies:
        cp.start()
    for cp in copies:
        cp.wait()


def body(inputs, gate_pre, up_pre, grad_out, gain, w_gate, w_up, w_down):
    V = pltpu.VMEM
    DMA = pltpu.SemaphoreType.DMA
    any_spec = pl.BlockSpec(memory_space=pl.ANY)
    vm_spec = pl.BlockSpec(memory_space=pltpu.VMEM)
    outs = pl.pallas_call(
        kernel,
        out_shape=(
            V((32, D), BF),
            V((F, 256), BF),
            V((F, 256), BF),
            V((F, 256), BF),
            V((1, D), F32),
        ),
        in_specs=[any_spec] * 8,
        out_specs=(vm_spec,) * 5,
        scratch_shapes=[
            V((32, D), BF), V((1, D), F32), V((F, T), BF), V((F, T), BF),
            V((F, D), BF), V((F, D), BF), V((F, D), BF),
            V((16, 32, D), BF), V((16, 32, D // 2), BF), V((2, 16, 32, D // 2), BF), V((32, D // 2), BF),
            V((F, T), F32), V((F, T), F32), V((F, T), F32),
            V((2, T, F), BF), V((3, F, T), BF), V((3, F, T), BF),
            V((16, 32, D), BF), V((4, 2, 16, D), BF), V((4, 2, 32, D), BF), V((4, 32, D), BF),
            V((2, 16, D), BF), V((2, 32, D), BF), V((32, D), F32),
            V((4, 2, F, 256), BF), V((2, F, 256), BF), V((2, 2, F, 256), BF), V((F, 256), BF),
            V((4, 2, 2, F, 256), BF), V((2, 2, F, 256), BF), V((2, 2, 2, F, 256), BF), V((2, F, 256), BF),
            V((16, 8, 256), F32), V((16, 8, 256), F32),
            DMA((8,)), DMA((2, NQ)), DMA((2, NQ, 12)), DMA((NQ,)), DMA((NQ, 15)),
            DMA((16,)), DMA((16,)), DMA((12,)), DMA((12,)), DMA((2,)), DMA((2,)),
        ],
        compiler_params=pltpu.CompilerParams(
            collective_id=0, has_side_effects=True, vmem_limit_bytes=56 * 2**20
        ),
    )(inputs, gate_pre.T, up_pre.T, grad_out, gain.reshape(1, D), w_gate.T, w_up.T, w_down)
    outs = pl.pallas_call(
        deliver,
        out_shape=tuple(jax.ShapeDtypeStruct(o.shape, o.dtype) for o in outs),
        in_specs=[vm_spec] * 5,
        out_specs=(any_spec,) * 5,
        scratch_shapes=[DMA((5,))],
        compiler_params=pltpu.CompilerParams(vmem_limit_bytes=40 * 2**20),
    )(*[pltpu.with_memory_space_constraint(o, pltpu.VMEM) for o in outs])
    return outs[0], outs[1].T, outs[2].T, outs[3], outs[4].reshape(D)


def solution(mesh):
    return jax.shard_map(
        body,
        mesh=mesh,
        in_specs=(
            P(("dp", "tensor"), None),
            P("dp", "tensor"),
            P("dp", "tensor"),
            P(("dp", "tensor"), None),
            P(),
            P(None, "tensor"),
            P(None, "tensor"),
            P("tensor", None),
        ),
        out_specs=(
            P(("dp", "tensor"), None),
            P("dp", "tensor"),
            P("dp", "tensor"),
            P("tensor", "dp"),
            P(),
        ),
        check_vma=False,
    )
```

```python
import functools

import jax
import jax.numpy as jnp
from jax import lax
from jax.experimental import pallas as pl
from jax.experimental.pallas import tpu as pltpu
from jax.sharding import PartitionSpec as P

MESH = pl.DeviceIdType.MESH
BF = jnp.bfloat16
F32 = jnp.float32
D = 4096
F = 448
T = 512
NQ = 4
QW = D // NQ
KS = (0, 1, 3, 2)
MODES = {'G': 'zzzz', 'N': 'zzyz', 'R': 'zzzy'}
RW = (9, 10, 6, 7)
ORDER = (
    ('G', 'e0', 0), ('G', 'e0', 3), ('G', 'e0', 1), ('G', 's2', 1, 0), ('G', 's2', 3, 0), ('prefac',), ('normed',),
    ('G', 's2', 0, 0), ('G', 'e0', 2), ('G', 's2', 2, 0), ('nx',), ('N', 'e0', 2), ('G', 'f2', 1, 0),
    ('G', 'f1', 0, 3), ('G', 'f1', 0, 1), ('G', 's2', 0, 3), ('G', 's2', 0, 1), ('G', 'f2', 3, 0), ('hx',),
    ('G', 'f2', 0, 0), ('G', 'f1', 3, 3), ('G', 'f1', 3, 1), ('G', 'f2', 2, 0), ('G', 's2', 3, 3), ('N', 'f1', 2, 3),
    ('N', 'f1', 2, 1), ('G', 'f1', 1, 3), ('G', 'f1', 1, 1), ('G', 's2', 1, 3), ('G', 'f2', 0, 3), ('G', 'f2', 0, 1),
    ('N', 'e0', 3), ('G', 'f1', 2, 3), ('G', 'f1', 2, 1), ('G', 's2', 2, 3), ('G', 'e3', 0), ('G', 's2', 0, 2),
    ('G', 'e3', 3), ('G', 'f2', 3, 3), ('N', 'e3', 2), ('N', 'e0', 0), ('G', 'e3', 1), ('G', 's2', 2, 1),
    ('G', 'f2', 1, 3), ('G', 's2', 1, 1), ('N', 'e0', 1), ('N', 'f1', 3, 3), ('N', 'f1', 3, 1), ('G', 's2', 1, 2),
    ('G', 'f2', 2, 3), ('G', 'e3', 2), ('G', 'f2', 0, 2), ('G', 's2', 2, 2), ('N', 's2', 2, 0), ('N', 'f1', 0, 3),
    ('N', 'f1', 0, 1), ('G', 'f2', 2, 1), ('G', 's2', 3, 1), ('G', 'f2', 1, 1), ('N', 'f1', 1, 3), ('N', 'f1', 1, 1),
    ('G', 's2', 3, 2), ('G', 'f2', 1, 2), ('N', 'e3', 3), ('G', 'done', 0), ('gh', 0), ('N', 's2', 0, 0),
    ('N', 's2', 2, 3), ('G', 'f2', 2, 2), ('N', 'f2', 2, 0), ('N', 's2', 0, 3), ('dr', 0), ('D', 'part', 2),
    ('D', 'x2'), ('G', 'f2', 3, 1), ('N', 'e3', 0), ('N', 's2', 2, 1), ('N', 'e3', 1), ('N', 's2', 0, 1),
    ('G', 'f2', 3, 2), ('G', 'done', 1), ('gh', 1), ('N', 's2', 0, 2), ('N', 's2', 2, 2), ('N', 'f2', 2, 3),
    ('N', 'f2', 0, 0), ('G', 'done', 2), ('gh', 2), ('N', 's2', 1, 0), ('dr', 1), ('D', 'part', 1), ('N', 'f2', 0, 3),
    ('D', 'x1'), ('dr', 2), ('D', 'part', 3), ('N', 'f2', 2, 1), ('D', 'x3'), ('N', 's2', 1, 3), ('G', 'done', 3),
    ('N', 's2', 1, 1), ('N', 'f2', 0, 1), ('gh', 3), ('acts',), ('N', 'f2', 0, 2), ('tr',), ('N', 'f2', 2, 2),
    ('pp', 2), ('pp', 6), ('pp', 7), ('wready',), ('R', 'r0', 3, 2), ('R', 'r0', 3, 1), ('pp', 1), ('N', 's2', 1, 2),
    ('R', 'r0', 3, 3), ('N', 's2', 3, 0), ('N', 's2', 3, 3), ('pp', 4), ('N', 'f2', 1, 0), ('N', 'f2', 1, 3),
    ('R', 'r0', 3, 0), ('dr', 3), ('D', 'part', 0), ('N', 'f2', 1, 1), ('pp', 3), ('N', 'done', 0), ('W', 'part', 2),
    ('W', 'x2'), ('N', 's2', 3, 1), ('N', 's2', 3, 2), ('N', 'f2', 1, 2), ('R', 'r1', 3, 2), ('R', 'r1', 3, 1),
    ('R', 'r1', 3, 3), ('D', 'cross'), ('R', 'r0', 1, 2), ('R', 'r1', 3, 0), ('pp', 0), ('R', 'r0', 0, 2), ('pp', 5),
    ('R', 'r0', 2, 2), ('N', 'f2', 3, 0), ('N', 'f2', 3, 3), ('N', 'done', 2), ('W', 'part', 3), ('R', 'r0', 2, 1),
    ('R', 'r0', 2, 3), ('R', 'r0', 2, 0), ('W', 'x3i'), ('N', 'f2', 3, 1), ('N', 'f2', 3, 2), ('R', 'r2', 3, 2),
    ('N', 'done', 1), ('W', 'part', 1), ('R', 'r1', 2, 2), ('R', 'r1', 0, 2), ('R', 'r1', 1, 2), ('W', 'x1i'),
    ('R', 'r2', 3, 1), ('R', 'r2', 3, 3), ('R', 'r1', 2, 1), ('R', 'r1', 2, 3), ('R', 'r1', 2, 0), ('W', 'x3d'),
    ('W', 'x1d'), ('N', 'done', 3), ('W', 'part', 0), ('D', 'fin'), ('R', 'r2', 2, 2), ('R', 'r0', 0, 1), ('gain0',),
    ('R', 'r2', 0, 2), ('R', 'r0', 0, 3), ('R', 'r4', 3), ('R', 'r2', 3, 0), ('R', 'r2', 1, 2), ('R', 'r0', 0, 0),
    ('R', 'r2', 2, 1), ('R', 'r0', 1, 1), ('R', 'r2', 2, 3), ('R', 'r4', 2), ('R', 'r0', 1, 3), ('R', 'r0', 1, 0),
    ('R', 'r2', 2, 0), ('W', 'cross'), ('R', 'r1', 0, 1), ('R', 'r1', 0, 3), ('R', 'r5', 3), ('R', 'r1', 0, 0),
    ('R', 'r5', 2), ('gain1',), ('R', 'r1', 1, 1), ('R', 'r1', 1, 3), ('R', 'r1', 1, 0), ('R', 'r2', 0, 1),
    ('R', 'r2', 0, 3), ('R', 'r4', 0), ('R', 'r2', 0, 0), ('R', 'r2', 1, 1), ('R', 'r2', 1, 3), ('R', 'r4', 1),
    ('W', 'fin'), ('R', 'r2', 1, 0), ('gain2',), ('R', 'r5', 0), ('R', 'r5', 1), ('fin',),
)
RELS = (2, 1, 3, 0)


def dot_nt(a, b):
    return lax.dot_general(a, b, (((1,), (1,)), ((), ())), preferred_element_type=F32)


def dot_nn(a, b):
    return lax.dot_general(a, b, (((1,), (0,)), ((), ())), preferred_element_type=F32)


def kernel(
    inputs, gate_pre, up_pre, grad_out, gain, w_gate, w_up, w_down,
    o_in, o_gate, o_up, o_down, o_gain,
    vin, vgain, vgp, vup, wg, wu, wd,
    g_all, g_sib, n_all, n_send, a1, a2, gh, acts, act_t, act_s,
    part, rh, rf, rs, zh_buf, zf_buf, gn,
    xp_d, xh_d, xf_d, xz_d, xp_w, xh_w, xf_w, xz_w,
    gt, og,
    loc, ag_s, ag_r, r_s, r_r, x_s, x_r, c_s, c_r, g_s, g_r,
):
    p = lax.axis_index("dp")
    t = lax.axis_index("tensor")
    x, zl, c = p // 4, lax.rem(p // 2, 2), lax.rem(p, 2)
    y, zh = t // 4, lax.rem(t, 4)
    oc = 1 - c
    sib = (x * 4 + zl * 2 + oc, t)
    zsib = (x * 4 + (1 - zl) * 2 + c, t)

    def ring(v, k):
        return lax.rem(v + k, 4)

    def ydev(k):
        return (p, ring(y, k) * 4 + zh)

    def zdev(k):
        return (p, y * 4 + ring(zh, k))

    def xdev(k):
        return (ring(x, k) * 4 + zl * 2 + c, t)

    def tdev(k):
        return (p, lax.rem(t + k, 16))

    def pdev(k):
        return (lax.rem(p + k, 16), t)

    def tid(ky, kz):
        return ring(y, ky) * 4 + ring(zh, kz)

    sent = []

    def send(src, dst, ss, rs_, dev):
        cp = pltpu.make_async_remote_copy(
            src_ref=src, dst_ref=dst, send_sem=ss, recv_sem=rs_, device_id=dev, device_id_type=MESH
        )
        cp.start()
        return cp

    def wait_sent(ref, sem, dev):
        pltpu.make_async_remote_copy(
            src_ref=ref, dst_ref=ref, send_sem=sem, recv_sem=sem, device_id=dev, device_id_type=MESH
        ).wait_send()

    def recv(dst, sem, ss, dev):
        pltpu.make_async_remote_copy(
            src_ref=dst, dst_ref=dst, send_sem=ss, recv_sem=sem, device_id=dev, device_id_type=MESH
        ).wait_recv()

    barrier = pltpu.get_barrier_semaphore()
    partners = [f(k) for f in (ydev, zdev, xdev) for k in (1, 3)] + [sib, zsib]
    for dev in partners:
        pl.semaphore_signal(barrier, inc=1, device_id=dev, device_id_type=MESH)
    local = []
    for i, (src, dst) in enumerate((
        (inputs, vin), (gain, vgain), (gate_pre, vgp), (up_pre, vup),
        (grad_out, g_all.at[t]), (w_down, wd), (w_gate, wg), (w_up, wu),
    )):
        cp = pltpu.make_async_copy(src, dst, loc.at[i])
        cp.start()
        local.append(cp)

    pl.semaphore_wait(barrier, len(partners))

    class Gather:
        def __init__(self, item, q, zfirst, piece, half, group, own):
            self.piece_t, self.half_t, self.group_t, self.own = piece, half, group, own
            self.zfirst = zfirst
            self.sem = ag_s.at[item, q]
            self.s = lambda i: self.sem
            self.r = lambda i: ag_r.at[item, q, i]
            self.dev1 = zdev if zfirst else ydev
            self.dev2 = ydev if zfirst else zdev

        def tt(self, ku, kv):
            return tid(kv, ku) if self.zfirst else tid(ku, kv)

        def piece(self, ku, kv):
            return self.piece_t(self.tt(ku, kv))

        def half(self, ku, kv, h):
            return self.half_t(self.tt(ku, kv), h)

        def push(self, src, dst, i, dev):
            send(src, dst, self.s(i), self.r(i), dev)

        def e0(self):
            ref = self.piece(0, 0)
            src = ref if self.own is None else self.own
            self.push(src, ref, 1, self.dev1(1))
            self.push(src, ref, 0, self.dev1(3))

        def s2(self, k):
            i = KS.index(k)
            ref = self.piece(k, 0)
            src = ref if self.own is None or k else self.own
            self.push(src, ref, 3 + i, self.dev2(1))
            self.push(src, ref, 3 + i, self.dev2(3))

        def f1(self, k):
            h = k // 2
            recv(self.piece(k, 0), self.r(h), self.s(h), self.dev1(k))
            self.push(self.half(k, 0, h), self.half(k, 0, h), 2, self.dev1(4 - k))

        def f2(self, k):
            i = KS.index(k)
            recv(self.group_t(2), self.r(3 + i), self.sem, self.dev2(1))
            self.push(self.half(k, 1, 0), self.half(k, 1, 0), 7, self.dev2(3))
            self.push(self.half(k, 3, 1), self.half(k, 3, 1), 7, self.dev2(1))

        def e3(self):
            recv(self.piece(2, 0), self.r(2), self.sem, self.dev1(1))

        def done(self):
            recv(self.group_t(4), self.r(7), self.sem, self.dev2(1))

        def settle(self):
            wait_sent(self.group_t(15), self.sem, self.dev1(1))

    def g_cols(q):
        return pl.ds(pl.multiple_of(ring(x, RELS[q]) * QW, QW), QW)

    def n_cols(q):
        return pl.ds(pl.multiple_of(ring(x, RELS[q]) * 512, 512), 512)

    GA = [
        Gather(
            0, q, MODES['G'][q] == 'z',
            lambda tt, q=q: g_all.at[tt, :, g_cols(q)],
            lambda tt, h, q=q: g_all.at[tt, pl.ds(16 * h, 16), g_cols(q)],
            lambda n, q=q: g_all.at[pl.ds(0, n), :, g_cols(q)],
            grad_out.at[:, g_cols(q)],
        )
        for q in range(NQ)
    ]
    NA = [
        Gather(
            1, q, MODES['N'][q] == 'z',
            lambda tt, q=q: n_all.at[:, tt, :, n_cols(q)],
            lambda tt, h, q=q: n_all.at[h, tt, :, n_cols(q)],
            lambda n, q=q: n_all.at[:, pl.ds(0, n), :, n_cols(q)],
            None,
        )
        for q in range(NQ)
    ]

    def normed():
        local[0].wait()
        local[1].wait()
        xin = vin[...].astype(F32)
        inv = lax.rsqrt(jnp.mean(xin * xin, axis=1, keepdims=True) + 1e-05)

        @pl.loop(0, 8)
        def _(j):
            own = pl.ds(pl.multiple_of((2 * j + c) * 256, 256), 256)
            oth = pl.ds(pl.multiple_of((2 * j + oc) * 256, 256), 256)
            col = pl.ds(pl.multiple_of(j * 256, 256), 256)
            n_all[c, t, :, col] = (vin[:, own].astype(F32) * inv * vgain[:, own]).astype(BF)
            n_send[:, col] = (vin[:, oth].astype(F32) * inv * vgain[:, oth]).astype(BF)

        sent.append(send(n_send, n_all.at[c, t], c_s.at[0], c_r.at[0], sib))

    def nx():
        recv(n_all.at[oc, t], c_r.at[0], c_s.at[0], sib)

    def prefac():
        local[2].wait()
        local[3].wait()

        @pl.loop(0, F // 64)
        def _(r):
            rows = pl.ds(pl.multiple_of(r * 64, 64), 64)
            gp = vgp[rows, :].astype(F32)
            up = vup[rows, :].astype(F32)
            s = jax.nn.sigmoid(gp)
            gs = gp * s
            a2[rows, :] = gs
            a1[rows, :] = up * (s * (1.0 + gp * (1.0 - s)))
            act_t[0, rows, :] = (gs * up).astype(BF)

        send(act_t.at[0], act_s.at[0], c_s.at[1], c_r.at[1], sib)

    begun = set()

    def gh_add(q):
        if "gh" not in begun:
            local[4].wait()
            local[5].wait()
        v = dot_nt(wd[:, g_cols(q)], g_all[:, :, g_cols(q)].reshape(T, QW))
        gh[...] = v if "gh" not in begun else gh[...] + v
        begun.add("gh")
        for i in range(2):
            j = 2 * ring(x, RELS[q]) + i
            src = g_all.at[:, :, pl.ds(pl.multiple_of((2 * j + oc) * 256, 256), 256)]
            dst = g_sib.at[:, :, pl.ds(pl.multiple_of(j * 256, 256), 256)]
            send(src, dst, c_s.at[2], c_r.at[3 + q], sib)

    def act_grads():
        @pl.loop(0, F // 64)
        def _(r):
            rows = pl.ds(pl.multiple_of(r * 64, 64), 64)
            v = gh[rows, :]
            act_t[1, rows, :] = (v * a1[rows, :]).astype(BF)
            act_t[2, rows, :] = (v * a2[rows, :]).astype(BF)

        for i in (1, 2):
            send(act_t.at[i], act_s.at[i], c_s.at[1], c_r.at[2], sib)

    def turn():
        @pl.loop(0, 4)
        def _(r):
            rows = pl.ds(pl.multiple_of(r * 128, 128), 128)
            for i in (1, 2):
                acts[i - 1, rows, :] = act_t[i, :, rows].T

    def h_ready():
        recv(act_s.at[0], c_r.at[1], c_s.at[1], sib)

    def d_ready(q):
        dst = g_sib.at[:, :, pl.ds(pl.multiple_of(ring(x, RELS[q]) * 512, 512), 512)]
        recv(dst, c_r.at[3 + q], c_s.at[2], sib)

    def w_ready():
        recv(act_s.at[pl.ds(1, 2)], c_r.at[2], c_s.at[1], sib)

    def add_rows(dst, srcs, rows, step):
        @pl.loop(0, rows // step)
        def _(r):
            rr = pl.ds(pl.multiple_of(r * step, step), step)
            v = dst[rr, :].astype(F32)
            for s_ in srcs:
                v = v + s_[rr, :].astype(F32)
            dst[rr, :] = v.astype(BF)

    oz = 1 - zl

    class DownSum:
        def push(self, src, dst, i, dev):
            sent.append(send(src, dst, x_s.at[i], x_r.at[i], dev))

        def part(self, rel):
            xr = ring(x, rel)

            @pl.loop(0, 2)
            def _(z):
                j = xr * 2 + z
                mine = g_all[:, :, pl.ds(pl.multiple_of((2 * j + c) * 256, 256), 256)].reshape(T, 256)
                his = g_sib[:, :, pl.ds(pl.multiple_of(j * 256, 256), 256)].reshape(T, 256)
                xp_d[xr, z] = (dot_nn(act_t[0], mine) + dot_nn(act_s[0], his)).astype(BF)

        def x2(self):
            xr = ring(x, 2)
            self.push(xp_d.at[xr, 0], xh_d.at[0], 0, xdev(1))
            self.push(xp_d.at[xr, 1], xh_d.at[1], 1, xdev(3))

        def x1(self):
            xr = ring(x, 1)
            recv(xh_d.at[0], x_r.at[0], x_s.at[0], xdev(3))
            add_rows(xp_d.at[xr, 0], [xh_d.at[0]], F, 64)
            self.push(xp_d.at[xr], xf_d.at[0], 2, xdev(1))

        def x3(self):
            xr = ring(x, 3)
            recv(xh_d.at[1], x_r.at[1], x_s.at[1], xdev(1))
            add_rows(xp_d.at[xr, 1], [xh_d.at[1]], F, 64)
            self.push(xp_d.at[xr], xf_d.at[1], 3, xdev(3))

        def cross(self):
            recv(xf_d.at[0], x_r.at[2], x_s.at[2], xdev(3))
            recv(xf_d.at[1], x_r.at[3], x_s.at[3], xdev(1))
            add_rows(xp_d.at[x, oz], [xf_d.at[0, oz], xf_d.at[1, oz]], F, 64)
            self.push(xp_d.at[x, oz], xz_d, 4, zsib)

        def fin(self):
            recv(xz_d, x_r.at[4], x_s.at[4], zsib)

            @pl.loop(0, F // 64)
            def _(r):
                rr = pl.ds(pl.multiple_of(r * 64, 64), 64)
                v = xp_d[x, zl, rr, :].astype(F32) + xf_d[0, zl, rr, :].astype(F32)
                v = v + xf_d[1, zl, rr, :].astype(F32) + xz_d[rr, :].astype(F32)
                o_down[rr, :] = v.astype(BF)


    class WeightSum:
        def push(self, src, dst, i, dev):
            sent.append(send(src, dst, x_s.at[5 + i], x_r.at[5 + i], dev))

        def get(self, dst, i, dev):
            recv(dst, x_r.at[5 + i], x_s.at[5 + i], dev)

        def part(self, rel):
            xr = ring(x, rel)

            @pl.loop(0, 2)
            def _(z):
                j = xr * 2 + z
                cols = pl.ds(pl.multiple_of(j * 256, 256), 256)
                wcols = pl.ds(pl.multiple_of((2 * j + c) * 256, 256), 256)
                mine = n_all[c, :, :, cols].reshape(T, 256)
                his = n_all[oc, :, :, cols].reshape(T, 256)
                gsum = jnp.zeros((8, 256), F32)
                for k, w_ref in enumerate((wg, wu)):
                    v = dot_nn(act_t[1 + k], mine) + dot_nn(act_s[1 + k], his)
                    xp_w[xr, k, z] = v.astype(BF)
                    gsum = gsum + jnp.sum((v * w_ref[:, wcols].astype(F32)).reshape(F // 8, 8, 256), axis=0)
                gt[t, pl.ds(j, 1), :] = jnp.sum(gsum, axis=0, keepdims=True) / vgain[:, wcols]

        def x2(self):
            xr = ring(x, 2)
            self.push(xp_w.at[xr, 0], xh_w.at[0], 0, xdev(1))
            self.push(xp_w.at[xr, 1], xh_w.at[1], 1, xdev(3))

        def x1i(self):
            self.push(xp_w.at[ring(x, 1), 1, oz], xf_w.at[0, 1, oz], 2, xdev(1))

        def x3i(self):
            self.push(xp_w.at[ring(x, 3), 0, oz], xf_w.at[1, 0, oz], 3, xdev(3))

        def x1d(self):
            xr = ring(x, 1)
            self.get(xh_w.at[0], 0, xdev(3))
            add_rows(xp_w.at[xr, 0, oz], [xh_w.at[0, oz]], F, 64)
            self.push(xp_w.at[xr, 0, oz], xf_w.at[0, 0, oz], 4, xdev(1))
            self.push(xp_w.at[xr, 1, zl], xf_w.at[0, 1, zl], 9, xdev(1))
            add_rows(xp_w.at[xr, 0, zl], [xh_w.at[0, zl]], F, 64)
            self.push(xp_w.at[xr, 0, zl], xf_w.at[0, 0, zl], 5, xdev(1))

        def x3d(self):
            xr = ring(x, 3)
            self.get(xh_w.at[1], 1, xdev(1))
            add_rows(xp_w.at[xr, 1, oz], [xh_w.at[1, oz]], F, 64)
            self.push(xp_w.at[xr, 1, oz], xf_w.at[1, 1, oz], 6, xdev(3))
            self.push(xp_w.at[xr, 0, zl], xf_w.at[1, 0, zl], 10, xdev(3))
            add_rows(xp_w.at[xr, 1, zl], [xh_w.at[1, zl]], F, 64)
            self.push(xp_w.at[xr, 1, zl], xf_w.at[1, 1, zl], 7, xdev(3))

        def cross(self):
            self.get(xf_w.at[0, 1, oz], 2, xdev(3))
            self.get(xf_w.at[1, 0, oz], 3, xdev(1))
            self.get(xf_w.at[0, 0, oz], 4, xdev(3))
            self.get(xf_w.at[1, 1, oz], 6, xdev(1))
            for k in (0, 1):
                add_rows(xp_w.at[x, k, oz], [xf_w.at[0, k, oz], xf_w.at[1, k, oz]], F, 64)
            self.push(xp_w.at[x, :, oz], xz_w, 8, zsib)

        def fin(self):
            self.get(xf_w.at[0, 1, zl], 9, xdev(3))
            self.get(xf_w.at[1, 0, zl], 10, xdev(1))
            self.get(xf_w.at[0, 0, zl], 5, xdev(3))
            self.get(xf_w.at[1, 1, zl], 7, xdev(1))
            self.get(xz_w, 8, zsib)
            for k, o_ref in enumerate((o_gate, o_up)):
                @pl.loop(0, F // 64)
                def _(r):
                    rr = pl.ds(pl.multiple_of(r * 64, 64), 64)
                    v = xp_w[x, k, zl, rr, :].astype(F32) + xf_w[0, k, zl, rr, :].astype(F32)
                    v = v + xf_w[1, k, zl, rr, :].astype(F32) + xz_w[k, rr, :].astype(F32)
                    o_ref[rr, :] = v.astype(BF)

    def gain0():
        for k in range(1, 16):
            send(gt.at[t], gt.at[t], g_s.at[0], g_r.at[0], tdev(k))

    def gain1():
        recv(gt.at[pl.ds(0, 15)], g_r.at[0], g_s.at[0], tdev(1))
        og[p] = jnp.sum(gt[...], axis=0)
        for k in range(1, 16):
            send(og.at[p], og.at[p], g_s.at[1], g_r.at[1], pdev(k))

    def gain2():
        recv(og.at[pl.ds(0, 15)], g_r.at[1], g_s.at[1], pdev(1))
        for k in (0, 1):
            v = og[k]
            for i in range(1, 8):
                v = v + og[2 * i + k]
            for j in range(8):
                o_gain[:, pl.ds((2 * j + k) * 256, 256)] = v[j : j + 1, :]

    def p_part(i):
        if "pp" not in begun:
            local[6].wait()
            local[7].wait()
            begun.add("pp")
        cols = pl.ds(i * 512, 512)
        v = dot_nn(acts[0], wg[:, cols]) + dot_nn(acts[1], wu[:, cols])
        part[:, :, cols] = v.astype(BF).reshape(16, 32, 512)

    class Scatter:
        def __init__(self, q, zlast):
            self.cols = pl.ds(128 * sum(RW[:q]), 128 * RW[q])
            self.zlast = zlast
            self.dev1 = ydev if zlast else zdev
            self.dev2 = zdev if zlast else ydev
            self.sem = r_s.at[q]
            self.s = lambda i: self.sem
            self.r = lambda i: r_r.at[q, i]

        def push(self, src, dst, i, dev):
            send(src, dst, self.s(i), self.r(i), dev)

        def tt(self, k1, k2):
            return tid(k1, k2) if self.zlast else tid(k2, k1)

        def blk(self, k1, k2):
            return part.at[self.tt(k1, k2), :, self.cols]

        def hblk(self, k1, k2, h):
            return part.at[self.tt(k1, k2), pl.ds(16 * h, 16), self.cols]

        def r0(self, k):
            i = KS.index(k)
            self.push(self.hblk(2, k, 0), rh.at[i, 0, :, self.cols], i, self.dev1(1))
            self.push(self.hblk(2, k, 1), rh.at[i, 1, :, self.cols], i, self.dev1(3))

        def r1(self, k):
            i = KS.index(k)
            recv(rh.at[i, :, :, self.cols], self.r(i), self.sem, self.dev1(1))
            for h, k1 in ((0, 1), (1, 3)):
                src = rh.at[i, h, :, self.cols]
                dst = self.hblk(k1, k, h)
                dst[...] = (dst[...].astype(F32) + src[...].astype(F32)).astype(BF)
                self.push(self.blk(k1, k), rf.at[i, h, :, self.cols], 4 + i, self.dev1(k1))

        def r2(self, k):
            i = KS.index(k)
            recv(rf.at[i, :, :, self.cols], self.r(4 + i), self.sem, self.dev1(1))
            v = self.blk(0, k)[...].astype(F32) + rf[i, 0, :, self.cols].astype(F32)
            v = v + rf[i, 1, :, self.cols].astype(F32)
            rs[i, :, self.cols] = v.astype(BF)
            if k == 2:
                for h, k2 in ((0, 1), (1, 3)):
                    src = rs.at[i, pl.ds(16 * h, 16), self.cols]
                    self.push(src, zh_buf.at[h, :, self.cols], 8, self.dev2(k2))

        def r4(self):
            recv(zh_buf.at[:, :, self.cols], self.r(8), self.sem, self.dev2(1))
            for h, k2 in ((0, 1), (1, 3)):
                src = zh_buf.at[h, :, self.cols]
                i = KS.index(k2)
                dst = rs.at[i, pl.ds(16 * h, 16), self.cols]
                dst[...] = (dst[...].astype(F32) + src[...].astype(F32)).astype(BF)
                self.push(rs.at[i, :, self.cols], zf_buf.at[h, :, self.cols], 9, self.dev2(k2))

        def r5(self):
            recv(zf_buf.at[:, :, self.cols], self.r(9), self.sem, self.dev2(1))
            v = rs[0, :, self.cols].astype(F32) + zf_buf[0, :, self.cols].astype(F32)
            gn[:, self.cols] = v + zf_buf[1, :, self.cols].astype(F32)

        def settle(self):
            wait_sent(part.at[pl.ds(0, 15), :, self.cols], self.sem, self.dev1(1))

    def finish():
        xin = vin[...].astype(F32)
        inv = lax.rsqrt(jnp.mean(xin * xin, axis=1, keepdims=True) + 1e-05)
        dotp = jnp.zeros((32, 1), F32)
        for q in range(NQ):
            cols = pl.ds(q * QW, QW)
            unit = vin[:, cols].astype(F32) * inv
            dotp = dotp + jnp.sum(gn[:, cols] * vgain[:, cols] * unit, axis=1, keepdims=True)
        dotp = dotp * (1.0 / D)
        for q in range(NQ):
            cols = pl.ds(q * QW, QW)
            unit = vin[:, cols].astype(F32) * inv
            res = g_all[t, :, cols].astype(F32) + inv * (gn[:, cols] * vgain[:, cols] - unit * dotp)
            o_in[:, cols] = res.astype(BF)

    RA = [Scatter(q, MODES["R"][q] == "z") for q in range(NQ)]
    per_quarter = {"G": GA, "N": NA, "R": RA}
    whole = {"D": DownSum(), "W": WeightSum()}
    single = {
        "normed": normed, "nx": nx, "prefac": prefac, "gh": gh_add, "acts": act_grads, "tr": turn, "hx": h_ready, "dr": d_ready,
        "wready": w_ready, "pp": p_part, "gain0": gain0, "gain1": gain1, "gain2": gain2, "fin": finish,
    }
    for name, *rest in ORDER:
        if name in per_quarter:
            step, q, *ks = rest
            getattr(per_quarter[name][q], step)(*ks)
        elif name in whole:
            step, *ks = rest
            getattr(whole[name], step)(*ks)
        else:
            single[name](*rest)
    for q in range(NQ):
        GA[q].settle()
        NA[q].settle()
        RA[q].settle()
    wait_sent(gt.at[pl.ds(0, 15)], g_s.at[0], tdev(1))
    wait_sent(og.at[pl.ds(0, 15)], g_s.at[1], pdev(1))
    wait_sent(act_t, c_s.at[1], sib)
    wait_sent(g_sib, c_s.at[2], sib)
    for cp in sent:
        cp.wait_send()


def deliver(*refs):
    copies = [pltpu.make_async_copy(refs[i], refs[5 + i], refs[10].at[i]) for i in range(5)]
    for cp in copies:
        cp.start()
    for cp in copies:
        cp.wait()


def body(inputs, gate_pre, up_pre, grad_out, gain, w_gate, w_up, w_down):
    V = pltpu.VMEM
    DMA = pltpu.SemaphoreType.DMA
    any_spec = pl.BlockSpec(memory_space=pl.ANY)
    vm_spec = pl.BlockSpec(memory_space=pltpu.VMEM)
    outs = pl.pallas_call(
        kernel,
        out_shape=(
            V((32, D), BF),
            V((F, 256), BF),
            V((F, 256), BF),
            V((F, 256), BF),
            V((1, D), F32),
        ),
        in_specs=[any_spec] * 8,
        out_specs=(vm_spec,) * 5,
        scratch_shapes=[
            V((32, D), BF), V((1, D), F32), V((F, T), BF), V((F, T), BF),
            V((F, D), BF), V((F, D), BF), V((F, D), BF),
            V((16, 32, D), BF), V((16, 32, D // 2), BF), V((2, 16, 32, D // 2), BF), V((32, D // 2), BF),
            V((F, T), F32), V((F, T), F32), V((F, T), F32),
            V((2, T, F), BF), V((3, F, T), BF), V((3, F, T), BF),
            V((16, 32, D), BF), V((4, 2, 16, D), BF), V((4, 2, 32, D), BF), V((4, 32, D), BF),
            V((2, 16, D), BF), V((2, 32, D), BF), V((32, D), F32),
            V((4, 2, F, 256), BF), V((2, F, 256), BF), V((2, 2, F, 256), BF), V((F, 256), BF),
            V((4, 2, 2, F, 256), BF), V((2, 2, F, 256), BF), V((2, 2, 2, F, 256), BF), V((2, F, 256), BF),
            V((16, 8, 256), F32), V((16, 8, 256), F32),
            DMA((8,)), DMA((2, NQ)), DMA((2, NQ, 8)), DMA((NQ,)), DMA((NQ, 10)),
            DMA((16,)), DMA((16,)), DMA((3,)), DMA((7,)), DMA((2,)), DMA((2,)),
        ],
        compiler_params=pltpu.CompilerParams(
            collective_id=0, has_side_effects=True, vmem_limit_bytes=56 * 2**20
        ),
    )(inputs, gate_pre.T, up_pre.T, grad_out, gain.reshape(1, D), w_gate.T, w_up.T, w_down)
    outs = pl.pallas_call(
        deliver,
        out_shape=tuple(jax.ShapeDtypeStruct(o.shape, o.dtype) for o in outs),
        in_specs=[vm_spec] * 5,
        out_specs=(any_spec,) * 5,
        scratch_shapes=[DMA((5,))],
        compiler_params=pltpu.CompilerParams(vmem_limit_bytes=40 * 2**20),
    )(*[pltpu.with_memory_space_constraint(o, pltpu.VMEM) for o in outs])
    return outs[0], outs[1].T, outs[2].T, outs[3], outs[4].reshape(D)


def solution(mesh):
    return jax.shard_map(
        body,
        mesh=mesh,
        in_specs=(
            P(("dp", "tensor"), None),
            P("dp", "tensor"),
            P("dp", "tensor"),
            P(("dp", "tensor"), None),
            P(),
            P(None, "tensor"),
            P(None, "tensor"),
            P("tensor", None),
        ),
        out_specs=(
            P(("dp", "tensor"), None),
            P("dp", "tensor"),
            P("dp", "tensor"),
            P("tensor", "dp"),
            P(),
        ),
        check_vma=False,
    )
```
